32 devices in a mesh: dp: 4 (over z), sp: 4 (over y, x), tp: 2 (over core).
Axes of the slice: x: 2, y: 2, z: 4, core: 2. Of those that a mesh axis runs over, the one named last changes fastest.
Arguments:
- inputs: bfloat16 [4, 2048, 2048], P('dp', 'sp'), may hold values from -6 to 6
- lengths: int32 [4], P('dp'), may hold values from 512 to 2048, as said below
- first_gain: float32 [2048], replicated, may hold values from 0.5 to 1.5
- first_bias: float32 [2048], replicated, may hold values from -4 to 4
- query_weight: bfloat16 [2048, 2048], P(None, 'tp'), may hold values from -0.1875 to 0.1875
- query_bias: float32 [2048], P('tp'), may hold values from -4 to 4
- keyval_weight: bfloat16 [2048, 256], replicated, may hold values from -0.1875 to 0.1875
- value_bias: float32 [128], replicated, may hold values from -4 to 4
- output_weight: bfloat16 [2048, 2048], P('tp'), may hold values from -0.5 to 0.5
- output_bias: float32 [2048], replicated, may hold values from -4 to 4
- second_gain: float32 [2048], replicated, may hold values from 0.5 to 1.5
- second_bias: float32 [2048], replicated, may hold values from -4 to 4
- up_weight: bfloat16 [2048, 8192], P(None, 'tp'), may hold values from -0.125 to 0.125
- up_bias: float32 [8192], P('tp'), may hold values from -6 to 6
- down_weight: bfloat16 [8192, 2048], P('tp'), may hold values from -0.09375 to 0.09375
- down_bias: float32 [2048], replicated, may hold values from -4 to 4
- cotangent: bfloat16 [4, 2048, 2048], P('dp', 'sp'), may hold values from -6 to 6
Outputs:
- outputs: bfloat16 [4, 2048, 2048], P('dp', 'sp')
- input_grad: bfloat16 [4, 2048, 2048], P('dp', 'sp')
- first_gain_grad: float32 [2048], replicated
- first_bias_grad: float32 [2048], replicated
- query_weight_grad: float32 [2048, 2048], P(('dp', 'sp'), 'tp')
- query_bias_grad: float32 [2048], P('tp')
- keyval_weight_grad: float32 [2048, 256], P(('dp', 'sp'))
- value_bias_grad: float32 [128], replicated
- output_weight_grad: float32 [2048, 2048], P('tp', ('dp', 'sp'))
- output_bias_grad: float32 [2048], replicated
- second_gain_grad: float32 [2048], replicated
- second_bias_grad: float32 [2048], replicated
- up_weight_grad: float32 [2048, 8192], P(('dp', 'sp'), 'tp')
- up_bias_grad: float32 [8192], P('tp')
- down_weight_grad: float32 [8192, 2048], P('tp', ('dp', 'sp'))
- down_bias_grad: float32 [2048], replicated
The draws below stay inside these ranges and needn't reach their ends.
Inputs may be any that keep to these rules, and one draw needn't show every extreme that they name: Row r's first lengths[r] tokens are real and the others padding; in every draw some row has all 2048 tokens real.
All inputs are finite; a program needn't handle non-finite values.
Results may differ from the reference program's by a relative error of at most 0.019.
Values may be sent and summed in bfloat16 or wider, within the bound.
A program may use at most 320 MiB of HBM per device.

```python
import math
import jax
import jax.numpy as jnp
from jax import lax

D = 2048
H = 16
HD = 128
FF = 8192
LEN = 2048
ROWS = 4


def draw_lengths(key, part):
    first_key, second_key = jax.random.split(key)
    drawn = jax.random.randint(first_key, (ROWS,), LEN // 4, LEN + 1, dtype=jnp.int32)
    full_row = jax.random.randint(second_key, (), 0, ROWS, dtype=jnp.int32)
    return jnp.where(jnp.arange(ROWS, dtype=jnp.int32) == full_row, LEN, drawn).astype(jnp.int32)


def with_spikes(array, own_key, source, target, parts, factor):
    def block_of(axis_at):
        return (jnp.arange(array.shape[axis_at]) // (array.shape[axis_at] // parts)).reshape((-1,) + (1,) * (array.ndim - 1 - axis_at))

    first = jax.random.permutation(own_key, parts)[block_of(target)]
    far = (block_of(target) + parts // 2) % parts
    return jnp.where((block_of(source) == first) | (block_of(source) == far), factor * array, array)


def block_scale(rng, extent, shards, least, high):
    level, own = 1.0, jax.random.fold_in(rng, 6)
    for axis_at, parts in shards:
        draws = jnp.exp(jax.random.uniform(jax.random.fold_in(own, axis_at), (parts,), jnp.float32, least / len(shards), high / len(shards)))
        level = level * jnp.repeat(draws, extent[axis_at] // parts).reshape([-1 if axis == axis_at else 1 for axis in range(len(extent))])
    return level


def noise(own_key, extent, deviation, bound, cuts=(), kind=jnp.bfloat16):
    gain = block_scale(own_key, extent, cuts, -0.22, 0.18) if cuts else 1.0
    values = jax.random.normal(own_key, extent, jnp.float32) * deviation * gain
    return jnp.minimum(jnp.maximum(values, -bound), bound).astype(kind)


def heavy_noise(stream_key, shape, width, reach, cuts, heavy, held_as=jnp.bfloat16):
    values = width * jax.random.normal(stream_key, shape, jnp.float32)
    if cuts:
        values = values * block_scale(stream_key, shape, cuts, -0.22, 0.18)
    return jnp.clip(with_spikes(values, jax.random.fold_in(stream_key, 3), *heavy), -reach, reach).astype(held_as)


def setup_inputs(seed: int = 0) -> dict:
    key_of = jax.random.split(jax.random.key(seed), 18)
    inputs = noise(key_of[0], (ROWS, LEN, D), 1.0, 6.0, ((0, 4), (1, 4)))
    lengths = draw_lengths(jax.random.fold_in(key_of[17], 71), 0)
    first_gain = jnp.clip(1.0 + 0.1 * jax.random.normal(key_of[2], (D,), jnp.float32), 0.5, 1.5)
    first_bias = noise(key_of[3], (D,), 0.3, 4.0, (), jnp.float32)
    query_weight = noise(key_of[4], (D, H * HD), (D // 2) ** -0.5, 0.1875, ((1, 2),))
    query_bias = noise(key_of[5], (H * HD,), 0.3, 4.0, ((0, 2),), jnp.float32)
    keyval_weight = noise(key_of[6], (D, 2 * HD), (D // 2) ** -0.5, 0.1875)
    value_bias = noise(key_of[7], (HD,), 0.3, 4.0, (), jnp.float32)
    output_weight = noise(key_of[8], (H * HD, D), (H * HD // 16) ** -0.5, 0.5, ((0, 2),))
    output_bias = noise(key_of[9], (D,), 0.3, 4.0, (), jnp.float32)
    second_gain = jnp.clip(1.0 + 0.1 * jax.random.normal(key_of[10], (D,), jnp.float32), 0.5, 1.5)
    second_bias = noise(key_of[11], (D,), 0.3, 4.0, (), jnp.float32)
    up_weight = noise(key_of[12], (D, FF), D ** -0.5, 0.125, ((1, 2),))
    up_bias = noise(key_of[13], (FF,), 0.5, 6.0, ((0, 2),), jnp.float32)
    down_weight = noise(key_of[14], (FF, D), (FF // 2) ** -0.5, 0.09375, ((0, 2),))
    down_bias = noise(key_of[15], (D,), 0.3, 4.0, (), jnp.float32)
    cotangent = heavy_noise(key_of[16], (ROWS, LEN, D), 1.0, 6.0, ((0, 4), (1, 4)), (1, 2, 4, 2.0))
    return dict(inputs=inputs, lengths=lengths, first_gain=first_gain, first_bias=first_bias, query_weight=query_weight, query_bias=query_bias, keyval_weight=keyval_weight, value_bias=value_bias, output_weight=output_weight, output_bias=output_bias, second_gain=second_gain, second_bias=second_bias, up_weight=up_weight, up_bias=up_bias, down_weight=down_weight, down_bias=down_bias, cotangent=cotangent)


EPS = 1e-05

@jax.custom_vjp
def low(v):
    return lax.optimization_barrier(v.astype(jnp.bfloat16)).astype(jnp.float32)

@jax.custom_vjp
def low_back(v):
    return v

def low_keep(v):
    return (low(v), None)

def low_pass(kept, grad):
    return (grad,)

def back_keep(v):
    return (v, None)

def back_low(kept, grad):
    return (low(grad),)
low.defvjp(low_keep, low_pass)
low_back.defvjp(back_keep, back_low)

def layer_norm(values, norm_gain, norm_bias):
    average = lax.optimization_barrier(jnp.mean(values, axis=-1, keepdims=True))
    centered = values - average
    variance = lax.optimization_barrier(jnp.mean(centered * centered, axis=-1, keepdims=True))
    return centered * lax.rsqrt(variance + EPS) * norm_gain + norm_bias

def attend_row(packed):
    query_row, keyval_row, length = packed
    keys_row = keyval_row[:, :HD]
    values_row = keyval_row[:, HD:]
    block = min(512, LEN)
    scale_factor = 1.0 / math.sqrt(HD)
    key_pos = jnp.arange(LEN, dtype=jnp.int32)
    highest = lax.Precision.HIGHEST

    def one_block(start):
        query_block = lax.dynamic_slice_in_dim(query_row, start, block, 0)
        scores = jnp.einsum('qhd,kd->hqk', query_block, keys_row, precision=highest) * scale_factor
        scores = low_back(scores)
        query_pos = start + jnp.arange(block, dtype=jnp.int32)
        allowed = (key_pos[None, :] <= query_pos[:, None]) & (key_pos[None, :] < length)
        scores = jnp.where(allowed[None], scores, -1e+30)
        top = lax.optimization_barrier(jnp.max(scores, axis=-1, keepdims=True))
        weights = jnp.exp(scores - top)
        prob = weights / lax.optimization_barrier(jnp.sum(weights, axis=-1, keepdims=True))
        mixed = jnp.einsum('hqk,kd->qhd', low(prob), values_row, precision=highest)
        return low(low_back(mixed))
    starts = jnp.arange(LEN // block, dtype=jnp.int32) * block
    pieces = lax.map(jax.checkpoint(one_block), starts)
    return pieces.reshape(LEN, H, HD)

def forward(inputs, first_gain, first_bias, query_weight, query_bias, keyval_weight, value_bias, output_weight, output_bias, second_gain, second_bias, up_weight, up_bias, down_weight, down_bias, lengths):
    highest = lax.Precision.HIGHEST
    v_first = low(layer_norm(inputs, first_gain, first_bias))
    query = low(low_back(jnp.einsum('rtd,de->rte', v_first, query_weight, precision=highest) + query_bias))
    kv_bias = jnp.concatenate([jnp.zeros((HD,), jnp.float32), value_bias])
    keyval = low(low_back(jnp.einsum('rtd,de->rte', v_first, keyval_weight, precision=highest) + kv_bias))
    attended = lax.map(jax.checkpoint(attend_row), (query.reshape(ROWS, LEN, H, HD), keyval, lengths))
    attended = attended.reshape(ROWS, LEN, H * HD)
    proj = low_back(jnp.einsum('rte,ed->rtd', attended, output_weight, precision=highest))
    resid = inputs + proj + output_bias
    u_second = low(layer_norm(resid, second_gain, second_bias))
    pre = low_back(jnp.einsum('rtd,df->rtf', u_second, up_weight, precision=highest) + up_bias)
    hidden = low(jax.nn.gelu(pre, approximate=True))
    mlp = low_back(jnp.einsum('rtf,fd->rtd', hidden, down_weight, precision=highest))
    return resid + mlp + down_bias

def reference(inputs, lengths, first_gain, first_bias, query_weight, query_bias, keyval_weight, value_bias, output_weight, output_bias, second_gain, second_bias, up_weight, up_bias, down_weight, down_bias, cotangent):
    params = (inputs.astype(jnp.float32), first_gain, first_bias, query_weight.astype(jnp.float32), query_bias, keyval_weight.astype(jnp.float32), value_bias, output_weight.astype(jnp.float32), output_bias, second_gain, second_bias, up_weight.astype(jnp.float32), up_bias, down_weight.astype(jnp.float32), down_bias)

    def apply_layer(*values):
        return forward(*values, lengths)
    result, pull = jax.vjp(apply_layer, *params)
    grads = pull(cotangent.astype(jnp.float32))
    return (result.astype(jnp.bfloat16), grads[0].astype(jnp.bfloat16), grads[1], grads[2], grads[3], grads[4], grads[5], grads[6], grads[7], grads[8], grads[9], grads[10], grads[11], grads[12], grads[13], grads[14])
```

```python
import functools
import math

import jax
import jax.numpy as jnp
from jax import lax
from jax.experimental import pallas as pl
from jax.experimental.pallas import tpu as pltpu
from jax.sharding import PartitionSpec as P

HD = 128
EPS = 1e-05
BF = jnp.bfloat16
F32 = jnp.float32
SCALE = 1.0 / math.sqrt(HD)
SCALE2 = SCALE * math.log2(math.e)
VMEM = 60 * 2**20
GELU_A = math.sqrt(2.0 / math.pi)
GELU_B = 0.044715


def nn(left, right):
    return jnp.dot(left, right, preferred_element_type=F32)


def nt(left, right):
    return lax.dot_general(left, right, (((1,), (1,)), ((), ())), preferred_element_type=F32)


def tn(left, right):
    return lax.dot_general(left, right, (((0,), (0,)), ((), ())), preferred_element_type=F32)


def params():
    return pltpu.CompilerParams(vmem_limit_bytes=VMEM)


def chunk_mask(first, length, chunk, size, seg, wide):
    key_pos = chunk * size + lax.broadcasted_iota(jnp.int32, (size, wide), 0)
    query_pos = first + lax.rem(lax.broadcasted_iota(jnp.int32, (size, wide), 1), seg)
    return (key_pos <= query_pos) & (key_pos < length)


def chunk_bounds(info_ref, row, seg, size):
    first, length = info_ref[0], info_ref[1 + row]
    full = jnp.minimum(first + 1, length) // size
    total = (jnp.minimum(first + seg, length) + size - 1) // size
    return first, length, full, total


def stack_heads(ref, heads):
    return jnp.concatenate([ref[0, :, h * HD : (h + 1) * HD] for h in range(heads)], axis=0)


def unstack_heads(ref, values, heads, seg):
    for h in range(heads):
        ref[0, :, h * HD : (h + 1) * HD] = values[h * seg : (h + 1) * seg]


def forward_kernel(size, heads, seg, info_ref, q_ref, k_ref, vt_ref, o_ref, lse_ref, top_s, sum_s, acc_s):
    first, length, full, total = chunk_bounds(info_ref, pl.program_id(0), seg, size)
    q = stack_heads(q_ref, heads)
    top_s[...] = jnp.full_like(top_s, -1e30)
    sum_s[...] = jnp.zeros_like(sum_s)
    acc_s[...] = jnp.zeros_like(acc_s)

    def step(masked, chunk, carry):
        at = pl.multiple_of(chunk * size, size)
        scores = nt(k_ref[0, pl.ds(at, size), :], q) * SCALE2
        if masked:
            scores = jnp.where(chunk_mask(first, length, chunk, size, seg, heads * seg), scores, -1e30)
        old = top_s[...]
        new = jnp.maximum(old, jnp.max(scores, axis=0, keepdims=True))
        weights = jnp.exp2(scores - new)
        shrink = jnp.exp2(old - new)
        sum_s[...] = sum_s[...] * shrink + jnp.sum(weights, axis=0, keepdims=True)
        acc_s[...] = acc_s[...] * shrink + nn(vt_ref[0, :, pl.ds(at, size)], weights.astype(BF))
        top_s[...] = new
        return carry

    lax.fori_loop(0, full, functools.partial(step, False), 0)
    lax.fori_loop(full, total, functools.partial(step, True), 0)
    unstack_heads(o_ref, (acc_s[...] * (1.0 / sum_s[...])).T.astype(BF), heads, seg)
    lse_ref[0, 0] = top_s[...] + jnp.log2(sum_s[...])


def attend_forward(info, query, keys, values_t, size, heads):
    rows, seg, width = query.shape
    length = keys.shape[1]
    groups, wide = width // (HD * heads), heads * seg
    head_spec = pl.BlockSpec((1, seg, heads * HD), lambda r, h, info: (r, 0, h))
    return pl.pallas_call(
        functools.partial(forward_kernel, size, heads, seg),
        grid_spec=pltpu.PrefetchScalarGridSpec(
            num_scalar_prefetch=1,
            grid=(rows, groups),
            in_specs=[
                head_spec,
                pl.BlockSpec((1, length, HD), lambda r, h, info: (r, 0, 0)),
                pl.BlockSpec((1, HD, length), lambda r, h, info: (r, 0, 0)),
            ],
            out_specs=[head_spec, pl.BlockSpec((1, 1, 1, wide), lambda r, h, info: (r, h, 0, 0))],
            scratch_shapes=[pltpu.VMEM((1, wide), F32), pltpu.VMEM((1, wide), F32), pltpu.VMEM((HD, wide), F32)],
        ),
        out_shape=[
            jax.ShapeDtypeStruct((rows, seg, width), BF),
            jax.ShapeDtypeStruct((rows, groups, 1, wide), F32),
        ],
        compiler_params=params(),
        cost_estimate=pl.CostEstimate(flops=8 * 10**9, bytes_accessed=4 * 2**20, transcendentals=8 * 10**6),
        name="attend_forward",
    )(info, query, keys, values_t)


def backward_kernel(
    size, heads, seg, info_ref, q_ref, do_ref, o_ref, lse_ref, k_ref, v_ref, kt_ref, dq_ref, dkv_ref, dqt_s
):
    first, length, full, total = chunk_bounds(info_ref, pl.program_id(0), seg, size)

    @pl.when(pl.program_id(1) == 0)
    def _():
        dkv_ref[...] = jnp.zeros_like(dkv_ref)

    q, dout, out = (stack_heads(ref, heads) for ref in (q_ref, do_ref, o_ref))
    delta = jnp.sum((dout.astype(F32) * out.astype(F32)).T, axis=0, keepdims=True)
    lse = lse_ref[0, 0]
    dqt_s[...] = jnp.zeros_like(dqt_s)

    def step(masked, chunk, carry):
        at = pl.multiple_of(chunk * size, size)
        prob = jnp.exp2(nt(k_ref[0, pl.ds(at, size), :], q) * SCALE2 - lse)
        if masked:
            prob = jnp.where(chunk_mask(first, length, chunk, size, seg, heads * seg), prob, 0.0)
        dprob = nt(v_ref[0, pl.ds(at, size), :], dout)
        dscore = (prob * (dprob - delta)).astype(BF)
        dkv_ref[0, pl.ds(at, size), HD:] += nn(prob.astype(BF), dout)
        dkv_ref[0, pl.ds(at, size), :HD] += nn(dscore, q) * SCALE
        dqt_s[...] += nn(kt_ref[0, :, pl.ds(at, size)], dscore)
        return carry

    lax.fori_loop(0, full, functools.partial(step, False), 0)
    lax.fori_loop(full, total, functools.partial(step, True), 0)
    unstack_heads(dq_ref, (dqt_s[...] * SCALE).T.astype(BF), heads, seg)


def attend_backward(info, query, dout, out, lse, keys, values, keys_t, size, heads):
    rows, seg, width = query.shape
    length = keys.shape[1]
    groups, wide = width // (HD * heads), heads * seg
    head_spec = pl.BlockSpec((1, seg, heads * HD), lambda r, h, info: (r, 0, h))
    key_spec = pl.BlockSpec((1, length, HD), lambda r, h, info: (r, 0, 0))
    return pl.pallas_call(
        functools.partial(backward_kernel, size, heads, seg),
        grid_spec=pltpu.PrefetchScalarGridSpec(
            num_scalar_prefetch=1,
            grid=(rows, groups),
            in_specs=[
                head_spec,
                head_spec,
                head_spec,
                pl.BlockSpec((1, 1, 1, wide), lambda r, h, info: (r, h, 0, 0)),
                key_spec,
                key_spec,
                pl.BlockSpec((1, HD, length), lambda r, h, info: (r, 0, 0)),
            ],
            out_specs=[head_spec, pl.BlockSpec((1, length, 2 * HD), lambda r, h, info: (r, 0, 0))],
            scratch_shapes=[pltpu.VMEM((HD, wide), F32)],
        ),
        out_shape=[
            jax.ShapeDtypeStruct((rows, seg, width), BF),
            jax.ShapeDtypeStruct((rows, length, 2 * HD), F32),
        ],
        compiler_params=params(),
        cost_estimate=pl.CostEstimate(flops=16 * 10**9, bytes_accessed=8 * 2**20, transcendentals=8 * 10**6),
        name="attend_backward",
    )(info, query, dout, out, lse, keys, values, keys_t)


def gelu_parts(v):
    square = v * v
    t = jnp.tanh(GELU_A * v * (1.0 + GELU_B * square))
    half = 0.5 * (1.0 + t)
    slope = half + 0.5 * v * (1.0 - t * t) * (GELU_A * (1.0 + 3.0 * GELU_B * square))
    return v * half, slope


def local_kernel(u_ref, dm_ref, up_ref, down_ref, bias_ref, mlp_ref, du_ref, dbias_ref, mlp_s, du_s):
    step = pl.program_id(0)

    @pl.when(step == 0)
    def _():
        mlp_s[...] = jnp.zeros_like(mlp_s)
        du_s[...] = jnp.zeros_like(du_s)

    hidden, slope = gelu_parts(nn(u_ref[...], up_ref[...]) + bias_ref[...])
    mlp_s[...] += nn(hidden.astype(BF), down_ref[...])
    dpre = (nt(dm_ref[...], down_ref[...]) * slope).astype(BF)
    dbias_ref[...] = jnp.sum(dpre.astype(F32), axis=0, keepdims=True)
    du_s[...] += nt(dpre, up_ref[...])

    @pl.when(step == pl.num_programs(0) - 1)
    def _():
        mlp_ref[...] = mlp_s[...].astype(BF)
        du_ref[...] = du_s[...].astype(BF)


def feed_local(u, dmlp, up, down, bias, tile):
    tokens, width = u.shape
    units = up.shape[1]
    whole = pl.BlockSpec((tokens, width), lambda i: (0, 0))
    return pl.pallas_call(
        local_kernel,
        grid=(units // tile,),
        in_specs=[
            whole,
            whole,
            pl.BlockSpec((width, tile), lambda i: (0, i)),
            pl.BlockSpec((tile, width), lambda i: (i, 0)),
            pl.BlockSpec((1, tile), lambda i: (0, i)),
        ],
        out_specs=[whole, whole, pl.BlockSpec((1, tile), lambda i: (0, i))],
        out_shape=[
            jax.ShapeDtypeStruct((tokens, width), BF),
            jax.ShapeDtypeStruct((tokens, width), BF),
            jax.ShapeDtypeStruct((1, units), F32),
        ],
        scratch_shapes=[pltpu.VMEM((tokens, width), F32)] * 2,
        compiler_params=params(),
        cost_estimate=pl.CostEstimate(
            flops=8 * tokens * width * units, bytes_accessed=4 * width * units, transcendentals=tokens * units
        ),
        name="feed_local",
    )(u, dmlp, up, down, bias)


def grad_kernel(at_ref, u_ref, dm_ref, up_ref, down_ref, bias_ref, out_ref):
    tile = up_ref.shape[1]
    hidden, slope = gelu_parts(nn(u_ref[...], up_ref[...]) + bias_ref[...])
    dpre = (nt(dm_ref[...], down_ref[...]) * slope).astype(BF)
    out_ref[:, :tile] = tn(u_ref[...], dpre).astype(BF)
    out_ref[:, tile:] = tn(dm_ref[...], hidden.astype(BF)).astype(BF)


def feed_grads(at, u, dmlp, up, down, bias, tile, count):
    tokens, width = u.shape
    whole = pl.BlockSpec((tokens, width), lambda i, at: (0, 0), pipeline_mode=pl.Buffered(1))
    return pl.pallas_call(
        grad_kernel,
        grid_spec=pltpu.PrefetchScalarGridSpec(
            num_scalar_prefetch=1,
            grid=(count,),
            in_specs=[
                whole,
                whole,
                pl.BlockSpec((width, tile), lambda i, at: (0, at[0] + i)),
                pl.BlockSpec((tile, width), lambda i, at: (at[0] + i, 0)),
                pl.BlockSpec((1, tile), lambda i, at: (0, at[0] + i)),
            ],
            out_specs=pl.BlockSpec((width, 2 * tile), lambda i, at: (0, i)),
        ),
        out_shape=jax.ShapeDtypeStruct((width, 2 * tile * count), BF),
        compiler_params=params(),
        cost_estimate=pl.CostEstimate(
            flops=8 * tokens * width * tile * count, bytes_accessed=4 * width * (tokens + 2 * tile * count), transcendentals=0
        ),
        name="feed_grads",
    )(at, u, dmlp, up, down, bias)


def normalize(values):
    average = jnp.mean(values, axis=-1, keepdims=True)
    centered = values - average
    variance = jnp.mean(centered * centered, axis=-1, keepdims=True)
    inv_std = lax.rsqrt(variance + EPS)
    return centered * inv_std, inv_std


def norm_back(gradient, scaled, inv_std, norm_gain):
    inner = gradient * norm_gain
    mean_one = jnp.mean(inner, axis=-1, keepdims=True)
    mean_two = jnp.mean(inner * scaled, axis=-1, keepdims=True)
    back = inv_std * (inner - mean_one - scaled * mean_two)
    return back, jnp.sum(gradient * scaled, axis=0), jnp.sum(gradient, axis=0)


def build(mesh):
    sp_size, dp_size = mesh.shape["sp"], mesh.shape["dp"]
    quads = sp_size // 4

    def swap(value, bit):
        return lax.ppermute(value, "sp", [(i, i ^ bit) for i in range(sp_size)])

    def swap_dp(value, bit):
        return lax.ppermute(value, "dp", [(i, i ^ bit) for i in range(dp_size)])

    def swap_tp(value):
        return lax.ppermute(value, "tp", [(0, 1), (1, 0)])

    def tp_sum(part):
        part = lax.optimization_barrier(part)
        other = swap_tp(part)
        return part.astype(F32) + other.astype(F32)

    def sum_all(vector):
        for bit in (1 << k for k in range(sp_size.bit_length() - 1)):
            vector = vector + swap(vector, bit)
        for bit in (1 << k for k in range(dp_size.bit_length() - 1)):
            vector = vector + swap_dp(vector, bit)
        return vector

    def gather_quad(own, core):
        half = own.shape[0] // 2
        mine = lax.dynamic_slice_in_dim(own, core * half, half, 0)
        from_x, from_y = swap(mine, 1), swap(mine, 2)
        far = (swap(from_x[: half // 2], 2), swap(from_y[half // 2 :], 1))
        parts = [from_x, from_y, *far]
        return jnp.concatenate([own, *parts, *[swap_tp(part) for part in parts]], axis=0)

    def scatter_quad(blocks):
        blocks = [block.astype(BF) for block in blocks]
        half = blocks[0].shape[0] // 2
        low, high = [b[:half] for b in blocks], [b[half:] for b in blocks]
        low_one, low_pass = swap(low[1], 1), swap(low[3], 1)
        high_one, high_pass = swap(high[2], 2), swap(high[3], 2)
        add = lambda *terms: sum(t.astype(F32) for t in terms)
        low_two = swap(add(low[2], low_pass).astype(BF), 2)
        high_two = swap(add(high[1], high_pass).astype(BF), 1)
        return jnp.concatenate([add(low[0], low_one, low_two), add(high[0], high_one, high_two)], axis=0).astype(BF)

    def scatter_rest(value):
        lead = value.shape[2]
        columns = value.shape[3]
        value = lax.psum_scatter(value.reshape(-1, columns), "dp", scatter_dimension=0, tiled=True)
        if quads > 1:
            groups = [[q * 4 + r for q in range(quads)] for r in range(4)]
            value = lax.psum_scatter(value, "sp", scatter_dimension=0, tiled=True, axis_index_groups=groups)
        return value.reshape(lead, columns)

    def per_device(
        inputs, lengths, first_gain, first_bias, query_weight, query_bias, keyval_weight, value_bias, output_weight,
        output_bias, second_gain, second_bias, up_weight, up_bias, down_weight, down_bias, cotangent,
    ):
        rows, seg, width = inputs.shape
        tokens = rows * seg
        place, core = lax.axis_index("sp"), lax.axis_index("tp")
        spot = lax.rem(place, 4)
        row_len = seg * sp_size
        info = jnp.concatenate([(place * seg).astype(jnp.int32).reshape(1), lengths])
        shard = width // (dp_size * sp_size)

        x = inputs.reshape(tokens, width).astype(F32)
        dmlp = cotangent.reshape(tokens, width)
        hat_one, inv_one = normalize(x)
        v_first = (hat_one * first_gain + first_bias).astype(BF)
        kv_bias = jnp.concatenate([jnp.zeros((HD,), F32), value_bias])
        keyval = (nn(v_first, keyval_weight) + kv_bias).astype(BF)

        if sp_size == 4:
            keyval_all = jnp.zeros((4, tokens, 2 * HD), BF)
            for bit in range(4):
                pairs = [(i, i ^ bit) for i in range(4) if i < i ^ bit]
                piece = lax.ppermute(keyval, "sp", pairs) if bit else keyval
                keyval_all = lax.dynamic_update_slice(keyval_all, piece[None], (spot ^ bit, 0, 0))
            keyval_all = keyval_all.reshape(1, row_len, 2 * HD)
        else:
            keyval_all = lax.all_gather(keyval.reshape(rows, seg, 2 * HD), "sp", axis=1, tiled=True)
        keys, values = keyval_all[:, :, :HD], keyval_all[:, :, HD:]
        keys_t, values_t = keys.transpose(0, 2, 1), values.transpose(0, 2, 1)

        query = (nn(v_first, query_weight) + query_bias).astype(BF).reshape(rows, seg, -1)
        size = min(512, row_len)
        attended, lse = attend_forward(info, query, keys, values_t, size, 4)
        attended_flat = attended.reshape(tokens, -1)

        dmlp_late, _ = lax.optimization_barrier((dmlp, keyval_all))
        dmlp_all = gather_quad(dmlp_late, core)

        proj = tp_sum(nn(attended_flat, output_weight).astype(BF))
        resid = x + proj + output_bias
        hat_two, inv_two = normalize(resid)
        u_second = (hat_two * second_gain + second_bias).astype(BF)
        u_all = gather_quad(u_second, core)

        up_bias_row = up_bias.reshape(1, -1)
        mlp_part, du_part, up_bias_grad = feed_local(u_second, dmlp, up_weight, down_weight, up_bias_row, 512)
        du_second = tp_sum(du_part)
        outputs = (resid + tp_sum(mlp_part) + down_bias).astype(BF).reshape(rows, seg, width)

        dout = dmlp.astype(F32)
        dres_norm, second_gain_grad, second_bias_grad = norm_back(du_second, hat_two, inv_two, second_gain)
        dres = dout + dres_norm
        dproj = dres.astype(BF)
        early = jnp.concatenate(
            [second_gain_grad, second_bias_grad, jnp.sum(dres, axis=0), jnp.sum(dout, axis=0), up_bias_grad[0]]
        )
        early = sum_all(early)

        units = up_weight.shape[1] // 4
        tile = 256
        pieces = 2
        count = units // tile // pieces
        shares = []
        for piece in range(pieces):
            at = ((spot * pieces + piece) * count).astype(jnp.int32).reshape(1)
            part = feed_grads(at, u_all, dmlp_all, up_weight, down_weight, up_bias_row, tile, count)
            share = scatter_rest(part.reshape(dp_size, quads, 4 * shard, -1)).reshape(4, shard, -1)
            blocks = [lax.dynamic_index_in_dim(share, spot ^ bit, 0, keepdims=False) for bit in range(4)]
            shares.append([blocks[0], *[swap(blocks[bit], bit) for bit in range(1, 4)]])
        up_grad = jnp.zeros((4, shard, units), F32)
        down_grad = jnp.zeros((4, shard, units), F32)
        for bit in range(4):
            tiles = [s[bit].astype(F32).reshape(shard, count, 2, tile) for s in shares]
            both = jnp.concatenate(tiles, axis=1)
            up_grad = lax.dynamic_update_slice(up_grad, both[:, :, 0].reshape(1, shard, units), (spot ^ bit, 0, 0))
            down_grad = lax.dynamic_update_slice(down_grad, both[:, :, 1].reshape(1, shard, units), (spot ^ bit, 0, 0))
        up_weight_grad = up_grad.transpose(1, 0, 2).reshape(shard, 4 * units)
        down_weight_grad = down_grad.transpose(0, 2, 1).reshape(4 * units, shard)

        def scatter_rows(value):
            value = value.reshape(dp_size * quads, 4, shard, -1)
            blocks = [
                lax.dynamic_index_in_dim(value, spot ^ bit, 1, keepdims=False).reshape(-1, value.shape[3])
                for bit in range(4)
            ]
            return scatter_rest(scatter_quad(blocks).reshape(dp_size, quads, shard, -1)).astype(F32)

        output_weight_grad = scatter_rows(tn(dproj, attended_flat).astype(BF)).T

        dattended = nt(dproj, output_weight).astype(BF).reshape(rows, seg, -1)
        dquery, dkeyval_part = attend_backward(info, query, dattended, attended, lse, keys, values, keys_t, size, 4)
        dquery = dquery.reshape(tokens, -1)

        if sp_size == 4:
            flat = dkeyval_part.reshape(row_len, 2, HD)
            mine = lax.dynamic_index_in_dim(flat, core, 1, keepdims=False)
            other = lax.dynamic_index_in_dim(flat, 1 - core, 1, keepdims=False)
            half = (mine + swap_tp(other.astype(BF)).astype(F32)).reshape(4, tokens, HD)
            blocks = [lax.dynamic_index_in_dim(half, spot ^ bit, 0, keepdims=False) for bit in range(4)]
            total = blocks[0]
            for bit in range(1, 4):
                pairs = [(i, i ^ bit) for i in range(4) if i > i ^ bit]
                total = total + lax.ppermute(blocks[bit].astype(BF), "sp", pairs).astype(F32)
            own = lax.optimization_barrier(total.astype(BF))
            far = swap_tp(own)
            dkeyval = jnp.where(core == 0, jnp.concatenate([own, far], 1), jnp.concatenate([far, own], 1))
        else:
            part = lax.psum(dkeyval_part.astype(BF), "tp")
            dkeyval = lax.psum_scatter(part, "sp", scatter_dimension=1, tiled=True).reshape(tokens, 2 * HD)
            own = lax.dynamic_slice_in_dim(dkeyval, core * HD, HD, 1)

        query_grad = scatter_rows(jnp.concatenate([tn(v_first, dquery), tn(v_first, own)], axis=1).astype(BF))
        query_weight_grad = query_grad[:, :-HD]
        own_grad = query_grad[:, -HD:]
        far_grad = swap_tp(own_grad)
        keyval_weight_grad = jnp.where(
            core == 0, jnp.concatenate([own_grad, far_grad], 1), jnp.concatenate([far_grad, own_grad], 1)
        )

        dv_first = tp_sum(nt(dquery, query_weight).astype(BF)) + nt(dkeyval, keyval_weight)
        dnorm, first_gain_grad, first_bias_grad = norm_back(dv_first, hat_one, inv_one, first_gain)
        input_grad = (dres + dnorm).astype(BF).reshape(rows, seg, width)
        late = jnp.concatenate(
            [
                first_gain_grad,
                first_bias_grad,
                jnp.sum(dquery.astype(F32), axis=0),
                jnp.sum(dkeyval[:, HD:].astype(F32), axis=0),
            ]
        )
        late = sum_all(late)
        heads_wide = query_bias.shape[0]
        return (
            outputs,
            input_grad,
            late[:width],
            late[width : 2 * width],
            query_weight_grad,
            late[2 * width : 2 * width + heads_wide],
            keyval_weight_grad,
            late[2 * width + heads_wide :],
            output_weight_grad,
            early[2 * width : 3 * width],
            early[:width],
            early[width : 2 * width],
            up_weight_grad,
            early[4 * width :],
            down_weight_grad,
            early[3 * width : 4 * width],
        )

    return per_device


def solution(mesh):
    placed = (
        P("dp", "sp", None),
        P("dp"),
        P(),
        P(),
        P(None, "tp"),
        P("tp"),
        P(),
        P(),
        P("tp", None),
        P(),
        P(),
        P(),
        P(None, "tp"),
        P("tp"),
        P("tp", None),
        P(),
        P("dp", "sp", None),
    )
    return jax.shard_map(
        build(mesh),
        mesh=mesh,
        in_specs=placed,
        out_specs=(
            P("dp", "sp", None),
            P("dp", "sp", None),
            P(),
            P(),
            P(("dp", "sp"), "tp"),
            P("tp"),
            P(("dp", "sp"), None),
            P(),
            P("tp", ("dp", "sp")),
            P(),
            P(),
            P(),
            P(("dp", "sp"), "tp"),
            P("tp"),
            P("tp", ("dp", "sp")),
            P(),
        ),
        check_vma=False,
    )
```

```python
import functools
import math

import jax
import jax.numpy as jnp
from jax import lax
from jax.experimental import pallas as pl
from jax.experimental.pallas import tpu as pltpu
from jax.sharding import PartitionSpec as P

HD = 128
EPS = 1e-05
BF = jnp.bfloat16
F32 = jnp.float32
SCALE = 1.0 / math.sqrt(HD)
SCALE2 = SCALE * math.log2(math.e)
VMEM = 60 * 2**20
GELU_A = math.sqrt(2.0 / math.pi)
GELU_B = 0.044715


def nn(left, right):
    return jnp.dot(left, right, preferred_element_type=F32)


def nt(left, right):
    return lax.dot_general(left, right, (((1,), (1,)), ((), ())), preferred_element_type=F32)


def tn(left, right):
    return lax.dot_general(left, right, (((0,), (0,)), ((), ())), preferred_element_type=F32)


def params():
    return pltpu.CompilerParams(vmem_limit_bytes=VMEM)


def cost(macs, moved):
    return pl.CostEstimate(flops=int(2 * macs), bytes_accessed=int(moved), transcendentals=0)


def whole(*shape):
    return pl.BlockSpec(shape, lambda *_: (0,) * len(shape))


def chunk_mask(first, length, chunk, size, seg, wide):
    key_pos = chunk * size + lax.broadcasted_iota(jnp.int32, (size, wide), 0)
    query_pos = first + lax.rem(lax.broadcasted_iota(jnp.int32, (size, wide), 1), seg)
    return (key_pos <= query_pos) & (key_pos < length)


def chunk_bounds(info_ref, row, seg, size):
    first, length = info_ref[0], info_ref[2 + row]
    full = jnp.minimum(first + 1, length) // size
    total = (jnp.minimum(first + seg, length) + size - 1) // size
    return first, length, full, total


def stack_heads(ref, heads):
    return jnp.concatenate([ref[0, :, h * HD : (h + 1) * HD] for h in range(heads)], axis=0)


def unstack_heads(ref, values, heads, seg):
    for h in range(heads):
        ref[0, :, h * HD : (h + 1) * HD] = values[h * seg : (h + 1) * seg]


def forward_kernel(size, heads, seg, info_ref, q_ref, kv_ref, o_ref, lse_ref, top_s, sum_s, acc_s):
    first, length, full, total = chunk_bounds(info_ref, pl.program_id(0), seg, size)
    q = stack_heads(q_ref, heads)
    top_s[...] = jnp.full_like(top_s, -1e30)
    sum_s[...] = jnp.zeros_like(sum_s)
    acc_s[...] = jnp.zeros_like(acc_s)

    def step(masked, chunk, carry):
        at = pl.ds(pl.multiple_of((chunk ^ info_ref[1]) * size, size), size)
        scores = nt(kv_ref[0, at, :HD], q) * SCALE2
        if masked:
            scores = jnp.where(chunk_mask(first, length, chunk, size, seg, heads * seg), scores, -1e30)
        old = top_s[...]
        new = jnp.maximum(old, jnp.max(scores, axis=0, keepdims=True))
        weights = jnp.exp2(scores - new)
        shrink = jnp.exp2(old - new)
        sum_s[...] = sum_s[...] * shrink + jnp.sum(weights, axis=0, keepdims=True)
        acc_s[...] = acc_s[...] * shrink + tn(kv_ref[0, at, HD:], weights.astype(BF))
        top_s[...] = new
        return carry

    lax.fori_loop(0, full, functools.partial(step, False), 0)
    lax.fori_loop(full, total, functools.partial(step, True), 0)
    unstack_heads(o_ref, (acc_s[...] * (1.0 / sum_s[...])).T.astype(BF), heads, seg)
    lse_ref[0, 0] = top_s[...] + jnp.log2(sum_s[...])


def attend_forward(info, query, keyval, size, heads):
    rows, seg, width = query.shape
    length = keyval.shape[1]
    groups, wide = width // (HD * heads), heads * seg
    head_spec = pl.BlockSpec((1, seg, heads * HD), lambda r, h, info: (r, 0, h))
    return pl.pallas_call(
        functools.partial(forward_kernel, size, heads, seg),
        grid_spec=pltpu.PrefetchScalarGridSpec(
            num_scalar_prefetch=1,
            grid=(rows, groups),
            in_specs=[head_spec, pl.BlockSpec((1, length, 2 * HD), lambda r, h, info: (r, 0, 0))],
            out_specs=[head_spec, pl.BlockSpec((1, 1, 1, wide), lambda r, h, info: (r, h, 0, 0))],
            scratch_shapes=[pltpu.VMEM((1, wide), F32), pltpu.VMEM((1, wide), F32), pltpu.VMEM((HD, wide), F32)],
        ),
        out_shape=[
            jax.ShapeDtypeStruct((rows, seg, width), BF),
            jax.ShapeDtypeStruct((rows, groups, 1, wide), F32),
        ],
        compiler_params=params(),
        cost_estimate=cost(8 * 10**9, 4 * 2**20),
        name="attend_forward",
    )(info, query, keyval)


def backward_kernel(
    size, heads, seg, info_ref, q_ref, do_ref, o_ref, lse_ref, kv_ref, dq_ref, bias_ref, dk_ref, dv_ref, dqt_s
):
    row, group = pl.program_id(0), pl.program_id(1)
    first, length, full, total = chunk_bounds(info_ref, row, seg, size)

    @pl.when(group == 0)
    def _():
        dk_ref[...] = jnp.zeros_like(dk_ref)
        dv_ref[...] = jnp.zeros_like(dv_ref)

    q, dout, out = (stack_heads(ref, heads) for ref in (q_ref, do_ref, o_ref))
    delta = jnp.sum((dout.astype(F32) * out.astype(F32)).T, axis=0, keepdims=True)
    lse = lse_ref[0, 0]
    dqt_s[...] = jnp.zeros_like(dqt_s)

    def step(masked, chunk, carry):
        at = pl.ds(pl.multiple_of((chunk ^ info_ref[1]) * size, size), size)
        prob = jnp.exp2(nt(kv_ref[0, at, :HD], q) * SCALE2 - lse)
        if masked:
            prob = jnp.where(chunk_mask(first, length, chunk, size, seg, heads * seg), prob, 0.0)
        dprob = nt(kv_ref[0, at, HD:], dout)
        dscore = (prob * (dprob - delta)).astype(BF)
        dv_ref[0, at, :] += nn(prob.astype(BF), dout)
        dk_ref[0, at, :] += nn(dscore, q) * SCALE
        dqt_s[...] += tn(kv_ref[0, at, :HD], dscore)
        return carry

    lax.fori_loop(0, full, functools.partial(step, False), 0)
    lax.fori_loop(full, total, functools.partial(step, True), 0)
    dq = (dqt_s[...] * SCALE).T.astype(BF)
    unstack_heads(dq_ref, dq, heads, seg)
    for h in range(heads):
        bias_ref[0, :, h * HD : (h + 1) * HD] = jnp.sum(
            dq[h * seg : (h + 1) * seg].astype(F32), axis=0, keepdims=True
        )


def attend_backward(info, query, dout, out, lse, keyval, size, heads):
    rows, seg, width = query.shape
    length = keyval.shape[1]
    groups, wide = width // (HD * heads), heads * seg
    head_spec = pl.BlockSpec((1, seg, heads * HD), lambda r, h, info: (r, 0, h))
    key_spec = pl.BlockSpec((1, length, HD), lambda r, h, info: (r, 0, 0))
    return pl.pallas_call(
        functools.partial(backward_kernel, size, heads, seg),
        grid_spec=pltpu.PrefetchScalarGridSpec(
            num_scalar_prefetch=1,
            grid=(rows, groups),
            in_specs=[
                head_spec,
                head_spec,
                head_spec,
                pl.BlockSpec((1, 1, 1, wide), lambda r, h, info: (r, h, 0, 0)),
                pl.BlockSpec((1, length, 2 * HD), lambda r, h, info: (r, 0, 0)),
            ],
            out_specs=[head_spec, pl.BlockSpec((1, 1, heads * HD), lambda r, h, info: (r, 0, h)), key_spec, key_spec],
            scratch_shapes=[pltpu.VMEM((HD, wide), F32)],
        ),
        out_shape=[
            jax.ShapeDtypeStruct((rows, seg, width), BF),
            jax.ShapeDtypeStruct((rows, 1, width), F32),
            jax.ShapeDtypeStruct((rows, length, HD), F32),
            jax.ShapeDtypeStruct((rows, length, HD), F32),
        ],
        compiler_params=params(),
        cost_estimate=cost(12 * 10**9, 8 * 2**20),
        name="attend_backward",
    )(info, query, dout, out, lse, keyval)


def gelu_parts(v):
    square = v * v
    t = jnp.tanh(GELU_A * v * (1.0 + GELU_B * square))
    half = 0.5 * (1.0 + t)
    slope = half + 0.5 * v * (1.0 - t * t) * (GELU_A * (1.0 + 3.0 * GELU_B * square))
    return v * half, slope


def local_kernel(
    u_ref, dm_ref, quad_ref, up_ref, down_ref, bias_ref,
    mlp_ref, du_ref, dbias_ref, u_all_ref, quad_far_ref, du_far_ref,
    mlp_s, du_s, du_out_s, u_s, send, recv, local,
):
    step, last = pl.program_id(0), pl.num_programs(0) - 1
    dp, sp, tp = lax.axis_index("dp"), lax.axis_index("sp"), lax.axis_index("tp")
    spot = lax.rem(sp, 4)
    half = u_ref.shape[0] // 2
    quarter = half // 2
    over_x, over_y, sibling = (dp, sp ^ 1, tp), (dp, sp ^ 2, tp), (dp, sp, 1 - tp)

    def remote(k, source, target, device):
        return pltpu.make_async_remote_copy(
            source, target, send.at[k], recv.at[k], device_id=device, device_id_type=pl.DeviceIdType.MESH
        )

    mine, theirs = u_all_ref.at[0], u_all_ref.at[1]
    own = u_s.at[pl.ds(pl.multiple_of(tp * half, half), half), :]
    top, bottom = pl.ds(0, quarter), pl.ds(quarter, quarter)
    to_x = remote(0, own, mine.at[spot], over_x)
    to_y = remote(1, own, mine.at[spot], over_y)
    pass_y = remote(2, mine.at[spot ^ 1, top], mine.at[spot ^ 1, top], over_y)
    pass_x = remote(3, mine.at[spot ^ 2, bottom], mine.at[spot ^ 2, bottom], over_x)
    share_x = remote(4, mine.at[spot ^ 1], theirs.at[spot ^ 1], sibling)
    share_y = remote(5, mine.at[spot ^ 2], theirs.at[spot ^ 2], sibling)
    share_far = remote(6, mine.at[spot ^ 3], theirs.at[spot ^ 3], sibling)
    share_quad = remote(7, quad_ref, quad_far_ref, sibling)
    share_du = remote(8, du_out_s, du_far_ref, sibling)
    keep_own = pltpu.make_async_copy(own, mine.at[spot], local.at[0])
    other = u_s.at[pl.ds(pl.multiple_of((1 - tp) * half, half), half), :]
    keep_other = pltpu.make_async_copy(other, theirs.at[spot], local.at[1])

    @pl.when(step == 0)
    def _():
        barrier = pltpu.get_barrier_semaphore()
        for device in (over_x, over_y, sibling):
            pl.semaphore_signal(barrier, inc=1, device_id=device, device_id_type=pl.DeviceIdType.MESH)
        pl.semaphore_wait(barrier, 3)
        u_s[...] = u_ref[...]
        to_x.start()
        to_y.start()
        share_quad.start()
        keep_own.start()
        keep_other.start()
        mlp_s[...] = jnp.zeros_like(mlp_s)
        du_s[...] = jnp.zeros_like(du_s)

    @pl.when(step == (last + 1) // 2)
    def _():
        to_x.wait_recv()
        to_y.wait_recv()
        pass_y.start()
        pass_x.start()
        share_x.start()
        share_y.start()

    hidden, slope = gelu_parts(nn(u_ref[...], up_ref[...]) + bias_ref[...])
    mlp_s[...] += nn(hidden.astype(BF), down_ref[...])
    dpre = (nt(dm_ref[...], down_ref[...]) * slope).astype(BF)
    dbias_ref[...] = jnp.sum(dpre.astype(F32), axis=0, keepdims=True)
    du_s[...] += nt(dpre, up_ref[...])

    @pl.when(step == last)
    def _():
        du_out_s[...] = du_s[...].astype(BF)
        share_du.start()
        pass_y.wait_recv()
        pass_x.wait_recv()
        share_far.start()
        mlp_ref[...] = mlp_s[...].astype(BF)
        du_ref[...] = du_out_s[...]
        for copy in (to_x, to_y, pass_y, pass_x):
            copy.wait_send()
        for copy in (share_x, share_y, share_far, share_quad, share_du):
            copy.wait()
        keep_own.wait()
        keep_other.wait()


def feed_local(u, dmlp, quad, up, down, bias, tile):
    tokens, width = u.shape
    units = up.shape[1]
    block = whole(tokens, width)
    anywhere = pl.BlockSpec(memory_space=pl.ANY)
    return pl.pallas_call(
        local_kernel,
        grid=(units // tile,),
        in_specs=[
            block,
            block,
            anywhere,
            pl.BlockSpec((width, tile), lambda i: (0, i)),
            pl.BlockSpec((tile, width), lambda i: (i, 0)),
            pl.BlockSpec((1, tile), lambda i: (0, i)),
        ],
        out_specs=[block, block, pl.BlockSpec((1, tile), lambda i: (0, i)), anywhere, anywhere, anywhere],
        out_shape=[
            jax.ShapeDtypeStruct((tokens, width), BF),
            jax.ShapeDtypeStruct((tokens, width), BF),
            jax.ShapeDtypeStruct((1, units), F32),
            jax.ShapeDtypeStruct((2, 4, tokens // 2, width), BF),
            jax.ShapeDtypeStruct(quad.shape, BF),
            jax.ShapeDtypeStruct((tokens, width), BF),
        ],
        scratch_shapes=[
            pltpu.VMEM((tokens, width), F32),
            pltpu.VMEM((tokens, width), F32),
            pltpu.VMEM((tokens, width), BF),
            pltpu.VMEM((tokens, width), BF),
            pltpu.SemaphoreType.DMA((9,)),
            pltpu.SemaphoreType.DMA((9,)),
            pltpu.SemaphoreType.DMA((2,)),
        ],
        compiler_params=pltpu.CompilerParams(vmem_limit_bytes=VMEM, collective_id=0, has_side_effects=True),
        cost_estimate=cost(4 * tokens * width * units, 4 * width * units),
        name="feed_local",
    )(u, dmlp, quad, up, down, bias)


def grad_kernel(u_parts, parts, at_ref, *refs):
    pieces, (up_ref, down_ref, bias_ref, out_ref, u_s, dm_s, sems) = refs[:parts], refs[parts:]

    def copies(target):
        offset = 0
        for k in range(u_parts) if target is u_s else range(u_parts, parts):
            piece = pieces[k]
            yield pltpu.make_async_copy(piece, target.at[pl.ds(offset, piece.shape[0]), :], sems.at[k])
            offset += piece.shape[0]

    @pl.when(pl.program_id(0) == 0)
    def _():
        for copy in copies(u_s):
            copy.start()
        for copy in copies(dm_s):
            copy.start()
        for copy in copies(u_s):
            copy.wait()

    tile = up_ref.shape[1]
    hidden, slope = gelu_parts(nn(u_s[...], up_ref[...]) + bias_ref[...])

    @pl.when(pl.program_id(0) == 0)
    def _():
        for copy in copies(dm_s):
            copy.wait()

    dpre = (nt(dm_s[...], down_ref[...]) * slope).astype(BF)
    out_ref[:, :tile] = tn(u_s[...], dpre).astype(BF)
    out_ref[:, tile:] = tn(dm_s[...], hidden.astype(BF)).astype(BF)


def feed_grads(at, u, dmlp, up, down, bias, tile, count):
    width = up.shape[0]
    tokens = sum(part.shape[0] for part in u)
    return pl.pallas_call(
        functools.partial(grad_kernel, len(u), len(u) + len(dmlp)),
        grid_spec=pltpu.PrefetchScalarGridSpec(
            num_scalar_prefetch=1,
            grid=(count,),
            in_specs=[
                *[pl.BlockSpec(memory_space=pl.ANY)] * (len(u) + len(dmlp)),
                pl.BlockSpec((width, tile), lambda i, at: (0, at[0] + i)),
                pl.BlockSpec((tile, width), lambda i, at: (at[0] + i, 0)),
                pl.BlockSpec((1, tile), lambda i, at: (0, at[0] + i)),
            ],
            out_specs=pl.BlockSpec((width, 2 * tile), lambda i, at: (0, i)),
            scratch_shapes=[
                pltpu.VMEM((tokens, width), BF),
                pltpu.VMEM((tokens, width), BF),
                pltpu.SemaphoreType.DMA((len(u) + len(dmlp),)),
            ],
        ),
        out_shape=jax.ShapeDtypeStruct((width, 2 * tile * count), BF),
        compiler_params=params(),
        cost_estimate=cost(4 * tokens * width * tile * count, 4 * width * (tokens + 2 * tile * count)),
        name="feed_grads",
    )(at, *u, *dmlp, up, down, bias)


def normalize(values):
    average = jnp.mean(values, axis=-1, keepdims=True)
    centered = values - average
    variance = jnp.mean(centered * centered, axis=-1, keepdims=True)
    inv_std = lax.rsqrt(variance + EPS)
    return centered * inv_std, inv_std


def norm_back(gradient, scaled, inv_std, norm_gain):
    inner = gradient * norm_gain
    mean_one = jnp.mean(inner, axis=-1, keepdims=True)
    mean_two = jnp.mean(inner * scaled, axis=-1, keepdims=True)
    return inv_std * (inner - mean_one - scaled * mean_two)


def column_sum(values):
    return jnp.sum(values, axis=0, keepdims=True)


def by_rows(body, tokens, tile, ins, outs, name, sums=0):
    row = lambda columns: pl.BlockSpec((tile, columns), lambda i: (i, 0))
    specs = [row(a.shape[1]) if cut else whole(*a.shape) for a, cut in ins]
    shapes = [jax.ShapeDtypeStruct((tokens, columns), dtype) for columns, dtype in outs]
    out_specs = [row(columns) for columns, _ in outs]
    if sums:
        shapes.append(jax.ShapeDtypeStruct((sums, outs[0][0]), F32))
        out_specs.append(whole(sums, outs[0][0]))
    moved = sum(a.size * a.dtype.itemsize for a, _ in ins) + sum(s.size * s.dtype.itemsize for s in shapes)
    return pl.pallas_call(
        body,
        grid=(tokens // tile,),
        in_specs=specs,
        out_specs=out_specs,
        out_shape=shapes,
        compiler_params=params(),
        cost_estimate=cost(moved * 200, moved),
        name=name,
    )(*[a for a, _ in ins])


def first_kernel(x_ref, gain_ref, bias_ref, w_ref, wb_ref, v_ref, kv_ref):
    hat, _ = normalize(x_ref[...].astype(F32))
    v = (hat * gain_ref[...] + bias_ref[...]).astype(BF)
    v_ref[...] = v
    kv_ref[...] = (nn(v, w_ref[...]) + wb_ref[...]).astype(BF)


def second_kernel(x_ref, own_ref, far_ref, ob_ref, gain_ref, bias_ref, resid_ref, u_ref):
    proj = own_ref[...].astype(F32) + far_ref[...].astype(F32)
    resid = x_ref[...].astype(F32) + proj + ob_ref[...]
    resid_ref[...] = resid
    hat, _ = normalize(resid)
    u_ref[...] = (hat * gain_ref[...] + bias_ref[...]).astype(BF)


def second_back_kernel(own_ref, far_ref, resid_ref, dm_ref, gain_ref, dres_ref, dproj_ref, sums_ref):
    @pl.when(pl.program_id(0) == 0)
    def _():
        sums_ref[...] = jnp.zeros_like(sums_ref)

    du = own_ref[...].astype(F32) + far_ref[...].astype(F32)
    hat, inv_std = normalize(resid_ref[...])
    dout = dm_ref[...].astype(F32)
    dres = dout + norm_back(du, hat, inv_std, gain_ref[...])
    dres_ref[...] = dres
    dproj_ref[...] = dres.astype(BF)
    sums_ref[...] += jnp.concatenate(
        [column_sum(du * hat), column_sum(du), column_sum(dres), column_sum(dout)], axis=0
    )


def first_back_kernel(own_ref, far_ref, dkv_ref, w_ref, x_ref, dres_ref, gain_ref, grad_ref, sums_ref):
    @pl.when(pl.program_id(0) == 0)
    def _():
        sums_ref[...] = jnp.zeros_like(sums_ref)

    dv = own_ref[...].astype(F32) + far_ref[...].astype(F32) + nt(dkv_ref[...], w_ref[...])
    hat, inv_std = normalize(x_ref[...].astype(F32))
    grad_ref[...] = (dres_ref[...] + norm_back(dv, hat, inv_std, gain_ref[...])).astype(BF)
    sums_ref[...] += jnp.concatenate([column_sum(dv * hat), column_sum(dv)], axis=0)


def output_kernel(resid_ref, own_ref, far_ref, bias_ref, out_ref):
    mlp = own_ref[...].astype(F32) + far_ref[...].astype(F32)
    out_ref[...] = (resid_ref[...] + mlp + bias_ref[...]).astype(BF)


def project(left, right, transposed, tile, name, bias=None):
    tokens, depth = left.shape
    columns = right.shape[0] if transposed else right.shape[1]

    def body(*refs):
        product = (nt if transposed else nn)(refs[0][...], refs[1][...])
        if bias is not None:
            product = product + refs[2][...]
        refs[-1][...] = product.astype(BF)

    spec = pl.BlockSpec((tile, depth), lambda i: (i, 0)) if transposed else pl.BlockSpec((depth, tile), lambda i: (0, i))
    extra = [] if bias is None else [bias.reshape(1, columns)]
    return pl.pallas_call(
        body,
        grid=(columns // tile,),
        in_specs=[whole(tokens, depth), spec] + [pl.BlockSpec((1, tile), lambda i: (0, i))] * len(extra),
        out_specs=pl.BlockSpec((tokens, tile), lambda i: (0, i)),
        out_shape=jax.ShapeDtypeStruct((tokens, columns), BF),
        compiler_params=params(),
        cost_estimate=cost(tokens * depth * columns, 2 * (tokens * (depth + columns) + depth * columns)),
        name=name,
    )(left, right, *extra)


def rows_kernel(groups, shard, count, spot_ref, left_ref, *refs):
    rights, (keep_ref, x_ref, y_ref) = refs[:count], refs[count:]
    step = pl.program_id(0)
    dest = spot_ref[0] ^ step
    cols = [left_ref[:, pl.ds(pl.multiple_of((g * 4 + dest) * shard, shard), shard)] for g in range(groups)]
    left = jnp.concatenate(cols, axis=1)
    product = jnp.concatenate([tn(left, right[...]).astype(BF) for right in rights], axis=1)
    half = product.shape[0] // 2
    low, high = product[:half], product[half:]

    @pl.when(step == 0)
    def _():
        keep_ref[0], keep_ref[1] = low, high

    @pl.when(step == 1)
    def _():
        x_ref[0], keep_ref[3] = low, high

    @pl.when(step == 2)
    def _():
        keep_ref[2], y_ref[0] = low, high

    @pl.when(step == 3)
    def _():
        x_ref[1], y_ref[1] = low, high


def rows_grad(spot, left, rights, groups, shard):
    tokens, width = left.shape
    columns = sum(right.shape[1] for right in rights)
    half = groups * shard // 2
    return pl.pallas_call(
        functools.partial(rows_kernel, groups, shard, len(rights)),
        grid_spec=pltpu.PrefetchScalarGridSpec(
            num_scalar_prefetch=1,
            grid=(4,),
            in_specs=[whole(tokens, width), *[whole(*right.shape) for right in rights]],
            out_specs=[whole(4, half, columns), whole(2, half, columns), whole(2, half, columns)],
        ),
        out_shape=[jax.ShapeDtypeStruct((n, half, columns), BF) for n in (4, 2, 2)],
        compiler_params=params(),
        cost_estimate=cost(tokens * width * columns, 2 * (tokens + columns) * width),
        name="rows_grad",
    )(spot, left, *rights)


def add_kernel(keep_ref, x_ref, y_ref, low_ref, high_ref):
    low_ref[...] = (keep_ref[2].astype(F32) + x_ref[1].astype(F32)).astype(BF)
    high_ref[...] = (keep_ref[3].astype(F32) + y_ref[1].astype(F32)).astype(BF)


def add_passed(keep, from_x, from_y):
    shape = keep.shape[1:]
    return pl.pallas_call(
        add_kernel,
        in_specs=[whole(*keep.shape), whole(*from_x.shape), whole(*from_y.shape)],
        out_specs=[whole(*shape), whole(*shape)],
        out_shape=[jax.ShapeDtypeStruct(shape, BF)] * 2,
        grid=(1,),
        compiler_params=params(),
        cost_estimate=cost(0, 8 * shape[0] * shape[1] * 2),
        name="add_passed",
    )(keep, from_x, from_y)


def total_kernel(keep_ref, x_ref, y_ref, low_ref, high_ref, out_ref):
    half = low_ref.shape[0]
    out_ref[:half] = (keep_ref[0].astype(F32) + x_ref[0].astype(F32) + low_ref[...].astype(F32)).astype(BF)
    out_ref[half:] = (keep_ref[1].astype(F32) + y_ref[0].astype(F32) + high_ref[...].astype(F32)).astype(BF)


def add_total(keep, from_x, from_y, low, high):
    half, columns = low.shape
    arrays = (keep, from_x, from_y, low, high)
    return pl.pallas_call(
        total_kernel,
        in_specs=[whole(*a.shape) for a in arrays],
        out_specs=whole(2 * half, columns),
        out_shape=jax.ShapeDtypeStruct((2 * half, columns), BF),
        grid=(1,),
        compiler_params=params(),
        cost_estimate=cost(0, 16 * half * columns),
        name="add_total",
    )(*arrays)


def place_kernel(tile, counts, spot_ref, *refs):
    shares, (up_ref, down_ref) = refs[:-2], refs[-2:]
    units = up_ref.shape[1] // 4
    for bit in range(4):
        at = (spot_ref[0] ^ bit) * units
        tile_at = 0
        for piece, count in enumerate(counts):
            for k in range(count):
                block = shares[piece * 4 + bit][:, k * 2 * tile : (k + 1) * 2 * tile].astype(F32)
                spot = pl.ds(pl.multiple_of(at + (tile_at + k) * tile, tile), tile)
                up_ref[:, spot] = block[:, :tile]
                down_ref[spot, :] = block[:, tile:].T
            tile_at += count


def place_shares(spot, shares, counts, tile, units):
    shard = shares[0].shape[0]
    return pl.pallas_call(
        functools.partial(place_kernel, tile, counts),
        grid_spec=pltpu.PrefetchScalarGridSpec(
            num_scalar_prefetch=1,
            grid=(1,),
            in_specs=[whole(*share.shape) for share in shares],
            out_specs=[whole(shard, units), whole(units, shard)],
        ),
        out_shape=[jax.ShapeDtypeStruct((shard, units), F32), jax.ShapeDtypeStruct((units, shard), F32)],
        compiler_params=params(),
        cost_estimate=cost(0, 12 * shard * units),
        name="place_shares",
    )(spot, *shares)


def build(mesh):
    sp_size, dp_size = mesh.shape["sp"], mesh.shape["dp"]
    quads = sp_size // 4

    def swap(value, bit, keep=None):
        pairs = [(i, i ^ bit) for i in range(sp_size)]
        return lax.ppermute(value, "sp", pairs if keep is None else [p for p in pairs if keep(*p)])

    def swap_dp(value, bit):
        return lax.ppermute(value, "dp", [(i, i ^ bit) for i in range(dp_size)])

    def swap_tp(value):
        return lax.ppermute(value, "tp", [(0, 1), (1, 0)])

    def sum_all(vector):
        for bit in (1 << k for k in range(sp_size.bit_length() - 1)):
            vector = vector + swap(vector, bit)
        for bit in (1 << k for k in range(dp_size.bit_length() - 1)):
            vector = vector + swap_dp(vector, bit)
        return vector

    def half_of(own, core):
        half = own.shape[0] // 2
        return lax.dynamic_slice_in_dim(own, core * half, half, 0)

    def gather_quad(mine):
        groups = None if quads == 1 else [[q * 4 + r for r in range(4)] for q in range(quads)]
        return lax.all_gather(mine, "sp", axis=0, tiled=True, axis_index_groups=groups)

    def scatter_rest(value, after=None):
        if after is not None:
            value, _ = lax.optimization_barrier((value, after))
        value = lax.psum_scatter(value, "dp", scatter_dimension=0, tiled=True)
        if quads > 1:
            groups = [[q * 4 + r for q in range(quads)] for r in range(4)]
            value = lax.psum_scatter(value, "sp", scatter_dimension=0, tiled=True, axis_index_groups=groups)
        return value

    def scatter_quad(spot, left, rights, shard):
        groups = dp_size * quads
        if shard % 128 == 0:
            keep, to_x, to_y = rows_grad(spot.reshape(1), left, rights, groups, shard)
            from_x, from_y = swap(to_x, 1), swap(to_y, 2)
            low, high = add_passed(keep, from_x, from_y)
            total = add_total(keep, from_x, from_y, swap(low, 2), swap(high, 1))
            formed = keep
        else:
            formed = value = jnp.concatenate([tn(left, right).astype(BF) for right in rights], axis=1)
            value = value.reshape(groups, 4, shard, -1)
            block = lambda bit: lax.dynamic_index_in_dim(value, spot ^ bit, 1, keepdims=False)
            total = block(0).astype(F32)
            for bit in range(1, 4):
                total = total + swap(block(bit), bit).astype(F32)
            total = total.astype(BF).reshape(groups * shard, -1)
        return total, formed

    def per_device(
        inputs, lengths, first_gain, first_bias, query_weight, query_bias, keyval_weight, value_bias, output_weight,
        output_bias, second_gain, second_bias, up_weight, up_bias, down_weight, down_bias, cotangent,
    ):
        rows, seg, width = inputs.shape
        tokens = rows * seg
        place, core = lax.axis_index("sp").astype(jnp.int32), lax.axis_index("tp")
        spot = lax.rem(place, 4)
        row_len = seg * sp_size
        one_quad = quads == 1
        shard = width // (dp_size * sp_size)
        info = jnp.concatenate([jnp.stack([place * seg, spot if one_quad else 0 * spot]), lengths])
        row = lambda vector: vector.reshape(1, -1)

        x = inputs.reshape(tokens, width)
        dmlp = cotangent.reshape(tokens, width)
        tile = min(tokens, 128)
        x, dmlp_mine = lax.optimization_barrier((x, half_of(dmlp, core)))
        dmlp_quad = gather_quad(dmlp_mine)
        kv_bias = row(jnp.concatenate([jnp.zeros((HD,), F32), value_bias]))
        v_first, keyval = by_rows(
            first_kernel, tokens, tile,
            [(x, True), (row(first_gain), False), (row(first_bias), False), (keyval_weight, False), (kv_bias, False)],
            [(width, BF), (2 * HD, BF)], "first_norm",
        )
        if one_quad:
            pieces = [keyval, *[swap(keyval, bit, lambda a, b: a < b) for bit in (1, 2, 3)]]
            keyval_all = jnp.concatenate(pieces, axis=0).reshape(1, row_len, 2 * HD)
            size = seg
        else:
            keyval_all = lax.all_gather(keyval.reshape(rows, seg, 2 * HD), "sp", axis=1, tiled=True)
            size = min(512, row_len)

        query = project(v_first, query_weight, False, 512, "query", query_bias).reshape(rows, seg, -1)
        query, keyval_all = lax.optimization_barrier((query, keyval_all))

        attended, lse = attend_forward(info, query, keyval_all, size, 4)
        attended_flat = attended.reshape(tokens, -1)
        proj = project(attended_flat, output_weight, False, 512, "proj")
        resid, u_second = by_rows(
            second_kernel, tokens, tile,
            [(x, True), (proj, True), (swap_tp(proj), True), (row(output_bias), False), (row(second_gain), False),
             (row(second_bias), False)],
            [(width, F32), (width, BF)], "second_norm",
        )
        up_bias_row = row(up_bias)
        mlp, du, up_bias_grad, u_all, dmlp_other, du_far = feed_local(
            u_second, dmlp, dmlp_quad, up_weight, down_weight, up_bias_row, 512
        )
        u_all = [u_all.reshape(4 * tokens, width)]
        dmlp_all = [dmlp_quad, dmlp_other]
        dres, dproj, second_sums = by_rows(
            second_back_kernel, tokens, tile,
            [(du, True), (du_far, True), (resid, True), (dmlp, True), (row(second_gain), False)],
            [(width, F32), (width, BF)], "second_back", sums=4,
        )

        units = up_weight.shape[1]
        unit_tile = 256
        tiles = units // 4 // unit_tile
        counts = (1, 3) if tiles == 4 else (tiles,)
        shares, done, share = [], 0, None
        last = dproj
        for count in counts:
            at = (spot * tiles + done).astype(jnp.int32).reshape(1)
            done += count
            at, _ = lax.optimization_barrier((at, last))
            last = feed_grads(at, u_all, dmlp_all, up_weight, down_weight, up_bias_row, unit_tile, count)
            share = scatter_rest(last, share)
            blocks = [lax.dynamic_slice_in_dim(share, (spot ^ bit) * shard, shard, 0) for bit in range(4)]
            shares += [blocks[0], *[swap(blocks[bit], bit) for bit in range(1, 4)]]
        dproj, mlp, _ = lax.optimization_barrier((dproj, mlp, last))
        up_weight_grad, down_weight_grad = place_shares(spot.reshape(1), shares, counts, unit_tile, units)

        output_part, formed = scatter_quad(spot, dproj, [attended_flat], shard)
        dproj, _ = lax.optimization_barrier((dproj, formed))
        dattended = project(dproj, output_weight, True, 512, "dattended").reshape(rows, seg, -1)
        (outputs,) = by_rows(
            output_kernel, tokens, tile,
            [(resid, True), (mlp, True), (swap_tp(mlp), True), (row(down_bias), False)], [(width, BF)], "outputs",
        )

        dquery, query_bias_grad, dkey, dvalue = attend_backward(info, query, dattended, attended, lse, keyval_all, size, 4)
        dquery = dquery.reshape(tokens, -1)
        query_bias_grad = jnp.sum(query_bias_grad[:, 0], axis=0)
        dv_part = project(dquery, query_weight, True, 512, "dv")

        even = core == 0
        if one_quad:
            dkey, dvalue = dkey[0], dvalue[0]
            far = swap_tp(jnp.where(even, dvalue, dkey).astype(BF))
            half = jnp.where(even, dkey, dvalue) + far.astype(F32)
            own = half[:tokens]
            for bit in range(1, 4):
                block = half[bit * tokens : (bit + 1) * tokens].astype(BF)
                own = own + swap(block, bit, lambda a, b: a > b).astype(F32)
            own = lax.optimization_barrier(own.astype(BF))
            far = swap_tp(own)
        else:
            part = lax.psum(jnp.concatenate([dkey, dvalue], axis=2).astype(BF), "tp")
            both = lax.psum_scatter(part, "sp", scatter_dimension=1, tiled=True).reshape(tokens, 2 * HD)
            own, far = jnp.where(even, both[:, :HD], both[:, HD:]), jnp.where(even, both[:, HD:], both[:, :HD])
        dkeyval = jnp.concatenate([jnp.where(even, own, far), jnp.where(even, far, own)], axis=1)

        query_part, _ = scatter_quad(spot, v_first, [dquery, own], shard)
        merged, _ = lax.optimization_barrier((jnp.concatenate([output_part, query_part], axis=1), share))
        both = scatter_rest(merged).astype(F32)
        output_weight_grad, query_grad = both[:, : output_part.shape[1]].T, both[:, output_part.shape[1] :]
        own_grad = query_grad[:, -HD:]
        far_grad = swap_tp(own_grad)
        keyval_weight_grad = jnp.concatenate(
            [jnp.where(even, own_grad, far_grad), jnp.where(even, far_grad, own_grad)], axis=1
        )

        input_grad, first_sums = by_rows(
            first_back_kernel, tokens, tile,
            [(dv_part, True), (swap_tp(dv_part), True), (dkeyval, True), (keyval_weight, False), (x, True), (dres, True),
             (row(first_gain), False)],
            [(width, BF)], "first_back", sums=2,
        )
        vectors = [
            first_sums[0], first_sums[1], query_bias_grad, jnp.sum(dkeyval[:, HD:].astype(F32), axis=0), second_sums[2],
            second_sums[0], second_sums[1], up_bias_grad[0], second_sums[3],
        ]
        total = sum_all(jnp.concatenate(vectors))
        small, offset = [], 0
        for vector in vectors:
            small.append(total[offset : offset + vector.shape[0]])
            offset += vector.shape[0]
        return (
            outputs.reshape(rows, seg, width),
            input_grad.reshape(rows, seg, width),
            small[0],
            small[1],
            query_grad[:, :-HD],
            small[2],
            keyval_weight_grad,
            small[3],
            output_weight_grad,
            small[4],
            small[5],
            small[6],
            up_weight_grad,
            small[7],
            down_weight_grad,
            small[8],
        )

    return per_device


def solution(mesh):
    placed = (
        P("dp", "sp", None),
        P("dp"),
        P(),
        P(),
        P(None, "tp"),
        P("tp"),
        P(),
        P(),
        P("tp", None),
        P(),
        P(),
        P(),
        P(None, "tp"),
        P("tp"),
        P("tp", None),
        P(),
        P("dp", "sp", None),
    )
    return jax.shard_map(
        build(mesh),
        mesh=mesh,
        in_specs=placed,
        out_specs=(
            P("dp", "sp", None),
            P("dp", "sp", None),
            P(),
            P(),
            P(("dp", "sp"), "tp"),
            P("tp"),
            P(("dp", "sp"), None),
            P(),
            P("tp", ("dp", "sp")),
            P(),
            P(),
            P(),
            P(("dp", "sp"), "tp"),
            P("tp"),
            P("tp", ("dp", "sp")),
            P(),
        ),
        check_vma=False,
    )
```

```python
import functools
import math

import jax
import jax.numpy as jnp
from jax import lax
from jax.experimental import pallas as pl
from jax.experimental.pallas import tpu as pltpu
from jax.sharding import PartitionSpec as P

HD = 128
EPS = 1e-05
BF = jnp.bfloat16
F32 = jnp.float32
SCALE = 1.0 / math.sqrt(HD)
SCALE2 = SCALE * math.log2(math.e)
VMEM = 60 * 2**20
GELU_A = math.sqrt(2.0 / math.pi)
GELU_B = 0.044715


def nn(left, right):
    return jnp.dot(left, right, preferred_element_type=F32)


def nt(left, right):
    return lax.dot_general(left, right, (((1,), (1,)), ((), ())), preferred_element_type=F32)


def tn(left, right):
    return lax.dot_general(left, right, (((0,), (0,)), ((), ())), preferred_element_type=F32)


def params():
    return pltpu.CompilerParams(vmem_limit_bytes=VMEM)


def cost(macs, moved, weight=10):
    return pl.CostEstimate(flops=int(2 * macs * weight), bytes_accessed=int(moved * weight), transcendentals=0)


def whole(*shape):
    return pl.BlockSpec(shape, lambda *_: (0,) * len(shape))


def chunk_mask(first, length, chunk, size, seg, wide):
    key_pos = chunk * size + lax.broadcasted_iota(jnp.int32, (size, wide), 0)
    query_pos = first + lax.rem(lax.broadcasted_iota(jnp.int32, (size, wide), 1), seg)
    return (key_pos <= query_pos) & (key_pos < length)


def chunk_bounds(info_ref, row, seg, size):
    first, length = info_ref[0], info_ref[3 + row]
    full = jnp.minimum(first + 1, length) // size
    total = (jnp.minimum(first + seg, length) + size - 1) // size
    return first, length, full, total


def stack_heads(ref, heads):
    return jnp.concatenate([ref[0, :, h * HD : (h + 1) * HD] for h in range(heads)], axis=0)


def unstack_heads(ref, values, heads, seg):
    for h in range(heads):
        ref[0, :, h * HD : (h + 1) * HD] = values[h * seg : (h + 1) * seg]


def forward_kernel(size, heads, seg, info_ref, q_ref, kv_ref, o_ref, lse_ref, top_s, sum_s, acc_s):
    first, length, full, total = chunk_bounds(info_ref, pl.program_id(0), seg, size)
    q = stack_heads(q_ref, heads)
    top_s[...] = jnp.full_like(top_s, -1e30)
    sum_s[...] = jnp.zeros_like(sum_s)
    acc_s[...] = jnp.zeros_like(acc_s)

    def step(masked, chunk, carry):
        at = pl.ds(pl.multiple_of((chunk ^ info_ref[1]) * size, size), size)
        scores = nt(kv_ref[info_ref[2], 0, at, :], q) * SCALE2
        if masked:
            scores = jnp.where(chunk_mask(first, length, chunk, size, seg, heads * seg), scores, -1e30)
        old = top_s[...]
        new = jnp.maximum(old, jnp.max(scores, axis=0, keepdims=True))
        weights = jnp.exp2(scores - new)
        shrink = jnp.exp2(old - new)
        sum_s[...] = sum_s[...] * shrink + jnp.sum(weights, axis=0, keepdims=True)
        acc_s[...] = acc_s[...] * shrink + tn(kv_ref[1 - info_ref[2], 0, at, :], weights.astype(BF))
        top_s[...] = new
        return carry

    lax.fori_loop(0, full, functools.partial(step, False), 0)
    lax.fori_loop(full, total, functools.partial(step, True), 0)
    unstack_heads(o_ref, (acc_s[...] * (1.0 / sum_s[...])).T.astype(BF), heads, seg)
    lse_ref[0, 0] = top_s[...] + jnp.log2(sum_s[...])


def attend_forward(info, query, keyval, size, heads):
    rows, seg, width = query.shape
    length = keyval.shape[2]
    groups, wide = width // (HD * heads), heads * seg
    head_spec = pl.BlockSpec((1, seg, heads * HD), lambda r, h, info: (r, 0, h))
    return pl.pallas_call(
        functools.partial(forward_kernel, size, heads, seg),
        grid_spec=pltpu.PrefetchScalarGridSpec(
            num_scalar_prefetch=1,
            grid=(rows, groups),
            in_specs=[head_spec, pl.BlockSpec((2, 1, length, HD), lambda r, h, info: (0, r, 0, 0))],
            out_specs=[head_spec, pl.BlockSpec((1, 1, 1, wide), lambda r, h, info: (r, h, 0, 0))],
            scratch_shapes=[pltpu.VMEM((1, wide), F32), pltpu.VMEM((1, wide), F32), pltpu.VMEM((HD, wide), F32)],
        ),
        out_shape=[
            jax.ShapeDtypeStruct((rows, seg, width), BF),
            jax.ShapeDtypeStruct((rows, groups, 1, wide), F32),
        ],
        compiler_params=params(),
        cost_estimate=cost(8 * 10**9, 4 * 2**20),
        name="attend_forward",
    )(info, query, keyval)


def backward_kernel(
    size, heads, seg, info_ref, q_ref, do_ref, o_ref, lse_ref, kv_ref, dq_ref, bias_ref, dk_ref, dv_ref, dqt_s
):
    row, group = pl.program_id(0), pl.program_id(1)
    first, length, full, total = chunk_bounds(info_ref, row, seg, size)

    @pl.when(group == 0)
    def _():
        dk_ref[...] = jnp.zeros_like(dk_ref)
        dv_ref[...] = jnp.zeros_like(dv_ref)

    q, dout, out = (stack_heads(ref, heads) for ref in (q_ref, do_ref, o_ref))
    delta = jnp.sum((dout.astype(F32) * out.astype(F32)).T, axis=0, keepdims=True)
    lse = lse_ref[0, 0]
    dqt_s[...] = jnp.zeros_like(dqt_s)

    def step(masked, chunk, carry):
        at = pl.ds(pl.multiple_of((chunk ^ info_ref[1]) * size, size), size)
        keys = kv_ref[info_ref[2], 0, at, :]
        prob = jnp.exp2(nt(keys, q) * SCALE2 - lse)
        if masked:
            prob = jnp.where(chunk_mask(first, length, chunk, size, seg, heads * seg), prob, 0.0)
        dprob = nt(kv_ref[1 - info_ref[2], 0, at, :], dout)
        dscore = (prob * (dprob - delta)).astype(BF)
        dv_ref[0, at, :] += nn(prob.astype(BF), dout)
        dk_ref[0, at, :] += nn(dscore, q) * SCALE
        dqt_s[...] += tn(keys, dscore)
        return carry

    lax.fori_loop(0, full, functools.partial(step, False), 0)
    lax.fori_loop(full, total, functools.partial(step, True), 0)
    dq = (dqt_s[...] * SCALE).T.astype(BF)
    unstack_heads(dq_ref, dq, heads, seg)
    for h in range(heads):
        bias_ref[0, :, h * HD : (h + 1) * HD] = jnp.sum(
            dq[h * seg : (h + 1) * seg].astype(F32), axis=0, keepdims=True
        )


def attend_backward(info, query, dout, out, lse, keyval, size, heads):
    rows, seg, width = query.shape
    length = keyval.shape[2]
    groups, wide = width // (HD * heads), heads * seg
    head_spec = pl.BlockSpec((1, seg, heads * HD), lambda r, h, info: (r, 0, h))
    key_spec = pl.BlockSpec((1, length, HD), lambda r, h, info: (r, 0, 0))
    return pl.pallas_call(
        functools.partial(backward_kernel, size, heads, seg),
        grid_spec=pltpu.PrefetchScalarGridSpec(
            num_scalar_prefetch=1,
            grid=(rows, groups),
            in_specs=[
                head_spec,
                head_spec,
                head_spec,
                pl.BlockSpec((1, 1, 1, wide), lambda r, h, info: (r, h, 0, 0)),
                pl.BlockSpec((2, 1, length, HD), lambda r, h, info: (0, r, 0, 0)),
            ],
            out_specs=[head_spec, pl.BlockSpec((1, 1, heads * HD), lambda r, h, info: (r, 0, h)), key_spec, key_spec],
            scratch_shapes=[pltpu.VMEM((HD, wide), F32)],
        ),
        out_shape=[
            jax.ShapeDtypeStruct((rows, seg, width), BF),
            jax.ShapeDtypeStruct((rows, 1, width), F32),
            jax.ShapeDtypeStruct((rows, length, HD), F32),
            jax.ShapeDtypeStruct((rows, length, HD), F32),
        ],
        compiler_params=params(),
        cost_estimate=cost(12 * 10**9, 8 * 2**20),
        name="attend_backward",
    )(info, query, dout, out, lse, keyval)


def gelu_parts(v):
    square = v * v
    t = jnp.tanh(GELU_A * v * (1.0 + GELU_B * square))
    half = 0.5 * (1.0 + t)
    slope = half + 0.5 * v * (1.0 - t * t) * (GELU_A * (1.0 + 3.0 * GELU_B * square))
    return v * half, slope


def local_kernel(
    u_ref, dm_ref, dm_x_ref, dm_y_ref, up_ref, down_ref, bias_ref,
    mlp_ref, du_ref, dbias_ref, u_all_ref, dm_rest_ref,
    mlp_s, du_s, u_s, send, recv, local,
):
    step, last = pl.program_id(0), pl.num_programs(0) - 1
    dp, sp, tp = lax.axis_index("dp"), lax.axis_index("sp"), lax.axis_index("tp")
    half = u_ref.shape[0] // 2
    quarter = half // 2
    over_x, over_y, sibling = (dp, sp ^ 1, tp), (dp, sp ^ 2, tp), (dp, sp, 1 - tp)

    def remote(k, source, target, device):
        return pltpu.make_async_remote_copy(
            source, target, send.at[k], recv.at[k], device_id=device, device_id_type=pl.DeviceIdType.MESH
        )

    own = u_s.at[pl.ds(pl.multiple_of(tp * half, half), half), :]
    other = u_s.at[pl.ds(pl.multiple_of((1 - tp) * half, half), half), :]
    top, bottom = pl.ds(0, quarter), pl.ds(quarter, quarter)
    to_x = remote(0, own, u_all_ref.at[1], over_x)
    to_y = remote(1, own, u_all_ref.at[2], over_y)
    pass_y = remote(2, u_all_ref.at[1, top], u_all_ref.at[3, top], over_y)
    pass_x = remote(3, u_all_ref.at[2, bottom], u_all_ref.at[3, bottom], over_x)
    shares = [remote(3 + k, u_all_ref.at[k], u_all_ref.at[3 + k], sibling) for k in (1, 2, 3)]
    dm_pass_y = remote(7, dm_x_ref.at[top], dm_rest_ref.at[0, top], over_y)
    dm_pass_x = remote(8, dm_y_ref.at[bottom], dm_rest_ref.at[0, bottom], over_x)
    dm_shares = [
        remote(9, dm_x_ref, dm_rest_ref.at[1], sibling),
        remote(10, dm_y_ref, dm_rest_ref.at[2], sibling),
        remote(11, dm_rest_ref.at[0], dm_rest_ref.at[3], sibling),
    ]
    keep_own = pltpu.make_async_copy(own, u_all_ref.at[0], local.at[0])
    keep_other = pltpu.make_async_copy(other, u_all_ref.at[7], local.at[1])

    @pl.when(step == 0)
    def _():
        barrier = pltpu.get_barrier_semaphore()
        for device in (over_x, over_y, sibling):
            pl.semaphore_signal(barrier, inc=1, device_id=device, device_id_type=pl.DeviceIdType.MESH)
        pl.semaphore_wait(barrier, 3)
        u_s[...] = u_ref[...]
        to_x.start()
        to_y.start()
        for copy in (dm_pass_y, dm_pass_x, dm_shares[0], dm_shares[1]):
            copy.start()
        keep_own.start()
        keep_other.start()
        mlp_s[...] = jnp.zeros_like(mlp_s)
        du_s[...] = jnp.zeros_like(du_s)

    @pl.when(step == (last + 1) * 5 // 8)
    def _():
        to_x.wait_recv()
        to_y.wait_recv()
        pass_y.start()
        pass_x.start()
        shares[0].start()
        shares[1].start()

    @pl.when(step == last)
    def _():
        dm_pass_y.wait_recv()
        dm_pass_x.wait_recv()
        dm_shares[2].start()

    hidden, slope = gelu_parts(nn(u_ref[...], up_ref[...]) + bias_ref[...])
    mlp_s[...] += nn(hidden.astype(BF), down_ref[...])
    dpre = (nt(dm_ref[...], down_ref[...]) * slope).astype(BF)
    dbias_ref[...] = jnp.sum(dpre.astype(F32), axis=0, keepdims=True)
    du_s[...] += nt(dpre, up_ref[...])

    @pl.when(step == last)
    def _():
        pass_y.wait_recv()
        pass_x.wait_recv()
        shares[2].start()
        mlp_ref[...] = mlp_s[...].astype(BF)
        du_ref[...] = du_s[...].astype(BF)
        for copy in (to_x, to_y, pass_y, pass_x, dm_pass_y, dm_pass_x):
            copy.wait_send()
        for copy in (*shares, *dm_shares):
            copy.wait()
        keep_own.wait()
        keep_other.wait()


def feed_local(u, dmlp, fars, up, down, bias, tile):
    tokens, width = u.shape
    units = up.shape[1]
    block = whole(tokens, width)
    anywhere = pl.BlockSpec(memory_space=pl.ANY)
    return pl.pallas_call(
        local_kernel,
        grid=(units // tile,),
        in_specs=[
            block,
            block,
            anywhere,
            anywhere,
            pl.BlockSpec((width, tile), lambda i: (0, i)),
            pl.BlockSpec((tile, width), lambda i: (i, 0)),
            pl.BlockSpec((1, tile), lambda i: (0, i)),
        ],
        out_specs=[block, block, pl.BlockSpec((1, tile), lambda i: (0, i)), anywhere, anywhere],
        out_shape=[
            jax.ShapeDtypeStruct((tokens, width), BF),
            jax.ShapeDtypeStruct((tokens, width), BF),
            jax.ShapeDtypeStruct((1, units), F32),
            jax.ShapeDtypeStruct((8, tokens // 2, width), BF),
            jax.ShapeDtypeStruct((4, tokens // 2, width), BF),
        ],
        scratch_shapes=[
            pltpu.VMEM((tokens, width), F32),
            pltpu.VMEM((tokens, width), F32),
            pltpu.VMEM((tokens, width), BF),
            pltpu.SemaphoreType.DMA((12,)),
            pltpu.SemaphoreType.DMA((12,)),
            pltpu.SemaphoreType.DMA((2,)),
        ],
        compiler_params=pltpu.CompilerParams(vmem_limit_bytes=VMEM, collective_id=0, has_side_effects=True),
        cost_estimate=cost(4 * tokens * width * units, 4 * width * units),
        name="feed_local",
    )(u, dmlp, *fars, up, down, bias)


def grad_kernel(u_parts, parts, at_ref, *refs):
    pieces, (up_ref, down_ref, bias_ref, out_ref, u_s, dm_s, sems) = refs[:parts], refs[parts:]

    def copies(target):
        offset = 0
        for k in range(u_parts) if target is u_s else range(u_parts, parts):
            piece = pieces[k]
            yield pltpu.make_async_copy(piece, target.at[pl.ds(offset, piece.shape[0]), :], sems.at[k])
            offset += piece.shape[0]

    @pl.when(pl.program_id(0) == 0)
    def _():
        for copy in copies(u_s):
            copy.start()
        for copy in copies(dm_s):
            copy.start()
        for copy in copies(u_s):
            copy.wait()
        for copy in copies(dm_s):
            copy.wait()

    tile = up_ref.shape[1]
    hidden, slope = gelu_parts(nn(u_s[...], up_ref[...]) + bias_ref[...])
    dpre = (nt(dm_s[...], down_ref[...]) * slope).astype(BF)
    out_ref[:, :tile] = tn(dpre, u_s[...]).T.astype(BF)
    out_ref[:, tile:] = tn(hidden.astype(BF), dm_s[...]).T.astype(BF)


def feed_grads(at, u, dmlp, up, down, bias, tile, count):
    width = up.shape[0]
    tokens = sum(part.shape[0] for part in u)
    return pl.pallas_call(
        functools.partial(grad_kernel, len(u), len(u) + len(dmlp)),
        grid_spec=pltpu.PrefetchScalarGridSpec(
            num_scalar_prefetch=1,
            grid=(count,),
            in_specs=[
                *[pl.BlockSpec(memory_space=pl.ANY)] * (len(u) + len(dmlp)),
                pl.BlockSpec((width, tile), lambda i, at: (0, at[0] + i)),
                pl.BlockSpec((tile, width), lambda i, at: (at[0] + i, 0)),
                pl.BlockSpec((1, tile), lambda i, at: (0, at[0] + i)),
            ],
            out_specs=pl.BlockSpec((width, 2 * tile), lambda i, at: (0, i)),
            scratch_shapes=[
                pltpu.VMEM((tokens, width), BF),
                pltpu.VMEM((tokens, width), BF),
                pltpu.SemaphoreType.DMA((len(u) + len(dmlp),)),
            ],
        ),
        out_shape=jax.ShapeDtypeStruct((width, 2 * tile * count), BF),
        compiler_params=params(),
        cost_estimate=cost(4 * tokens * width * tile * count, 4 * width * (tokens + 2 * tile * count)),
        name="feed_grads",
    )(at, *u, *dmlp, up, down, bias)


def normalize(values):
    average = jnp.mean(values, axis=-1, keepdims=True)
    centered = values - average
    variance = jnp.mean(centered * centered, axis=-1, keepdims=True)
    inv_std = lax.rsqrt(variance + EPS)
    return centered * inv_std, inv_std


def norm_back(gradient, scaled, inv_std, norm_gain):
    inner = gradient * norm_gain
    mean_one = jnp.mean(inner, axis=-1, keepdims=True)
    mean_two = jnp.mean(inner * scaled, axis=-1, keepdims=True)
    return inv_std * (inner - mean_one - scaled * mean_two)


def column_sum(values):
    return jnp.sum(values, axis=0, keepdims=True)


def by_rows(body, tokens, tile, ins, outs, name, sums=0):
    row = lambda columns: pl.BlockSpec((tile, columns), lambda i: (i, 0))
    specs = [row(a.shape[1]) if cut else whole(*a.shape) for a, cut in ins]
    shapes = [jax.ShapeDtypeStruct((tokens, columns), dtype) for columns, dtype in outs]
    out_specs = [row(columns) for columns, _ in outs]
    if sums:
        shapes.append(jax.ShapeDtypeStruct((sums, outs[0][0]), F32))
        out_specs.append(whole(sums, outs[0][0]))
    moved = sum(a.size * a.dtype.itemsize for a, _ in ins) + sum(s.size * s.dtype.itemsize for s in shapes)
    return pl.pallas_call(
        body,
        grid=(tokens // tile,),
        in_specs=specs,
        out_specs=out_specs,
        out_shape=shapes,
        compiler_params=params(),
        cost_estimate=cost(moved * 200, moved),
        name=name,
    )(*[a for a, _ in ins])


def first_kernel(x_ref, gain_ref, bias_ref, w_ref, wb_ref, v_ref, kv_ref):
    hat, _ = normalize(x_ref[...].astype(F32))
    v = (hat * gain_ref[...] + bias_ref[...]).astype(BF)
    v_ref[...] = v
    kv_ref[...] = (nn(v, w_ref[...]) + wb_ref[...]).astype(BF)


def exchange_rows(part, finish, tokens, tile, firsts, ins, outs, name, collective_id, sums=0):
    count = tokens // tile
    now, late = lambda i: (jnp.minimum(i, count - 1), 0), lambda i: (jnp.maximum(i - 1, 0), 0)
    spec = lambda a, cut, at: pl.BlockSpec((tile, a.shape[1]), at) if cut else whole(*a.shape)
    width = outs[0][0]

    def kernel(*refs):
        first_refs, refs = refs[: len(firsts)], refs[len(firsts) :]
        in_refs, refs = refs[: len(ins)], refs[len(ins) :]
        out_refs, (own_s, far_s, send, recv) = refs[:-4], refs[-4:]
        step = pl.program_id(0)
        sibling = (lax.axis_index("dp"), lax.axis_index("sp"), 1 - lax.axis_index("tp"))

        def copy(k):
            return pltpu.make_async_remote_copy(
                own_s.at[k], far_s.at[k], send.at[k], recv.at[k],
                device_id=sibling, device_id_type=pl.DeviceIdType.MESH,
            )

        @pl.when(step == 0)
        def _():
            barrier = pltpu.get_barrier_semaphore()
            pl.semaphore_signal(barrier, inc=1, device_id=sibling, device_id_type=pl.DeviceIdType.MESH)
            pl.semaphore_wait(barrier, 1)
            if sums:
                out_refs[-1][...] = jnp.zeros_like(out_refs[-1])

        @pl.when(step < count)
        def _():
            own_s[step] = part(*first_refs).astype(BF)
            copy(step).start()

        @pl.when(step > 0)
        def _():
            copy(step - 1).wait_recv()
            finish(own_s[step - 1].astype(F32) + far_s[step - 1].astype(F32), in_refs, out_refs)

        @pl.when(step == count)
        def _():
            for k in range(count):
                copy(k).wait_send()

    shapes = [jax.ShapeDtypeStruct((tokens, columns), dtype) for columns, dtype in outs]
    out_specs = [pl.BlockSpec((tile, columns), late) for columns, _ in outs]
    if sums:
        shapes.append(jax.ShapeDtypeStruct((sums, width), F32))
        out_specs.append(whole(sums, width))
    moved = sum(a.size * a.dtype.itemsize for a, _ in (*firsts, *ins))
    return pl.pallas_call(
        kernel,
        grid=(count + 1,),
        in_specs=[spec(a, cut, now) for a, cut in firsts] + [spec(a, cut, late) for a, cut in ins],
        out_specs=out_specs,
        out_shape=shapes,
        scratch_shapes=[
            pltpu.VMEM((count, tile, width), BF),
            pltpu.VMEM((count, tile, width), BF),
            pltpu.SemaphoreType.DMA((count,)),
            pltpu.SemaphoreType.DMA((count,)),
        ],
        compiler_params=pltpu.CompilerParams(vmem_limit_bytes=VMEM, collective_id=collective_id, has_side_effects=True),
        cost_estimate=cost(moved * 200, moved),
        name=name,
    )(*[a for a, _ in firsts], *[a for a, _ in ins])


def proj_part(attended_ref, w_ref):
    return nn(attended_ref[...], w_ref[...])


def second_finish(proj, ins, outs):
    x_ref, ob_ref, gain_ref, bias_ref = ins
    resid_ref, u_ref = outs
    resid = x_ref[...].astype(F32) + proj + ob_ref[...]
    resid_ref[...] = resid
    hat, _ = normalize(resid)
    u_ref[...] = (hat * gain_ref[...] + bias_ref[...]).astype(BF)


def dv_part(dq_ref, w_ref):
    return nt(dq_ref[...], w_ref[...])


def first_finish(dv, ins, outs):
    dkv_ref, w_ref, x_ref, dres_ref, gain_ref = ins
    grad_ref, sums_ref = outs
    dv = dv + nt(dkv_ref[...], w_ref[...])
    hat, inv_std = normalize(x_ref[...].astype(F32))
    grad_ref[...] = (dres_ref[...] + norm_back(dv, hat, inv_std, gain_ref[...])).astype(BF)
    sums_ref[...] += jnp.concatenate([column_sum(dv * hat), column_sum(dv)], axis=0)


def second_back_kernel(own_ref, far_ref, resid_ref, dm_ref, gain_ref, dres_ref, dproj_ref, sums_ref):
    @pl.when(pl.program_id(0) == 0)
    def _():
        sums_ref[...] = jnp.zeros_like(sums_ref)

    du = own_ref[...].astype(F32) + far_ref[...].astype(F32)
    hat, inv_std = normalize(resid_ref[...])
    dout = dm_ref[...].astype(F32)
    dres = dout + norm_back(du, hat, inv_std, gain_ref[...])
    dres_ref[...] = dres
    dproj_ref[...] = dres.astype(BF)
    sums_ref[...] += jnp.concatenate(
        [column_sum(du * hat), column_sum(du), column_sum(dres), column_sum(dout)], axis=0
    )


def output_kernel(resid_ref, own_ref, far_ref, bias_ref, out_ref):
    mlp = own_ref[...].astype(F32) + far_ref[...].astype(F32)
    out_ref[...] = (resid_ref[...] + mlp + bias_ref[...]).astype(BF)


def project(left, right, transposed, tile, name, bias=None):
    tokens, depth = left.shape
    columns = right.shape[0] if transposed else right.shape[1]

    def body(*refs):
        product = (nt if transposed else nn)(refs[0][...], refs[1][...])
        if bias is not None:
            product = product + refs[2][...]
        refs[-1][...] = product.astype(BF)

    spec = pl.BlockSpec((tile, depth), lambda i: (i, 0)) if transposed else pl.BlockSpec((depth, tile), lambda i: (0, i))
    extra = [] if bias is None else [bias.reshape(1, columns)]
    return pl.pallas_call(
        body,
        grid=(columns // tile,),
        in_specs=[whole(tokens, depth), spec] + [pl.BlockSpec((1, tile), lambda i: (0, i))] * len(extra),
        out_specs=pl.BlockSpec((tokens, tile), lambda i: (0, i)),
        out_shape=jax.ShapeDtypeStruct((tokens, columns), BF),
        compiler_params=params(),
        cost_estimate=cost(tokens * depth * columns, 2 * (tokens * (depth + columns) + depth * columns)),
        name=name,
    )(left, right, *extra)


def rows_kernel(groups, shard, count, spot_ref, left_ref, *refs):
    rights, (keep_ref, x_ref, y_ref) = refs[:count], refs[count:]
    step = pl.program_id(0)
    dest = spot_ref[0] ^ step
    cols = [left_ref[:, pl.ds(pl.multiple_of((g * 4 + dest) * shard, shard), shard)] for g in range(groups)]
    left = jnp.concatenate(cols, axis=1)
    product = jnp.concatenate([tn(left, right[...]).astype(BF) for right in rights], axis=1)
    half = product.shape[0] // 2
    low, high = product[:half], product[half:]

    @pl.when(step == 0)
    def _():
        keep_ref[0], keep_ref[1] = low, high

    @pl.when(step == 1)
    def _():
        x_ref[0], keep_ref[3] = low, high

    @pl.when(step == 2)
    def _():
        keep_ref[2], y_ref[0] = low, high

    @pl.when(step == 3)
    def _():
        x_ref[1], y_ref[1] = low, high


def rows_grad(spot, left, rights, groups, shard):
    tokens, width = left.shape
    columns = sum(right.shape[1] for right in rights)
    half = groups * shard // 2
    return pl.pallas_call(
        functools.partial(rows_kernel, groups, shard, len(rights)),
        grid_spec=pltpu.PrefetchScalarGridSpec(
            num_scalar_prefetch=1,
            grid=(4,),
            in_specs=[whole(tokens, width), *[whole(*right.shape) for right in rights]],
            out_specs=[whole(4, half, columns), whole(2, half, columns), whole(2, half, columns)],
        ),
        out_shape=[jax.ShapeDtypeStruct((n, half, columns), BF) for n in (4, 2, 2)],
        compiler_params=params(),
        cost_estimate=cost(tokens * width * columns, 2 * (tokens + columns) * width),
        name="rows_grad",
    )(spot, left, *rights)


def add_kernel(keep_ref, x_ref, y_ref, low_ref, high_ref):
    low_ref[...] = (keep_ref[2].astype(F32) + x_ref[1].astype(F32)).astype(BF)
    high_ref[...] = (keep_ref[3].astype(F32) + y_ref[1].astype(F32)).astype(BF)


def add_passed(keep, from_x, from_y):
    shape = keep.shape[1:]
    return pl.pallas_call(
        add_kernel,
        in_specs=[whole(*keep.shape), whole(*from_x.shape), whole(*from_y.shape)],
        out_specs=[whole(*shape), whole(*shape)],
        out_shape=[jax.ShapeDtypeStruct(shape, BF)] * 2,
        grid=(1,),
        compiler_params=params(),
        cost_estimate=cost(0, 8 * shape[0] * shape[1] * 2),
        name="add_passed",
    )(keep, from_x, from_y)


def total_kernel(ready, *refs):
    out_ref, offset = refs[-1], 0
    for k in range(ready):
        columns = refs[k].shape[1]
        out_ref[:, offset : offset + columns] = refs[k][...]
        offset += columns
    for k in range(ready, len(refs) - 1, 5):
        keep_ref, x_ref, y_ref, low_ref, high_ref = refs[k : k + 5]
        half, columns = low_ref.shape
        at = slice(offset, offset + columns)
        out_ref[:half, at] = (keep_ref[0].astype(F32) + x_ref[0].astype(F32) + low_ref[...].astype(F32)).astype(BF)
        out_ref[half:, at] = (keep_ref[1].astype(F32) + y_ref[0].astype(F32) + high_ref[...].astype(F32)).astype(BF)
        offset += columns


def add_total(ready, quads):
    arrays = [*ready, *[array for quad in quads for array in quad]]
    lead = 2 * quads[0][3].shape[0]
    columns = sum(a.shape[1] for a in ready) + sum(quad[3].shape[1] for quad in quads)
    return pl.pallas_call(
        functools.partial(total_kernel, len(ready)),
        in_specs=[whole(*a.shape) for a in arrays],
        out_specs=whole(lead, columns),
        out_shape=jax.ShapeDtypeStruct((lead, columns), BF),
        grid=(1,),
        compiler_params=params(),
        cost_estimate=cost(0, 8 * lead * columns),
        name="add_total",
    )(*arrays)


def finish_kernel(both_ref, out_ref, query_ref, kv_ref):
    first, second = out_ref.shape[0], query_ref.shape[1]
    out_ref[...] = both_ref[:, :first].astype(F32).T
    query_ref[...] = both_ref[:, first : first + second].astype(F32)
    kv_ref[...] = both_ref[:, first + second :].astype(F32)


def finish(both, first, second):
    shard, columns = both.shape
    shapes = [(first, shard), (shard, second), (shard, columns - first - second)]
    return pl.pallas_call(
        finish_kernel,
        in_specs=[whole(shard, columns)],
        out_specs=[whole(*shape) for shape in shapes],
        out_shape=[jax.ShapeDtypeStruct(shape, F32) for shape in shapes],
        grid=(1,),
        compiler_params=params(),
        cost_estimate=cost(0, 6 * shard * columns),
        name="finish",
    )(both)


def place_kernel(tile, counts, spot_ref, *refs):
    shares, (up_ref, down_ref) = refs[:-2], refs[-2:]
    units = up_ref.shape[1] // 4
    for bit in range(4):
        at = (spot_ref[0] ^ bit) * units
        tile_at = 0
        for piece, count in enumerate(counts):
            for k in range(count):
                block = shares[piece * 4 + bit][:, k * 2 * tile : (k + 1) * 2 * tile].astype(F32)
                spot = pl.ds(pl.multiple_of(at + (tile_at + k) * tile, tile), tile)
                up_ref[:, spot] = block[:, :tile]
                down_ref[spot, :] = block[:, tile:].T
            tile_at += count


def place_shares(spot, shares, counts, tile, units):
    shard = shares[0].shape[0]
    return pl.pallas_call(
        functools.partial(place_kernel, tile, counts),
        grid_spec=pltpu.PrefetchScalarGridSpec(
            num_scalar_prefetch=1,
            grid=(1,),
            in_specs=[whole(*share.shape) for share in shares],
            out_specs=[whole(shard, units), whole(units, shard)],
        ),
        out_shape=[jax.ShapeDtypeStruct((shard, units), F32), jax.ShapeDtypeStruct((units, shard), F32)],
        compiler_params=params(),
        cost_estimate=cost(0, 12 * shard * units),
        name="place_shares",
    )(spot, *shares)


def build(mesh):
    sp_size, dp_size = mesh.shape["sp"], mesh.shape["dp"]
    quads = sp_size // 4

    def swap(value, bit, keep=None):
        pairs = [(i, i ^ bit) for i in range(sp_size)]
        return lax.ppermute(value, "sp", pairs if keep is None else [p for p in pairs if keep(*p)])

    def swap_dp(value, bit):
        return lax.ppermute(value, "dp", [(i, i ^ bit) for i in range(dp_size)])

    def swap_tp(value):
        return lax.ppermute(value, "tp", [(0, 1), (1, 0)])

    def sum_all(vector):
        for bit in (1 << k for k in range(sp_size.bit_length() - 1)):
            vector = vector + swap(vector, bit)
        for bit in (1 << k for k in range(dp_size.bit_length() - 1)):
            vector = vector + swap_dp(vector, bit)
        return vector

    def half_of(own, core):
        half = own.shape[0] // 2
        return lax.dynamic_slice_in_dim(own, core * half, half, 0)

    def scatter_rest(value, after=None):
        if after is not None:
            value, _ = lax.optimization_barrier((value, after))
        value = lax.psum_scatter(value, "dp", scatter_dimension=0, tiled=True)
        if quads > 1:
            groups = [[q * 4 + r for q in range(quads)] for r in range(4)]
            value = lax.psum_scatter(value, "sp", scatter_dimension=0, tiled=True, axis_index_groups=groups)
        return value

    def start_quad(spot, left, rights, shard):
        groups = dp_size * quads
        if shard % 128 == 0:
            keep, to_x, to_y = rows_grad(spot.reshape(1), left, rights, groups, shard)
            return [keep, swap(to_x, 1), swap(to_y, 2)]
        value = jnp.concatenate([tn(left, right).astype(BF) for right in rights], axis=1)
        value = value.reshape(groups, 4, shard, -1)
        blocks = [
            lax.dynamic_index_in_dim(value, spot ^ bit, 1, keepdims=False).reshape(groups * shard, -1)
            for bit in range(4)
        ]
        return [blocks[0], *[swap(blocks[bit], bit) for bit in range(1, 4)]]

    def middle_quad(parts):
        if len(parts) == 4:
            return parts
        low, high = add_passed(*parts)
        return [*parts, swap(low, 2), swap(high, 1)]

    def end_quads(ready, quads):
        if len(quads[0]) == 5:
            return add_total(ready, quads)
        return jnp.concatenate([*ready, *[sum(p.astype(F32) for p in quad).astype(BF) for quad in quads]], axis=1)

    def per_device(
        inputs, lengths, first_gain, first_bias, query_weight, query_bias, keyval_weight, value_bias, output_weight,
        output_bias, second_gain, second_bias, up_weight, up_bias, down_weight, down_bias, cotangent,
    ):
        rows, seg, width = inputs.shape
        tokens = rows * seg
        place, core = lax.axis_index("sp").astype(jnp.int32), lax.axis_index("tp")
        spot = lax.rem(place, 4)
        row_len = seg * sp_size
        one_quad = quads == 1
        shard = width // (dp_size * sp_size)
        even = core == 0
        info = jnp.concatenate([jnp.stack([place * seg, spot if one_quad else 0 * spot, core.astype(jnp.int32)]), lengths])
        row = lambda vector: vector.reshape(1, -1)

        x = inputs.reshape(tokens, width)
        dmlp = cotangent.reshape(tokens, width)
        tile = min(tokens, 128)
        x, dmlp_mine, dmlp_other = lax.optimization_barrier((x, half_of(dmlp, core), half_of(dmlp, 1 - core)))
        half_weight = lax.dynamic_slice_in_dim(keyval_weight, core * HD, HD, 1)
        half_bias = row(jnp.where(even, 0.0, value_bias))
        v_first, kv_half = by_rows(
            first_kernel, tokens, tile,
            [(x, True), (row(first_gain), False), (row(first_bias), False), (half_weight, False), (half_bias, False)],
            [(width, BF), (HD, BF)], "first_norm",
        )
        if one_quad:
            pieces = [kv_half, *[swap(kv_half, bit, lambda a, b: a < b) for bit in (1, 2, 3)]]
            kv_mine = jnp.concatenate(pieces, axis=0).reshape(1, row_len, HD)
            size = seg
        else:
            kv_mine = lax.all_gather(kv_half.reshape(rows, seg, HD), "sp", axis=1, tiled=True)
            size = min(512, row_len)
        dmlp_send, kv_mine = lax.optimization_barrier((dmlp_mine, kv_mine))
        dmlp_fars = [swap(dmlp_send, bit) for bit in (1, 2)]
        keyval_all = jnp.stack([kv_mine, swap_tp(kv_mine)])

        query = project(v_first, query_weight, False, 512, "query", query_bias).reshape(rows, seg, -1)
        query, keyval_all = lax.optimization_barrier((query, keyval_all))

        attended, lse = attend_forward(info, query, keyval_all, size, 4)
        attended_flat = attended.reshape(tokens, -1)
        resid, u_second = exchange_rows(
            proj_part, second_finish, tokens, tile, [(attended_flat, True), (output_weight, False)],
            [(x, True), (row(output_bias), False), (row(second_gain), False), (row(second_bias), False)],
            [(width, F32), (width, BF)], "second_norm", 1,
        )
        up_bias_row = row(up_bias)
        mlp, du, up_bias_grad, u_all, dmlp_rest = feed_local(
            u_second, dmlp, dmlp_fars, up_weight, down_weight, up_bias_row, 512
        )
        u_all = [u_all.reshape(4 * tokens, width)]
        dmlp_all = [dmlp_mine, *dmlp_fars, dmlp_rest.reshape(-1, width), dmlp_other]

        units = up_weight.shape[1]
        unit_tile = 256
        tiles = units // 4 // unit_tile
        counts = (1, tiles - 1)
        feed_part = lambda at, count: feed_grads(
            at.reshape(1), u_all, dmlp_all, up_weight, down_weight, up_bias_row, unit_tile, count
        )
        shares = []

        def spread(share):
            blocks = [lax.dynamic_slice_in_dim(share, (spot ^ bit) * shard, shard, 0) for bit in range(4)]
            shares.extend([blocks[0], *[swap(blocks[bit], bit) for bit in range(1, 4)]])

        first_part = feed_part(spot * tiles, counts[0])
        first_share = scatter_rest(first_part)
        spread(first_share)
        at, _ = lax.optimization_barrier((spot * tiles + counts[0], first_part))
        last_part = feed_part(at, counts[1])
        last_share = scatter_rest(last_part)
        spread(last_share)

        du_far, _ = lax.optimization_barrier((swap_tp(du), last_part))
        dres, dproj, second_sums = by_rows(
            second_back_kernel, tokens, tile,
            [(du, True), (du_far, True), (resid, True), (dmlp, True), (row(second_gain), False)],
            [(width, F32), (width, BF)], "second_back", sums=4,
        )
        output_quad = start_quad(spot, dproj, [attended_flat], shard)
        dproj, output_keep = lax.optimization_barrier((dproj, output_quad[0]))
        dattended = project(dproj, output_weight, True, 512, "dattended").reshape(rows, seg, -1)
        dattended, first_shares = lax.optimization_barrier((dattended, shares[:4]))
        shares[:4] = first_shares
        up_weight_grad, down_weight_grad = place_shares(spot.reshape(1), shares, counts, unit_tile, units)
        (outputs,) = by_rows(
            output_kernel, tokens, tile,
            [(resid, True), (mlp, True), (swap_tp(mlp), True), (row(down_bias), False)], [(width, BF)], "outputs",
        )

        dquery, query_bias_grad, dkey, dvalue = attend_backward(info, query, dattended, attended, lse, keyval_all, size, 4)
        dquery = dquery.reshape(tokens, -1)
        query_bias_grad = jnp.sum(query_bias_grad[:, 0], axis=0)
        dquery, output_quad = lax.optimization_barrier((dquery, [output_keep, *output_quad[1:]]))
        output_quad = middle_quad(output_quad)
        query_quad = start_quad(spot, v_first, [dquery], shard)
        dkey, dvalue, query_first = lax.optimization_barrier((dkey, dvalue, query_quad[0]))
        query_quad[0] = query_first
        output_part = end_quads([], [output_quad])

        if one_quad:
            dkey, dvalue = dkey[0], dvalue[0]
            far = swap_tp(jnp.where(even, dvalue, dkey).astype(BF))
            half = jnp.where(even, dkey, dvalue) + far.astype(F32)
            own = half[:tokens]
            for bit in range(1, 4):
                block = half[bit * tokens : (bit + 1) * tokens].astype(BF)
                own = own + swap(block, bit, lambda a, b: a > b).astype(F32)
            own = lax.optimization_barrier(own.astype(BF))
            far = swap_tp(own)
        else:
            part = lax.psum(jnp.concatenate([dkey, dvalue], axis=2).astype(BF), "tp")
            both = lax.psum_scatter(part, "sp", scatter_dimension=1, tiled=True).reshape(tokens, 2 * HD)
            own, far = jnp.where(even, both[:, :HD], both[:, HD:]), jnp.where(even, both[:, HD:], both[:, :HD])
        dkeyval = jnp.concatenate([jnp.where(even, own, far), jnp.where(even, far, own)], axis=1)

        kv_quad = start_quad(spot, v_first, [dkeyval], shard)
        merged = end_quads([output_part], [middle_quad(query_quad), middle_quad(kv_quad)])
        both = scatter_rest(merged, last_share)
        output_weight_grad, query_weight_grad, keyval_weight_grad = finish(
            both, output_weight.shape[0], query_weight.shape[1]
        )

        input_grad, first_sums = exchange_rows(
            dv_part, first_finish, tokens, tile, [(dquery, True), (query_weight, False)],
            [(dkeyval, True), (keyval_weight, False), (x, True), (dres, True), (row(first_gain), False)],
            [(width, BF)], "first_back", 2, sums=2,
        )
        vectors = [
            first_sums[0], first_sums[1], query_bias_grad, jnp.sum(dkeyval[:, HD:].astype(F32), axis=0), second_sums[2],
            second_sums[0], second_sums[1], up_bias_grad[0], second_sums[3],
        ]
        vector, _ = lax.optimization_barrier((jnp.concatenate(vectors), merged))
        total = sum_all(vector)
        small, offset = [], 0
        for vector in vectors:
            small.append(total[offset : offset + vector.shape[0]])
            offset += vector.shape[0]
        return (
            outputs.reshape(rows, seg, width),
            input_grad.reshape(rows, seg, width),
            small[0],
            small[1],
            query_weight_grad,
            small[2],
            keyval_weight_grad,
            small[3],
            output_weight_grad,
            small[4],
            small[5],
            small[6],
            up_weight_grad,
            small[7],
            down_weight_grad,
            small[8],
        )

    return per_device


def solution(mesh):
    placed = (
        P("dp", "sp", None),
        P("dp"),
        P(),
        P(),
        P(None, "tp"),
        P("tp"),
        P(),
        P(),
        P("tp", None),
        P(),
        P(),
        P(),
        P(None, "tp"),
        P("tp"),
        P("tp", None),
        P(),
        P("dp", "sp", None),
    )
    return jax.shard_map(
        build(mesh),
        mesh=mesh,
        in_specs=placed,
        out_specs=(
            P("dp", "sp", None),
            P("dp", "sp", None),
            P(),
            P(),
            P(("dp", "sp"), "tp"),
            P("tp"),
            P(("dp", "sp"), None),
            P(),
            P("tp", ("dp", "sp")),
            P(),
            P(),
            P(),
            P(("dp", "sp"), "tp"),
            P("tp"),
            P("tp", ("dp", "sp")),
            P(),
        ),
        check_vma=False,
    )
```

```python
import functools
import math

import jax
import jax.numpy as jnp
from jax import lax
from jax.experimental import pallas as pl
from jax.experimental.pallas import tpu as pltpu
from jax.sharding import PartitionSpec as P

HD = 128
EPS = 1e-05
BF = jnp.bfloat16
F32 = jnp.float32
SCALE = 1.0 / math.sqrt(HD)
SCALE2 = SCALE * math.log2(math.e)
VMEM = 60 * 2**20
GELU_A = math.sqrt(2.0 / math.pi)
GELU_B = 0.044715


def nn(left, right):
    return jnp.dot(left, right, preferred_element_type=F32)


def nt(left, right):
    return lax.dot_general(left, right, (((1,), (1,)), ((), ())), preferred_element_type=F32)


def tn(left, right):
    return lax.dot_general(left, right, (((0,), (0,)), ((), ())), preferred_element_type=F32)


def params():
    return pltpu.CompilerParams(vmem_limit_bytes=VMEM)


def cost(macs, moved, weight=10):
    return pl.CostEstimate(flops=int(2 * macs * weight), bytes_accessed=int(moved * weight), transcendentals=0)


def whole(*shape):
    return pl.BlockSpec(shape, lambda *_: (0,) * len(shape))


def chunk_mask(first, length, chunk, size, seg, wide):
    key_pos = chunk * size + lax.broadcasted_iota(jnp.int32, (size, wide), 0)
    query_pos = first + lax.rem(lax.broadcasted_iota(jnp.int32, (size, wide), 1), seg)
    return (key_pos <= query_pos) & (key_pos < length)


def chunk_bounds(info_ref, row, seg, size):
    first, length = info_ref[0], info_ref[3 + row]
    full = jnp.minimum(first + 1, length) // size
    total = (jnp.minimum(first + seg, length) + size - 1) // size
    return first, length, full, total


def stack_heads(ref, heads):
    return jnp.concatenate([ref[0, :, h * HD : (h + 1) * HD] for h in range(heads)], axis=0)


def unstack_heads(ref, values, heads, seg):
    for h in range(heads):
        ref[0, :, h * HD : (h + 1) * HD] = values[h * seg : (h + 1) * seg]


def forward_kernel(size, heads, seg, info_ref, q_ref, kv_ref, o_ref, lse_ref, top_s, sum_s, acc_s):
    first, length, full, total = chunk_bounds(info_ref, pl.program_id(0), seg, size)
    q = stack_heads(q_ref, heads)
    top_s[...] = jnp.full_like(top_s, -1e30)
    sum_s[...] = jnp.zeros_like(sum_s)
    acc_s[...] = jnp.zeros_like(acc_s)

    def step(masked, chunk, carry):
        at = pl.ds(pl.multiple_of((chunk ^ info_ref[1]) * size, size), size)
        scores = nt(kv_ref[info_ref[2], 0, at, :], q) * SCALE2
        if masked:
            scores = jnp.where(chunk_mask(first, length, chunk, size, seg, heads * seg), scores, -1e30)
        old = top_s[...]
        new = jnp.maximum(old, jnp.max(scores, axis=0, keepdims=True))
        weights = jnp.exp2(scores - new)
        shrink = jnp.exp2(old - new)
        sum_s[...] = sum_s[...] * shrink + jnp.sum(weights, axis=0, keepdims=True)
        acc_s[...] = acc_s[...] * shrink + tn(kv_ref[1 - info_ref[2], 0, at, :], weights.astype(BF))
        top_s[...] = new
        return carry

    lax.fori_loop(0, full, functools.partial(step, False), 0)
    lax.fori_loop(full, total, functools.partial(step, True), 0)
    unstack_heads(o_ref, (acc_s[...] * (1.0 / sum_s[...])).T.astype(BF), heads, seg)
    lse_ref[0, 0] = top_s[...] + jnp.log2(sum_s[...])


def attend_forward(info, query, keyval, size, heads):
    rows, seg, width = query.shape
    length = keyval.shape[2]
    groups, wide = width // (HD * heads), heads * seg
    head_spec = pl.BlockSpec((1, seg, heads * HD), lambda r, h, info: (r, 0, h))
    return pl.pallas_call(
        functools.partial(forward_kernel, size, heads, seg),
        grid_spec=pltpu.PrefetchScalarGridSpec(
            num_scalar_prefetch=1,
            grid=(rows, groups),
            in_specs=[head_spec, pl.BlockSpec((2, 1, length, HD), lambda r, h, info: (0, r, 0, 0))],
            out_specs=[head_spec, pl.BlockSpec((1, 1, 1, wide), lambda r, h, info: (r, h, 0, 0))],
            scratch_shapes=[pltpu.VMEM((1, wide), F32), pltpu.VMEM((1, wide), F32), pltpu.VMEM((HD, wide), F32)],
        ),
        out_shape=[
            jax.ShapeDtypeStruct((rows, seg, width), BF),
            jax.ShapeDtypeStruct((rows, groups, 1, wide), F32),
        ],
        compiler_params=params(),
        cost_estimate=cost(8 * 10**9, 4 * 2**20),
        name="attend_forward",
    )(info, query, keyval)


def backward_kernel(
    size, heads, seg, info_ref, q_ref, do_ref, o_ref, lse_ref, kv_ref, dq_ref, bias_ref, dk_ref, dv_ref, dqt_s
):
    row, group = pl.program_id(0), pl.program_id(1)
    first, length, full, total = chunk_bounds(info_ref, row, seg, size)

    @pl.when(group == 0)
    def _():
        dk_ref[...] = jnp.zeros_like(dk_ref)
        dv_ref[...] = jnp.zeros_like(dv_ref)

    q, dout, out = (stack_heads(ref, heads) for ref in (q_ref, do_ref, o_ref))
    delta = jnp.sum((dout.astype(F32) * out.astype(F32)).T, axis=0, keepdims=True)
    lse = lse_ref[0, 0]
    dqt_s[...] = jnp.zeros_like(dqt_s)

    def step(masked, chunk, carry):
        at = pl.ds(pl.multiple_of((chunk ^ info_ref[1]) * size, size), size)
        keys = kv_ref[info_ref[2], 0, at, :]
        prob = jnp.exp2(nt(keys, q) * SCALE2 - lse)
        if masked:
            prob = jnp.where(chunk_mask(first, length, chunk, size, seg, heads * seg), prob, 0.0)
        dprob = nt(kv_ref[1 - info_ref[2], 0, at, :], dout)
        dscore = (prob * (dprob - delta)).astype(BF)
        dv_ref[0, at, :] += nn(prob.astype(BF), dout)
        dk_ref[0, at, :] += nn(dscore, q) * SCALE
        dqt_s[...] += tn(keys, dscore)
        return carry

    lax.fori_loop(0, full, functools.partial(step, False), 0)
    lax.fori_loop(full, total, functools.partial(step, True), 0)
    dq = (dqt_s[...] * SCALE).T.astype(BF)
    unstack_heads(dq_ref, dq, heads, seg)
    for h in range(heads):
        bias_ref[0, :, h * HD : (h + 1) * HD] = jnp.sum(
            dq[h * seg : (h + 1) * seg].astype(F32), axis=0, keepdims=True
        )


def attend_backward(info, query, dout, out, lse, keyval, size, heads):
    rows, seg, width = query.shape
    length = keyval.shape[2]
    groups, wide = width // (HD * heads), heads * seg
    head_spec = pl.BlockSpec((1, seg, heads * HD), lambda r, h, info: (r, 0, h))
    key_spec = pl.BlockSpec((1, length, HD), lambda r, h, info: (r, 0, 0))
    return pl.pallas_call(
        functools.partial(backward_kernel, size, heads, seg),
        grid_spec=pltpu.PrefetchScalarGridSpec(
            num_scalar_prefetch=1,
            grid=(rows, groups),
            in_specs=[
                head_spec,
                head_spec,
                head_spec,
                pl.BlockSpec((1, 1, 1, wide), lambda r, h, info: (r, h, 0, 0)),
                pl.BlockSpec((2, 1, length, HD), lambda r, h, info: (0, r, 0, 0)),
            ],
            out_specs=[head_spec, pl.BlockSpec((1, 1, heads * HD), lambda r, h, info: (r, 0, h)), key_spec, key_spec],
            scratch_shapes=[pltpu.VMEM((HD, wide), F32)],
        ),
        out_shape=[
            jax.ShapeDtypeStruct((rows, seg, width), BF),
            jax.ShapeDtypeStruct((rows, 1, width), F32),
            jax.ShapeDtypeStruct((rows, length, HD), F32),
            jax.ShapeDtypeStruct((rows, length, HD), F32),
        ],
        compiler_params=params(),
        cost_estimate=cost(12 * 10**9, 8 * 2**20),
        name="attend_backward",
    )(info, query, dout, out, lse, keyval)


def gelu_parts(v):
    square = v * v
    t = jnp.tanh(GELU_A * v * (1.0 + GELU_B * square))
    half = 0.5 * (1.0 + t)
    slope = half + 0.5 * v * (1.0 - t * t) * (GELU_A * (1.0 + 3.0 * GELU_B * square))
    return v * half, slope


def local_kernel(parts, u_ref, dm_ref, *refs):
    piece_refs, refs = refs[:parts], refs[parts:]
    up_ref, down_ref, bias_ref, hidden_ref, du_ref, dbias_ref, u_all_ref, dm_rest_ref, du_s, u_s, send, recv, local = refs
    step, last = pl.program_id(0), pl.num_programs(0) - 1
    dp, sp, tp = lax.axis_index("dp"), lax.axis_index("sp"), lax.axis_index("tp")
    half = u_ref.shape[0] // 2
    quarter = half // 2
    over_x, over_y, sibling = (dp, sp ^ 1, tp), (dp, sp ^ 2, tp), (dp, sp, 1 - tp)

    def remote(k, source, target, device):
        return pltpu.make_async_remote_copy(
            source, target, send.at[k], recv.at[k], device_id=device, device_id_type=pl.DeviceIdType.MESH
        )

    own = u_s.at[pl.ds(pl.multiple_of(tp * half, half), half), :]
    other = u_s.at[pl.ds(pl.multiple_of((1 - tp) * half, half), half), :]
    top, bottom = pl.ds(0, quarter), pl.ds(quarter, quarter)
    to_x = remote(0, own, u_all_ref.at[1], over_x)
    to_y = remote(1, own, u_all_ref.at[2], over_y)
    pass_y = remote(2, u_all_ref.at[1, top], u_all_ref.at[3, top], over_y)
    pass_x = remote(3, u_all_ref.at[2, bottom], u_all_ref.at[3, bottom], over_x)
    shares = [remote(3 + k, u_all_ref.at[k], u_all_ref.at[3 + k], sibling) for k in (1, 2, 3)]
    dm_shares = [remote(7 + k, piece, dm_rest_ref.at[k], sibling) for k, piece in enumerate(piece_refs)]
    keep_own = pltpu.make_async_copy(own, u_all_ref.at[0], local.at[0])
    keep_other = pltpu.make_async_copy(other, u_all_ref.at[7], local.at[1])

    @pl.when(step == 0)
    def _():
        barrier = pltpu.get_barrier_semaphore()
        for device in (over_x, over_y, sibling):
            pl.semaphore_signal(barrier, inc=1, device_id=device, device_id_type=pl.DeviceIdType.MESH)
        pl.semaphore_wait(barrier, 3)
        u_s[...] = u_ref[...]
        to_x.start()
        to_y.start()
        for copy in dm_shares:
            copy.start()
        keep_own.start()
        keep_other.start()
        du_s[...] = jnp.zeros_like(du_s)

    @pl.when(step == (last + 1) * 5 // 8)
    def _():
        to_x.wait_recv()
        to_y.wait_recv()
        pass_y.start()
        pass_x.start()
        shares[0].start()
        shares[1].start()

    hidden, slope = gelu_parts(nn(u_ref[...], up_ref[...]) + bias_ref[...])
    hidden_ref[...] = hidden.astype(BF)
    dpre = (nt(dm_ref[...], down_ref[...]) * slope).astype(BF)
    dbias_ref[...] = jnp.sum(dpre.astype(F32), axis=0, keepdims=True)
    du_s[...] += nt(dpre, up_ref[...])

    @pl.when(step == last)
    def _():
        pass_y.wait_recv()
        pass_x.wait_recv()
        shares[2].start()
        du_ref[...] = du_s[...].astype(BF)
        for copy in (to_x, to_y, pass_y, pass_x):
            copy.wait_send()
        for copy in (*shares, *dm_shares):
            copy.wait()
        keep_own.wait()
        keep_other.wait()


def feed_local(u, dmlp, pieces, up, down, bias, tile):
    tokens, width = u.shape
    units = up.shape[1]
    block = whole(tokens, width)
    anywhere = pl.BlockSpec(memory_space=pl.ANY)
    return pl.pallas_call(
        functools.partial(local_kernel, len(pieces)),
        grid=(units // tile,),
        in_specs=[
            block,
            block,
            *[anywhere] * len(pieces),
            pl.BlockSpec((width, tile), lambda i: (0, i)),
            pl.BlockSpec((tile, width), lambda i: (i, 0)),
            pl.BlockSpec((1, tile), lambda i: (0, i)),
        ],
        out_specs=[
            pl.BlockSpec((tokens, tile), lambda i: (0, i)),
            block,
            pl.BlockSpec((1, tile), lambda i: (0, i)),
            anywhere,
            anywhere,
        ],
        out_shape=[
            jax.ShapeDtypeStruct((tokens, units), BF),
            jax.ShapeDtypeStruct((tokens, width), BF),
            jax.ShapeDtypeStruct((1, units), F32),
            jax.ShapeDtypeStruct((8, tokens // 2, width), BF),
            jax.ShapeDtypeStruct((len(pieces), *pieces[0].shape), BF),
        ],
        scratch_shapes=[
            pltpu.VMEM((tokens, width), F32),
            pltpu.VMEM((tokens, width), BF),
            pltpu.SemaphoreType.DMA((7 + len(pieces),)),
            pltpu.SemaphoreType.DMA((7 + len(pieces),)),
            pltpu.SemaphoreType.DMA((2,)),
        ],
        compiler_params=pltpu.CompilerParams(vmem_limit_bytes=VMEM, collective_id=0, has_side_effects=True),
        cost_estimate=cost(3 * tokens * width * units, 4 * width * units),
        name="feed_local",
    )(u, dmlp, *pieces, up, down, bias)


def mlp_kernel(hidden_ref, down_ref, out_ref, total_s):
    @pl.when(pl.program_id(0) == 0)
    def _():
        total_s[...] = jnp.zeros_like(total_s)

    total_s[...] += nn(hidden_ref[...], down_ref[...])

    @pl.when(pl.program_id(0) == pl.num_programs(0) - 1)
    def _():
        out_ref[...] = total_s[...].astype(BF)


def feed_out(hidden, down, tile):
    tokens, units = hidden.shape
    width = down.shape[1]
    return pl.pallas_call(
        mlp_kernel,
        grid=(units // tile,),
        in_specs=[pl.BlockSpec((tokens, tile), lambda i: (0, i)), pl.BlockSpec((tile, width), lambda i: (i, 0))],
        out_specs=whole(tokens, width),
        out_shape=jax.ShapeDtypeStruct((tokens, width), BF),
        scratch_shapes=[pltpu.VMEM((tokens, width), F32)],
        compiler_params=params(),
        cost_estimate=cost(tokens * width * units, 2 * width * units, 10),
        name="feed_out",
    )(hidden, down)


def grad_kernel(u_parts, parts, at_ref, *refs):
    pieces, (up_ref, down_ref, bias_ref, out_ref, u_s, dm_s, sems) = refs[:parts], refs[parts:]

    def copies(target):
        offset = 0
        for k in range(u_parts) if target is u_s else range(u_parts, parts):
            piece = pieces[k]
            yield pltpu.make_async_copy(piece, target.at[pl.ds(offset, piece.shape[0]), :], sems.at[k])
            offset += piece.shape[0]

    @pl.when(pl.program_id(0) == 0)
    def _():
        for copy in copies(u_s):
            copy.start()
        for copy in copies(dm_s):
            copy.start()
        for copy in copies(u_s):
            copy.wait()
        for copy in copies(dm_s):
            copy.wait()

    tile = up_ref.shape[1]
    hidden, slope = gelu_parts(nn(u_s[...], up_ref[...]) + bias_ref[...])
    dpre = (nt(dm_s[...], down_ref[...]) * slope).astype(BF)
    out_ref[:, :tile] = tn(dpre, u_s[...]).T.astype(BF)
    out_ref[:, tile:] = tn(hidden.astype(BF), dm_s[...]).T.astype(BF)


def feed_grads(at, u, dmlp, up, down, bias, tile, count):
    width = up.shape[0]
    tokens = sum(part.shape[0] for part in u)
    return pl.pallas_call(
        functools.partial(grad_kernel, len(u), len(u) + len(dmlp)),
        grid_spec=pltpu.PrefetchScalarGridSpec(
            num_scalar_prefetch=1,
            grid=(count,),
            in_specs=[
                *[pl.BlockSpec(memory_space=pl.ANY)] * (len(u) + len(dmlp)),
                pl.BlockSpec((width, tile), lambda i, at: (0, at[0] + i)),
                pl.BlockSpec((tile, width), lambda i, at: (at[0] + i, 0)),
                pl.BlockSpec((1, tile), lambda i, at: (0, at[0] + i)),
            ],
            out_specs=pl.BlockSpec((width, 2 * tile), lambda i, at: (0, i)),
            scratch_shapes=[
                pltpu.VMEM((tokens, width), BF),
                pltpu.VMEM((tokens, width), BF),
                pltpu.SemaphoreType.DMA((len(u) + len(dmlp),)),
            ],
        ),
        out_shape=jax.ShapeDtypeStruct((width, 2 * tile * count), BF),
        compiler_params=params(),
        cost_estimate=cost(4 * tokens * width * tile * count, 4 * width * (tokens + 2 * tile * count)),
        name="feed_grads",
    )(at, *u, *dmlp, up, down, bias)


def normalize(values):
    average = jnp.mean(values, axis=-1, keepdims=True)
    centered = values - average
    variance = jnp.mean(centered * centered, axis=-1, keepdims=True)
    inv_std = lax.rsqrt(variance + EPS)
    return centered * inv_std, inv_std


def norm_back(gradient, scaled, inv_std, norm_gain):
    inner = gradient * norm_gain
    mean_one = jnp.mean(inner, axis=-1, keepdims=True)
    mean_two = jnp.mean(inner * scaled, axis=-1, keepdims=True)
    return inv_std * (inner - mean_one - scaled * mean_two)


def column_sum(values):
    return jnp.sum(values, axis=0, keepdims=True)


def by_rows(body, tokens, tile, ins, outs, name, sums=0, weight=1):
    row = lambda columns: pl.BlockSpec((tile, columns), lambda i: (i, 0))
    specs = [row(a.shape[1]) if cut else whole(*a.shape) for a, cut in ins]
    shapes = [jax.ShapeDtypeStruct((tokens, columns), dtype) for columns, dtype in outs]
    out_specs = [row(columns) for columns, _ in outs]
    if sums:
        shapes.append(jax.ShapeDtypeStruct((sums, outs[0][0]), F32))
        out_specs.append(whole(sums, outs[0][0]))
    moved = sum(a.size * a.dtype.itemsize for a, _ in ins) + sum(s.size * s.dtype.itemsize for s in shapes)
    return pl.pallas_call(
        body,
        grid=(tokens // tile,),
        in_specs=specs,
        out_specs=out_specs,
        out_shape=shapes,
        compiler_params=params(),
        cost_estimate=cost(moved * 200, moved, weight),
        name=name,
    )(*[a for a, _ in ins])


def first_kernel(x_ref, gain_ref, bias_ref, w_ref, wb_ref, v_ref, kv_ref):
    hat, _ = normalize(x_ref[...].astype(F32))
    v = (hat * gain_ref[...] + bias_ref[...]).astype(BF)
    v_ref[...] = v
    kv_ref[...] = (nn(v, w_ref[...]) + wb_ref[...]).astype(BF)


def exchange_rows(part, finish, tokens, tile, firsts, ins, outs, name, collective_id, sums=0):
    count = tokens // tile
    now, late = lambda i: (jnp.minimum(i, count - 1), 0), lambda i: (jnp.maximum(i - 1, 0), 0)
    spec = lambda a, cut, at: pl.BlockSpec((tile, a.shape[1]), at) if cut else whole(*a.shape)
    width = outs[0][0]

    def kernel(*refs):
        first_refs, refs = refs[: len(firsts)], refs[len(firsts) :]
        in_refs, refs = refs[: len(ins)], refs[len(ins) :]
        out_refs, (own_s, far_s, send, recv) = refs[:-4], refs[-4:]
        step = pl.program_id(0)
        sibling = (lax.axis_index("dp"), lax.axis_index("sp"), 1 - lax.axis_index("tp"))

        def copy(k):
            return pltpu.make_async_remote_copy(
                own_s.at[k], far_s.at[k], send.at[k], recv.at[k],
                device_id=sibling, device_id_type=pl.DeviceIdType.MESH,
            )

        @pl.when(step == 0)
        def _():
            barrier = pltpu.get_barrier_semaphore()
            pl.semaphore_signal(barrier, inc=1, device_id=sibling, device_id_type=pl.DeviceIdType.MESH)
            pl.semaphore_wait(barrier, 1)
            if sums:
                out_refs[-1][...] = jnp.zeros_like(out_refs[-1])

        @pl.when(step < count)
        def _():
            own_s[step] = part(*first_refs).astype(BF)
            copy(step).start()

        @pl.when(step > 0)
        def _():
            copy(step - 1).wait_recv()
            finish(own_s[step - 1].astype(F32) + far_s[step - 1].astype(F32), in_refs, out_refs)

        @pl.when(step == count)
        def _():
            for k in range(count):
                copy(k).wait_send()

    shapes = [jax.ShapeDtypeStruct((tokens, columns), dtype) for columns, dtype in outs]
    out_specs = [pl.BlockSpec((tile, columns), late) for columns, _ in outs]
    if sums:
        shapes.append(jax.ShapeDtypeStruct((sums, width), F32))
        out_specs.append(whole(sums, width))
    moved = sum(a.size * a.dtype.itemsize for a, _ in (*firsts, *ins))
    return pl.pallas_call(
        kernel,
        grid=(count + 1,),
        in_specs=[spec(a, cut, now) for a, cut in firsts] + [spec(a, cut, late) for a, cut in ins],
        out_specs=out_specs,
        out_shape=shapes,
        scratch_shapes=[
            pltpu.VMEM((count, tile, width), BF),
            pltpu.VMEM((count, tile, width), BF),
            pltpu.SemaphoreType.DMA((count,)),
            pltpu.SemaphoreType.DMA((count,)),
        ],
        compiler_params=pltpu.CompilerParams(vmem_limit_bytes=VMEM, collective_id=collective_id, has_side_effects=True),
        cost_estimate=cost(moved * 200, moved, 1),
        name=name,
    )(*[a for a, _ in firsts], *[a for a, _ in ins])


def proj_part(attended_ref, w_ref):
    return nn(attended_ref[...], w_ref[...])


def second_finish(proj, ins, outs):
    x_ref, ob_ref, gain_ref, bias_ref = ins
    resid_ref, u_ref = outs
    resid = x_ref[...].astype(F32) + proj + ob_ref[...]
    resid_ref[...] = resid
    hat, _ = normalize(resid)
    u_ref[...] = (hat * gain_ref[...] + bias_ref[...]).astype(BF)


def dv_part(dq_ref, w_ref):
    return nt(dq_ref[...], w_ref[...])


def first_finish(dv, ins, outs):
    dkv_ref, w_ref, x_ref, dres_ref, gain_ref = ins
    grad_ref, sums_ref = outs
    dv = dv + nt(dkv_ref[...], w_ref[...])
    hat, inv_std = normalize(x_ref[...].astype(F32))
    grad_ref[...] = (dres_ref[...] + norm_back(dv, hat, inv_std, gain_ref[...])).astype(BF)
    sums_ref[...] += jnp.concatenate([column_sum(dv * hat), column_sum(dv)], axis=0)


def second_back_kernel(own_ref, far_ref, resid_ref, dm_ref, gain_ref, dres_ref, dproj_ref, sums_ref):
    @pl.when(pl.program_id(0) == 0)
    def _():
        sums_ref[...] = jnp.zeros_like(sums_ref)

    du = own_ref[...].astype(F32) + far_ref[...].astype(F32)
    hat, inv_std = normalize(resid_ref[...])
    dout = dm_ref[...].astype(F32)
    dres = dout + norm_back(du, hat, inv_std, gain_ref[...])
    dres_ref[...] = dres
    dproj_ref[...] = dres.astype(BF)
    sums_ref[...] += jnp.concatenate(
        [column_sum(du * hat), column_sum(du), column_sum(dres), column_sum(dout)], axis=0
    )


def output_kernel(resid_ref, own_ref, far_ref, bias_ref, out_ref):
    mlp = own_ref[...].astype(F32) + far_ref[...].astype(F32)
    out_ref[...] = (resid_ref[...] + mlp + bias_ref[...]).astype(BF)


def project(left, right, transposed, tile, name, bias=None):
    tokens, depth = left.shape
    columns = right.shape[0] if transposed else right.shape[1]

    def body(*refs):
        product = (nt if transposed else nn)(refs[0][...], refs[1][...])
        if bias is not None:
            product = product + refs[2][...]
        refs[-1][...] = product.astype(BF)

    spec = pl.BlockSpec((tile, depth), lambda i: (i, 0)) if transposed else pl.BlockSpec((depth, tile), lambda i: (0, i))
    extra = [] if bias is None else [bias.reshape(1, columns)]
    return pl.pallas_call(
        body,
        grid=(columns // tile,),
        in_specs=[whole(tokens, depth), spec] + [pl.BlockSpec((1, tile), lambda i: (0, i))] * len(extra),
        out_specs=pl.BlockSpec((tokens, tile), lambda i: (0, i)),
        out_shape=jax.ShapeDtypeStruct((tokens, columns), BF),
        compiler_params=params(),
        cost_estimate=cost(tokens * depth * columns, 2 * (tokens * (depth + columns) + depth * columns)),
        name=name,
    )(left, right, *extra)


def rows_kernel(groups, shard, count, spot_ref, left_ref, *refs):
    rights, (keep_ref, x_ref, y_ref) = refs[:count], refs[count:]
    step = pl.program_id(0)
    dest = spot_ref[0] ^ step
    cols = [left_ref[:, pl.ds(pl.multiple_of((g * 4 + dest) * shard, shard), shard)] for g in range(groups)]
    left = jnp.concatenate(cols, axis=1)
    product = jnp.concatenate([tn(left, right[...]).astype(BF) for right in rights], axis=1)
    half = product.shape[0] // 2
    low, high = product[:half], product[half:]

    @pl.when(step == 0)
    def _():
        keep_ref[0], keep_ref[1] = low, high

    @pl.when(step == 1)
    def _():
        x_ref[0], keep_ref[3] = low, high

    @pl.when(step == 2)
    def _():
        keep_ref[2], y_ref[0] = low, high

    @pl.when(step == 3)
    def _():
        x_ref[1], y_ref[1] = low, high


def rows_grad(spot, left, rights, groups, shard):
    tokens, width = left.shape
    columns = sum(right.shape[1] for right in rights)
    half = groups * shard // 2
    return pl.pallas_call(
        functools.partial(rows_kernel, groups, shard, len(rights)),
        grid_spec=pltpu.PrefetchScalarGridSpec(
            num_scalar_prefetch=1,
            grid=(4,),
            in_specs=[whole(tokens, width), *[whole(*right.shape) for right in rights]],
            out_specs=[whole(4, half, columns), whole(2, half, columns), whole(2, half, columns)],
        ),
        out_shape=[jax.ShapeDtypeStruct((n, half, columns), BF) for n in (4, 2, 2)],
        compiler_params=params(),
        cost_estimate=cost(tokens * width * columns, 2 * (tokens + columns) * width, 1),
        name="rows_grad",
    )(spot, left, *rights)


def direct_kernel(groups, shard, spot_ref, left_ref, right_ref, *out_refs):
    for bit in range(4):
        dest = spot_ref[0] ^ bit
        cols = [left_ref[:, pl.ds(pl.multiple_of((g * 4 + dest) * shard, shard), shard)] for g in range(groups)]
        out_refs[bit][...] = tn(jnp.concatenate(cols, axis=1), right_ref[...]).astype(BF)


def rows_direct(spot, left, right, groups, shard):
    shape = (groups * shard, right.shape[1])
    return pl.pallas_call(
        functools.partial(direct_kernel, groups, shard),
        grid_spec=pltpu.PrefetchScalarGridSpec(
            num_scalar_prefetch=1,
            grid=(1,),
            in_specs=[whole(*left.shape), whole(*right.shape)],
            out_specs=[whole(*shape)] * 4,
        ),
        out_shape=[jax.ShapeDtypeStruct(shape, BF)] * 4,
        compiler_params=params(),
        cost_estimate=cost(left.size * right.shape[1], 2 * left.size, 1),
        name="rows_direct",
    )(spot, left, right)


def add_kernel(keep_ref, x_ref, y_ref, low_ref, high_ref):
    low_ref[...] = (keep_ref[2].astype(F32) + x_ref[1].astype(F32)).astype(BF)
    high_ref[...] = (keep_ref[3].astype(F32) + y_ref[1].astype(F32)).astype(BF)


def add_passed(keep, from_x, from_y):
    shape = keep.shape[1:]
    return pl.pallas_call(
        add_kernel,
        in_specs=[whole(*keep.shape), whole(*from_x.shape), whole(*from_y.shape)],
        out_specs=[whole(*shape), whole(*shape)],
        out_shape=[jax.ShapeDtypeStruct(shape, BF)] * 2,
        grid=(1,),
        compiler_params=params(),
        cost_estimate=cost(0, 8 * shape[0] * shape[1] * 2, 1),
        name="add_passed",
    )(keep, from_x, from_y)


def total_kernel(ready, *refs):
    out_ref, offset = refs[-1], 0
    for k in range(ready):
        columns = refs[k].shape[1]
        out_ref[:, offset : offset + columns] = refs[k][...]
        offset += columns
    keep_ref, x_ref, y_ref, low_ref, high_ref = refs[ready : ready + 5]
    half, columns = low_ref.shape
    at = slice(offset, offset + columns)
    out_ref[:half, at] = (keep_ref[0].astype(F32) + x_ref[0].astype(F32) + low_ref[...].astype(F32)).astype(BF)
    out_ref[half:, at] = (keep_ref[1].astype(F32) + y_ref[0].astype(F32) + high_ref[...].astype(F32)).astype(BF)
    rest = refs[ready + 5 : -1]
    if rest:
        out_ref[:, offset + columns :] = sum(ref[...].astype(F32) for ref in rest).astype(BF)


def add_total(ready, quads):
    arrays = [*ready, *[array for quad in quads for array in quad]]
    lead = 2 * quads[0][3].shape[0]
    columns = sum(a.shape[1] for a in ready) + sum(quad[3].shape[1] for quad in quads)
    return pl.pallas_call(
        functools.partial(total_kernel, len(ready)),
        in_specs=[whole(*a.shape) for a in arrays],
        out_specs=whole(lead, columns),
        out_shape=jax.ShapeDtypeStruct((lead, columns), BF),
        grid=(1,),
        compiler_params=params(),
        cost_estimate=cost(0, 8 * lead * columns, 1),
        name="add_total",
    )(*arrays)


def finish_kernel(output_ref, both_ref, out_ref, query_ref, kv_ref):
    columns = query_ref.shape[1]
    out_ref[...] = output_ref[...].astype(F32).T
    query_ref[...] = both_ref[:, :columns].astype(F32)
    kv_ref[...] = both_ref[:, columns:].astype(F32)


def finish(output, both, columns):
    shard, total = both.shape
    shapes = [(output.shape[1], shard), (shard, columns), (shard, total - columns)]
    return pl.pallas_call(
        finish_kernel,
        in_specs=[whole(*output.shape), whole(shard, total)],
        out_specs=[whole(*shape) for shape in shapes],
        out_shape=[jax.ShapeDtypeStruct(shape, F32) for shape in shapes],
        grid=(1,),
        compiler_params=params(),
        cost_estimate=cost(0, 6 * shard * total, 1),
        name="finish",
    )(output, both)


def pack_kernel(*refs):
    *in_refs, kv_ref, out_ref = refs
    offset = 0
    for ref in in_refs:
        for k in range(ref.shape[0]):
            out_ref[:, offset : offset + ref.shape[1]] = ref[k : k + 1]
            offset += ref.shape[1]
    out_ref[:, offset:] = column_sum(kv_ref[:, HD:].astype(F32))


def pack(arrays, dkeyval):
    size = sum(a.size for a in arrays) + HD
    return pl.pallas_call(
        pack_kernel,
        in_specs=[whole(*a.shape) for a in (*arrays, dkeyval)],
        out_specs=whole(1, size),
        out_shape=jax.ShapeDtypeStruct((1, size), F32),
        grid=(1,),
        compiler_params=params(),
        cost_estimate=cost(0, 8 * size, 1),
        name="pack",
    )(*arrays, dkeyval)


def place_kernel(tile, counts, spot_ref, *refs):
    shares, (up_ref, down_ref) = refs[:-2], refs[-2:]
    units = up_ref.shape[1] // 4
    for bit in range(4):
        at = (spot_ref[0] ^ bit) * units
        tile_at = 0
        for piece, count in enumerate(counts):
            for k in range(count):
                block = shares[piece * 4 + bit][:, k * 2 * tile : (k + 1) * 2 * tile].astype(F32)
                spot = pl.ds(pl.multiple_of(at + (tile_at + k) * tile, tile), tile)
                up_ref[:, spot] = block[:, :tile]
                down_ref[spot, :] = block[:, tile:].T
            tile_at += count


def place_shares(spot, shares, counts, tile, units):
    shard = shares[0].shape[0]
    return pl.pallas_call(
        functools.partial(place_kernel, tile, counts),
        grid_spec=pltpu.PrefetchScalarGridSpec(
            num_scalar_prefetch=1,
            grid=(1,),
            in_specs=[whole(*share.shape) for share in shares],
            out_specs=[whole(shard, units), whole(units, shard)],
        ),
        out_shape=[jax.ShapeDtypeStruct((shard, units), F32), jax.ShapeDtypeStruct((units, shard), F32)],
        compiler_params=params(),
        cost_estimate=cost(0, 12 * shard * units, 1),
        name="place_shares",
    )(spot, *shares)


def build(mesh):
    sp_size, dp_size = mesh.shape["sp"], mesh.shape["dp"]
    quads = sp_size // 4

    def swap(value, bit, keep=None):
        pairs = [(i, i ^ bit) for i in range(sp_size)]
        return lax.ppermute(value, "sp", pairs if keep is None else [p for p in pairs if keep(*p)])

    def swap_dp(value, bit):
        return lax.ppermute(value, "dp", [(i, i ^ bit) for i in range(dp_size)])

    def swap_tp(value):
        return lax.ppermute(value, "tp", [(0, 1), (1, 0)])

    def sum_all(vector, fill):
        for exchange, size in ((swap, sp_size), (swap_dp, dp_size)):
            bit = 1
            while bit < size:
                if bit * 2 < size:
                    near, far, both = (exchange(vector, k) for k in (bit, 2 * bit, 3 * bit))
                    if exchange is swap_dp:
                        (near, far, both), fill = lax.optimization_barrier(((near, far, both), fill))
                    vector = (vector + near) + (far + both)
                else:
                    vector = vector + exchange(vector, bit)
                bit *= 4
        return vector, fill

    def half_of(own, core):
        half = own.shape[0] // 2
        return lax.dynamic_slice_in_dim(own, core * half, half, 0)

    def scatter_rest(value, after=None):
        if after is not None:
            value, _ = lax.optimization_barrier((value, after))
        value = lax.psum_scatter(value, "dp", scatter_dimension=0, tiled=True)
        if quads > 1:
            groups = [[q * 4 + r for q in range(quads)] for r in range(4)]
            value = lax.psum_scatter(value, "sp", scatter_dimension=0, tiled=True, axis_index_groups=groups)
        return value

    def start_quad(spot, left, rights, shard, after=()):
        groups = dp_size * quads
        if shard % 128 == 0:
            keep, to_x, to_y = rows_grad(spot.reshape(1), left, rights, groups, shard)
            to_x, to_y, _ = lax.optimization_barrier((to_x, to_y, after))
            return [keep, swap(to_x, 1), swap(to_y, 2)]
        value = jnp.concatenate([tn(left, right).astype(BF) for right in rights], axis=1)
        value = value.reshape(groups, 4, shard, -1)
        blocks = [
            lax.dynamic_index_in_dim(value, spot ^ bit, 1, keepdims=False).reshape(groups * shard, -1)
            for bit in range(4)
        ]
        return [blocks[0], *[swap(blocks[bit], bit) for bit in range(1, 4)]]

    def direct_quad(spot, left, right, shard):
        if shard % 128 == 0:
            blocks = rows_direct(spot.reshape(1), left, right, dp_size * quads, shard)
            return [blocks[0], *[swap(blocks[bit], bit) for bit in range(1, 4)]]
        return start_quad(spot, left, [right], shard)

    def middle_quad(parts):
        if len(parts) == 4:
            return parts, parts[0]
        low, high = add_passed(*parts)
        return [*parts, swap(low, 2), swap(high, 1)], low

    def end_quads(ready, quads):
        if len(quads[0]) == 5:
            return add_total(ready, quads)
        return jnp.concatenate([*ready, *[sum(p.astype(F32) for p in quad).astype(BF) for quad in quads]], axis=1)

    def per_device(
        inputs, lengths, first_gain, first_bias, query_weight, query_bias, keyval_weight, value_bias, output_weight,
        output_bias, second_gain, second_bias, up_weight, up_bias, down_weight, down_bias, cotangent,
    ):
        rows, seg, width = inputs.shape
        tokens = rows * seg
        place, core = lax.axis_index("sp").astype(jnp.int32), lax.axis_index("tp")
        spot = lax.rem(place, 4)
        row_len = seg * sp_size
        one_quad = quads == 1
        shard = width // (dp_size * sp_size)
        even = core == 0
        info = jnp.concatenate([jnp.stack([place * seg, spot if one_quad else 0 * spot, core.astype(jnp.int32)]), lengths])
        row = lambda vector: vector.reshape(1, -1)

        x = inputs.reshape(tokens, width)
        dmlp = cotangent.reshape(tokens, width)
        tile = min(tokens, 128)
        piece = lambda at: lax.dynamic_slice_in_dim(dmlp, at * (tokens // 4), tokens // 4, 0)
        x, dmlp_top, dmlp_bottom = lax.optimization_barrier((x, piece(2 * core), piece(2 * core + 1)))
        half_weight = lax.dynamic_slice_in_dim(keyval_weight, core * HD, HD, 1)
        half_bias = row(jnp.where(even, 0.0, value_bias))
        v_first, kv_half = by_rows(
            first_kernel, tokens, tile,
            [(x, True), (row(first_gain), False), (row(first_bias), False), (half_weight, False), (half_bias, False)],
            [(width, BF), (HD, BF)], "first_norm",
        )
        top_x, bottom_y = swap(dmlp_top, 1), swap(dmlp_bottom, 2)
        v_late, top_x, bottom_y = lax.optimization_barrier((v_first, top_x, bottom_y))
        query = project(v_late, query_weight, False, 512, "query", query_bias).reshape(rows, seg, -1)
        if one_quad:
            pieces = [kv_half, *[swap(kv_half, bit, lambda a, b: a < b) for bit in (1, 2, 3)]]
            pieces, query = lax.optimization_barrier((pieces, query))
            kv_mine = jnp.concatenate(pieces, axis=0).reshape(1, row_len, HD)
            size = seg
        else:
            kv_mine = lax.all_gather(kv_half.reshape(rows, seg, HD), "sp", axis=1, tiled=True)
            size = min(512, row_len)
        top_x, bottom_y, top, bottom, kv_mine = lax.optimization_barrier((top_x, bottom_y, dmlp_top, dmlp_bottom, kv_mine))
        dmlp_pieces = [top_x, swap(bottom, 1), swap(top, 2), bottom_y, swap(top_x, 2), swap(bottom_y, 1)]
        keyval_all = jnp.stack([kv_mine, swap_tp(kv_mine)])

        query, keyval_all = lax.optimization_barrier((query, keyval_all))

        attended, lse = attend_forward(info, query, keyval_all, size, 4)
        attended_flat = attended.reshape(tokens, -1)
        resid, u_second = exchange_rows(
            proj_part, second_finish, tokens, tile, [(attended_flat, True), (output_weight, False)],
            [(x, True), (row(output_bias), False), (row(second_gain), False), (row(second_bias), False)],
            [(width, F32), (width, BF)], "second_norm", 1,
        )
        up_bias_row = row(up_bias)
        hidden, du, up_bias_grad, u_all, dmlp_rest = feed_local(
            u_second, dmlp, dmlp_pieces, up_weight, down_weight, up_bias_row, 512
        )
        u_all = [u_all.reshape(4 * tokens, width)]
        dmlp_all = [dmlp_top, dmlp_bottom, *dmlp_pieces, dmlp_rest.reshape(-1, width), half_of(dmlp, 1 - core)]

        units = up_weight.shape[1]
        unit_tile = 256
        tiles = units // 4 // unit_tile
        counts = (1, tiles - 1)
        feed_part = lambda at, count: feed_grads(
            at.reshape(1), u_all, dmlp_all, up_weight, down_weight, up_bias_row, unit_tile, count
        )
        shares = []

        def spread(share):
            blocks = [lax.dynamic_slice_in_dim(share, (spot ^ bit) * shard, shard, 0) for bit in range(4)]
            shares.extend([blocks[0], *[swap(blocks[bit], bit) for bit in range(1, 4)]])

        first_part = feed_part(spot * tiles, counts[0])
        first_share = scatter_rest(first_part)
        at, _ = lax.optimization_barrier((spot * tiles + counts[0], first_part))
        last_part = feed_part(at, counts[1])
        last_share = scatter_rest(last_part)

        du_far, _ = lax.optimization_barrier((swap_tp(du), last_part))
        dres, dproj, second_sums = by_rows(
            second_back_kernel, tokens, tile,
            [(du, True), (du_far, True), (resid, True), (dmlp, True), (row(second_gain), False)],
            [(width, F32), (width, BF)], "second_back", sums=4,
        )
        output_quad = start_quad(spot, dproj, [attended_flat], shard)
        dproj, output_keep = lax.optimization_barrier((dproj, output_quad[0]))
        dattended = project(dproj, output_weight, True, 512, "dattended").reshape(rows, seg, -1)
        dattended, first_share = lax.optimization_barrier((dattended, first_share))
        dquery, query_bias_grad, dkey, dvalue = attend_backward(info, query, dattended, attended, lse, keyval_all, size, 4)
        dquery = dquery.reshape(tokens, -1)
        query_bias_grad = jnp.sum(query_bias_grad[:, 0], axis=0)
        dquery, output_quad = lax.optimization_barrier((dquery, [output_keep, *output_quad[1:]]))
        output_quad, formed = middle_quad(output_quad)
        dquery, _ = lax.optimization_barrier((dquery, formed))
        if one_quad:
            dkey, dvalue = dkey[0], dvalue[0]
            far = swap_tp(jnp.where(even, dvalue, dkey).astype(BF))
            half = jnp.where(even, dkey, dvalue) + far.astype(F32)
            sends = [half[bit * tokens : (bit + 1) * tokens].astype(BF) for bit in range(1, 4)]
            query_quad = start_quad(spot, v_first, [dquery], shard, sends)
            arrived = [swap(send, bit, lambda a, b: a > b) for bit, send in enumerate(sends, 1)]
            own = half[:tokens]
            for term in arrived:
                own = own + term.astype(F32)
            own = lax.optimization_barrier(own.astype(BF))
            far = swap_tp(own)
            output_part = end_quads([], [output_quad])
            hidden, _ = lax.optimization_barrier((hidden, (own, output_part, query_quad[0])))
            mlp = feed_out(hidden, down_weight, 512)
            far, mlp = lax.optimization_barrier((far, mlp))
        else:
            query_quad = start_quad(spot, v_first, [dquery], shard)
            mlp = feed_out(hidden, down_weight, 512)
            part = lax.psum(jnp.concatenate([dkey, dvalue], axis=2).astype(BF), "tp")
            both = lax.psum_scatter(part, "sp", scatter_dimension=1, tiled=True).reshape(tokens, 2 * HD)
            own, far = jnp.where(even, both[:, :HD], both[:, HD:]), jnp.where(even, both[:, HD:], both[:, :HD])
            output_part = end_quads([], [output_quad])
        dkeyval = jnp.concatenate([jnp.where(even, own, far), jnp.where(even, far, own)], axis=1)

        (outputs,) = by_rows(
            output_kernel, tokens, tile,
            [(resid, True), (mlp, True), (swap_tp(mlp), True), (row(down_bias), False)], [(width, BF)], "outputs", weight=1,
        )

        kv_quad = direct_quad(spot, v_first, dkeyval, shard)
        query_quad, formed = middle_quad(query_quad)
        dkv_late, _ = lax.optimization_barrier((dkeyval, (kv_quad[0], formed)))
        input_grad, first_sums = exchange_rows(
            dv_part, first_finish, tokens, tile, [(dquery, True), (query_weight, False)],
            [(dkv_late, True), (keyval_weight, False), (x, True), (dres, True), (row(first_gain), False)],
            [(width, BF)], "first_back", 2, sums=2,
        )
        query_quad, first_sums = lax.optimization_barrier((query_quad, first_sums))
        merged = end_quads([], [query_quad, kv_quad])
        output_share = scatter_rest(output_part)
        first_share, _ = lax.optimization_barrier((first_share, merged))
        spread(first_share)
        spread(last_share)
        up_weight_grad, down_weight_grad = place_shares(spot.reshape(1), shares, counts, unit_tile, units)
        both = scatter_rest(merged)

        arrays, _ = lax.optimization_barrier(([first_sums, query_bias_grad.reshape(1, -1), second_sums, up_bias_grad], merged))
        vector = pack(arrays, dkeyval)
        total, (outputs, up_weight_grad, down_weight_grad) = sum_all(vector, (outputs, up_weight_grad, down_weight_grad))
        (output_share, both), _ = lax.optimization_barrier(((output_share, both), (total, up_weight_grad)))
        output_weight_grad, query_weight_grad, keyval_weight_grad = finish(output_share, both, query_weight.shape[1])
        sizes = [width, width, query_bias.shape[0], width, width, width, width, up_bias.shape[0], HD]
        small, offset = [], 0
        for size in sizes:
            small.append(total[0, offset : offset + size])
            offset += size
        return (
            outputs.reshape(rows, seg, width),
            input_grad.reshape(rows, seg, width),
            small[0],
            small[1],
            query_weight_grad,
            small[2],
            keyval_weight_grad,
            small[8],
            output_weight_grad,
            small[5],
            small[3],
            small[4],
            up_weight_grad,
            small[7],
            down_weight_grad,
            small[6],
        )

    return per_device


def solution(mesh):
    placed = (
        P("dp", "sp", None),
        P("dp"),
        P(),
        P(),
        P(None, "tp"),
        P("tp"),
        P(),
        P(),
        P("tp", None),
        P(),
        P(),
        P(),
        P(None, "tp"),
        P("tp"),
        P("tp", None),
        P(),
        P("dp", "sp", None),
    )
    return jax.shard_map(
        build(mesh),
        mesh=mesh,
        in_specs=placed,
        out_specs=(
            P("dp", "sp", None),
            P("dp", "sp", None),
            P(),
            P(),
            P(("dp", "sp"), "tp"),
            P("tp"),
            P(("dp", "sp"), None),
            P(),
            P("tp", ("dp", "sp")),
            P(),
            P(),
            P(),
            P(("dp", "sp"), "tp"),
            P("tp"),
            P("tp", ("dp", "sp")),
            P(),
        ),
        check_vma=False,
    )
```

```python
import functools
import math

import jax
import jax.numpy as jnp
from jax import lax
from jax.experimental import pallas as pl
from jax.experimental.pallas import tpu as pltpu
from jax.sharding import PartitionSpec as P

HD = 128
EPS = 1e-05
BF = jnp.bfloat16
F32 = jnp.float32
SCALE = 1.0 / math.sqrt(HD)
SCALE2 = SCALE * math.log2(math.e)
VMEM = 60 * 2**20
GELU_A = math.sqrt(2.0 / math.pi)
GELU_B = 0.044715


def nn(left, right):
    return jnp.dot(left, right, preferred_element_type=F32)


def nt(left, right):
    return lax.dot_general(left, right, (((1,), (1,)), ((), ())), preferred_element_type=F32)


def tn(left, right):
    return lax.dot_general(left, right, (((0,), (0,)), ((), ())), preferred_element_type=F32)


def params():
    return pltpu.CompilerParams(vmem_limit_bytes=VMEM)


def cost(macs, moved, weight=10):
    return pl.CostEstimate(flops=int(2 * macs * weight), bytes_accessed=int(moved * weight), transcendentals=0)


def whole(*shape):
    return pl.BlockSpec(shape, lambda *_: (0,) * len(shape))


def chunk_mask(first, length, chunk, size, seg, wide):
    key_pos = chunk * size + lax.broadcasted_iota(jnp.int32, (size, wide), 0)
    query_pos = first + lax.rem(lax.broadcasted_iota(jnp.int32, (size, wide), 1), seg)
    return (key_pos <= query_pos) & (key_pos < length)


def chunk_bounds(info_ref, row, seg, size):
    first, length = info_ref[0], info_ref[3 + row]
    full = jnp.minimum(first + 1, length) // size
    total = (jnp.minimum(first + seg, length) + size - 1) // size
    return first, length, full, total


def stack_heads(ref, heads):
    return jnp.concatenate([ref[0, :, h * HD : (h + 1) * HD] for h in range(heads)], axis=0)


def unstack_heads(ref, values, heads, seg):
    for h in range(heads):
        ref[0, :, h * HD : (h + 1) * HD] = values[h * seg : (h + 1) * seg]


def forward_kernel(size, heads, seg, info_ref, q_ref, kv_ref, o_ref, lse_ref, top_s, sum_s, acc_s):
    first, length, full, total = chunk_bounds(info_ref, pl.program_id(0), seg, size)
    q = stack_heads(q_ref, heads)
    top_s[...] = jnp.full_like(top_s, -1e30)
    sum_s[...] = jnp.zeros_like(sum_s)
    acc_s[...] = jnp.zeros_like(acc_s)

    def step(masked, chunk, carry):
        at = pl.ds(pl.multiple_of((chunk ^ info_ref[1]) * size, size), size)
        scores = nt(kv_ref[info_ref[2], 0, at, :], q) * SCALE2
        if masked:
            scores = jnp.where(chunk_mask(first, length, chunk, size, seg, heads * seg), scores, -1e30)
        old = top_s[...]
        new = jnp.maximum(old, jnp.max(scores, axis=0, keepdims=True))
        weights = jnp.exp2(scores - new)
        shrink = jnp.exp2(old - new)
        sum_s[...] = sum_s[...] * shrink + jnp.sum(weights, axis=0, keepdims=True)
        acc_s[...] = acc_s[...] * shrink + tn(kv_ref[1 - info_ref[2], 0, at, :], weights.astype(BF))
        top_s[...] = new
        return carry

    lax.fori_loop(0, full, functools.partial(step, False), 0)
    lax.fori_loop(full, total, functools.partial(step, True), 0)
    unstack_heads(o_ref, (acc_s[...] * (1.0 / sum_s[...])).T.astype(BF), heads, seg)
    lse_ref[0, 0] = top_s[...] + jnp.log2(sum_s[...])


def attend_forward(info, query, keyval, size, heads):
    rows, seg, width = query.shape
    length = keyval.shape[2]
    groups, wide = width // (HD * heads), heads * seg
    head_spec = pl.BlockSpec((1, seg, heads * HD), lambda r, h, info: (r, 0, h))
    return pl.pallas_call(
        functools.partial(forward_kernel, size, heads, seg),
        grid_spec=pltpu.PrefetchScalarGridSpec(
            num_scalar_prefetch=1,
            grid=(rows, groups),
            in_specs=[head_spec, pl.BlockSpec((2, 1, length, HD), lambda r, h, info: (0, r, 0, 0))],
            out_specs=[head_spec, pl.BlockSpec((1, 1, 1, wide), lambda r, h, info: (r, h, 0, 0))],
            scratch_shapes=[pltpu.VMEM((1, wide), F32), pltpu.VMEM((1, wide), F32), pltpu.VMEM((HD, wide), F32)],
        ),
        out_shape=[
            jax.ShapeDtypeStruct((rows, seg, width), BF),
            jax.ShapeDtypeStruct((rows, groups, 1, wide), F32),
        ],
        compiler_params=params(),
        cost_estimate=cost(8 * 10**9, 4 * 2**20),
        name="attend_forward",
    )(info, query, keyval)


def backward_kernel(
    size, heads, seg, info_ref, q_ref, do_ref, o_ref, lse_ref, kv_ref, dq_ref, bias_ref, dk_ref, dv_ref, dqt_s
):
    row, group = pl.program_id(0), pl.program_id(1)
    first, length, full, total = chunk_bounds(info_ref, row, seg, size)

    @pl.when(group == 0)
    def _():
        dk_ref[...] = jnp.zeros_like(dk_ref)
        dv_ref[...] = jnp.zeros_like(dv_ref)

    q, dout, out = (stack_heads(ref, heads) for ref in (q_ref, do_ref, o_ref))
    delta = jnp.sum((dout.astype(F32) * out.astype(F32)).T, axis=0, keepdims=True)
    lse = lse_ref[0, 0]
    dqt_s[...] = jnp.zeros_like(dqt_s)

    def step(masked, chunk, carry):
        at = pl.ds(pl.multiple_of((chunk ^ info_ref[1]) * size, size), size)
        keys = kv_ref[info_ref[2], 0, at, :]
        prob = jnp.exp2(nt(keys, q) * SCALE2 - lse)
        if masked:
            prob = jnp.where(chunk_mask(first, length, chunk, size, seg, heads * seg), prob, 0.0)
        dprob = nt(kv_ref[1 - info_ref[2], 0, at, :], dout)
        dscore = (prob * (dprob - delta)).astype(BF)
        dv_ref[0, at, :] += nn(prob.astype(BF), dout)
        dk_ref[0, at, :] += nn(dscore, q) * SCALE
        dqt_s[...] += tn(keys, dscore)
        return carry

    lax.fori_loop(0, full, functools.partial(step, False), 0)
    lax.fori_loop(full, total, functools.partial(step, True), 0)
    dq = (dqt_s[...] * SCALE).T.astype(BF)
    unstack_heads(dq_ref, dq, heads, seg)
    for h in range(heads):
        bias_ref[0, :, h * HD : (h + 1) * HD] = jnp.sum(
            dq[h * seg : (h + 1) * seg].astype(F32), axis=0, keepdims=True
        )


def attend_backward(info, query, dout, out, lse, keyval, size, heads):
    rows, seg, width = query.shape
    length = keyval.shape[2]
    groups, wide = width // (HD * heads), heads * seg
    head_spec = pl.BlockSpec((1, seg, heads * HD), lambda r, h, info: (r, 0, h))
    key_spec = pl.BlockSpec((1, length, HD), lambda r, h, info: (r, 0, 0))
    return pl.pallas_call(
        functools.partial(backward_kernel, size, heads, seg),
        grid_spec=pltpu.PrefetchScalarGridSpec(
            num_scalar_prefetch=1,
            grid=(rows, groups),
            in_specs=[
                head_spec,
                head_spec,
                head_spec,
                pl.BlockSpec((1, 1, 1, wide), lambda r, h, info: (r, h, 0, 0)),
                pl.BlockSpec((2, 1, length, HD), lambda r, h, info: (0, r, 0, 0)),
            ],
            out_specs=[head_spec, pl.BlockSpec((1, 1, heads * HD), lambda r, h, info: (r, 0, h)), key_spec, key_spec],
            scratch_shapes=[pltpu.VMEM((HD, wide), F32)],
        ),
        out_shape=[
            jax.ShapeDtypeStruct((rows, seg, width), BF),
            jax.ShapeDtypeStruct((rows, 1, width), F32),
            jax.ShapeDtypeStruct((rows, length, HD), F32),
            jax.ShapeDtypeStruct((rows, length, HD), F32),
        ],
        compiler_params=params(),
        cost_estimate=cost(12 * 10**9, 8 * 2**20),
        name="attend_backward",
    )(info, query, dout, out, lse, keyval)


def gelu_parts(v):
    square = v * v
    t = jnp.tanh(GELU_A * v * (1.0 + GELU_B * square))
    half = 0.5 * (1.0 + t)
    slope = half + 0.5 * v * (1.0 - t * t) * (GELU_A * (1.0 + 3.0 * GELU_B * square))
    return v * half, slope


def local_kernel(parts, u_ref, dm_ref, *refs):
    piece_refs, refs = refs[:parts], refs[parts:]
    up_ref, down_ref, bias_ref, hidden_ref, du_ref, dbias_ref, u_all_ref, dm_rest_ref, du_s, u_s, send, recv, local = refs
    step, last = pl.program_id(0), pl.num_programs(0) - 1
    dp, sp, tp = lax.axis_index("dp"), lax.axis_index("sp"), lax.axis_index("tp")
    half = u_ref.shape[0] // 2
    quarter = half // 2
    over_x, over_y, sibling = (dp, sp ^ 1, tp), (dp, sp ^ 2, tp), (dp, sp, 1 - tp)

    def remote(k, source, target, device):
        return pltpu.make_async_remote_copy(
            source, target, send.at[k], recv.at[k], device_id=device, device_id_type=pl.DeviceIdType.MESH
        )

    own = u_s.at[pl.ds(pl.multiple_of(tp * half, half), half), :]
    other = u_s.at[pl.ds(pl.multiple_of((1 - tp) * half, half), half), :]
    top, bottom = pl.ds(0, quarter), pl.ds(quarter, quarter)
    own_top = u_s.at[pl.ds(pl.multiple_of(tp * half, quarter), quarter), :]
    own_bottom = u_s.at[pl.ds(pl.multiple_of(tp * half + quarter, quarter), quarter), :]
    first = [remote(0, own_top, u_all_ref.at[1, top], over_x), remote(1, own_bottom, u_all_ref.at[2, bottom], over_y)]
    second = [remote(2, own_bottom, u_all_ref.at[1, bottom], over_x), remote(3, own_top, u_all_ref.at[2, top], over_y)]
    passes = [
        remote(4, u_all_ref.at[1, top], u_all_ref.at[3, top], over_y),
        remote(5, u_all_ref.at[2, bottom], u_all_ref.at[3, bottom], over_x),
    ]
    shares = [remote(5 + k, u_all_ref.at[k], u_all_ref.at[3 + k], sibling) for k in (1, 2, 3)]
    dm_shares = [remote(9 + k, piece, dm_rest_ref.at[k], sibling) for k, piece in enumerate(piece_refs)]
    keep_own = pltpu.make_async_copy(own, u_all_ref.at[0], local.at[0])
    keep_other = pltpu.make_async_copy(other, u_all_ref.at[7], local.at[1])

    @pl.when(step == 0)
    def _():
        barrier = pltpu.get_barrier_semaphore()
        for device in (over_x, over_y, sibling):
            pl.semaphore_signal(barrier, inc=1, device_id=device, device_id_type=pl.DeviceIdType.MESH)
        pl.semaphore_wait(barrier, 3)
        u_s[...] = u_ref[...]
        for copy in (*first, *second, *dm_shares):
            copy.start()
        keep_own.start()
        keep_other.start()
        du_s[...] = jnp.zeros_like(du_s)

    @pl.when(step == (last + 1) // 2)
    def _():
        for copy in first:
            copy.wait_recv()
        for copy in passes:
            copy.start()

    @pl.when(step == last)
    def _():
        for copy in second:
            copy.wait_recv()
        shares[0].start()
        shares[1].start()

    hidden, slope = gelu_parts(nn(u_ref[...], up_ref[...]) + bias_ref[...])
    hidden_ref[...] = hidden.astype(BF)
    dpre = (nt(dm_ref[...], down_ref[...]) * slope).astype(BF)
    dbias_ref[...] = jnp.sum(dpre.astype(F32), axis=0, keepdims=True)
    du_s[...] += nt(dpre, up_ref[...])

    @pl.when(step == last)
    def _():
        for copy in passes:
            copy.wait_recv()
        shares[2].start()
        du_ref[...] = du_s[...].astype(BF)
        for copy in (*first, *second, *passes):
            copy.wait_send()
        for copy in (*shares, *dm_shares):
            copy.wait()
        keep_own.wait()
        keep_other.wait()


def feed_local(u, dmlp, pieces, up, down, bias, tile):
    tokens, width = u.shape
    units = up.shape[1]
    block = whole(tokens, width)
    anywhere = pl.BlockSpec(memory_space=pl.ANY)
    return pl.pallas_call(
        functools.partial(local_kernel, len(pieces)),
        grid=(units // tile,),
        in_specs=[
            block,
            block,
            *[anywhere] * len(pieces),
            pl.BlockSpec((width, tile), lambda i: (0, i)),
            pl.BlockSpec((tile, width), lambda i: (i, 0)),
            pl.BlockSpec((1, tile), lambda i: (0, i)),
        ],
        out_specs=[
            pl.BlockSpec((tokens, tile), lambda i: (0, i)),
            block,
            pl.BlockSpec((1, tile), lambda i: (0, i)),
            anywhere,
            anywhere,
        ],
        out_shape=[
            jax.ShapeDtypeStruct((tokens, units), BF),
            jax.ShapeDtypeStruct((tokens, width), BF),
            jax.ShapeDtypeStruct((1, units), F32),
            jax.ShapeDtypeStruct((8, tokens // 2, width), BF),
            jax.ShapeDtypeStruct((len(pieces), *pieces[0].shape), BF),
        ],
        scratch_shapes=[
            pltpu.VMEM((tokens, width), F32),
            pltpu.VMEM((tokens, width), BF),
            pltpu.SemaphoreType.DMA((9 + len(pieces),)),
            pltpu.SemaphoreType.DMA((9 + len(pieces),)),
            pltpu.SemaphoreType.DMA((2,)),
        ],
        compiler_params=pltpu.CompilerParams(vmem_limit_bytes=VMEM, collective_id=0, has_side_effects=True),
        cost_estimate=cost(3 * tokens * width * units, 4 * width * units),
        name="feed_local",
    )(u, dmlp, *pieces, up, down, bias)


def mlp_kernel(hidden_ref, down_ref, out_ref, total_s):
    @pl.when(pl.program_id(0) == 0)
    def _():
        total_s[...] = jnp.zeros_like(total_s)

    total_s[...] += nn(hidden_ref[...], down_ref[...])

    @pl.when(pl.program_id(0) == pl.num_programs(0) - 1)
    def _():
        out_ref[...] = total_s[...].astype(BF)


def feed_out(hidden, down, tile):
    tokens, units = hidden.shape
    width = down.shape[1]
    return pl.pallas_call(
        mlp_kernel,
        grid=(units // tile,),
        in_specs=[pl.BlockSpec((tokens, tile), lambda i: (0, i)), pl.BlockSpec((tile, width), lambda i: (i, 0))],
        out_specs=whole(tokens, width),
        out_shape=jax.ShapeDtypeStruct((tokens, width), BF),
        scratch_shapes=[pltpu.VMEM((tokens, width), F32)],
        compiler_params=params(),
        cost_estimate=cost(tokens * width * units, 2 * width * units, 10),
        name="feed_out",
    )(hidden, down)


def grad_kernel(u_parts, parts, at_ref, *refs):
    pieces, (up_ref, down_ref, bias_ref, out_ref, u_s, dm_s, sems) = refs[:parts], refs[parts:]

    def copies(target):
        offset = 0
        for k in range(u_parts) if target is u_s else range(u_parts, parts):
            piece = pieces[k]
            yield pltpu.make_async_copy(piece, target.at[pl.ds(offset, piece.shape[0]), :], sems.at[k])
            offset += piece.shape[0]

    @pl.when(pl.program_id(0) == 0)
    def _():
        for copy in copies(u_s):
            copy.start()
        for copy in copies(dm_s):
            copy.start()
        for copy in copies(u_s):
            copy.wait()
        for copy in copies(dm_s):
            copy.wait()

    tile = up_ref.shape[1]
    hidden, slope = gelu_parts(nn(u_s[...], up_ref[...]) + bias_ref[...])
    dpre = (nt(dm_s[...], down_ref[...]) * slope).astype(BF)
    out_ref[:, :tile] = tn(dpre, u_s[...]).T.astype(BF)
    out_ref[:, tile:] = tn(hidden.astype(BF), dm_s[...]).T.astype(BF)


def feed_grads(at, u, dmlp, up, down, bias, tile, count):
    width = up.shape[0]
    tokens = sum(part.shape[0] for part in u)
    return pl.pallas_call(
        functools.partial(grad_kernel, len(u), len(u) + len(dmlp)),
        grid_spec=pltpu.PrefetchScalarGridSpec(
            num_scalar_prefetch=1,
            grid=(count,),
            in_specs=[
                *[pl.BlockSpec(memory_space=pl.ANY)] * (len(u) + len(dmlp)),
                pl.BlockSpec((width, tile), lambda i, at: (0, at[0] + i)),
                pl.BlockSpec((tile, width), lambda i, at: (at[0] + i, 0)),
                pl.BlockSpec((1, tile), lambda i, at: (0, at[0] + i)),
            ],
            out_specs=pl.BlockSpec((width, 2 * tile), lambda i, at: (0, i)),
            scratch_shapes=[
                pltpu.VMEM((tokens, width), BF),
                pltpu.VMEM((tokens, width), BF),
                pltpu.SemaphoreType.DMA((len(u) + len(dmlp),)),
            ],
        ),
        out_shape=jax.ShapeDtypeStruct((width, 2 * tile * count), BF),
        compiler_params=params(),
        cost_estimate=cost(4 * tokens * width * tile * count, 4 * width * (tokens + 2 * tile * count)),
        name="feed_grads",
    )(at, *u, *dmlp, up, down, bias)


def normalize(values):
    average = jnp.mean(values, axis=-1, keepdims=True)
    centered = values - average
    variance = jnp.mean(centered * centered, axis=-1, keepdims=True)
    inv_std = lax.rsqrt(variance + EPS)
    return centered * inv_std, inv_std


def norm_back(gradient, scaled, inv_std, norm_gain):
    inner = gradient * norm_gain
    mean_one = jnp.mean(inner, axis=-1, keepdims=True)
    mean_two = jnp.mean(inner * scaled, axis=-1, keepdims=True)
    return inv_std * (inner - mean_one - scaled * mean_two)


def column_sum(values):
    return jnp.sum(values, axis=0, keepdims=True)


def by_rows(body, tokens, tile, ins, outs, name, sums=0, weight=1):
    row = lambda columns: pl.BlockSpec((tile, columns), lambda i: (i, 0))
    specs = [row(a.shape[1]) if cut else whole(*a.shape) for a, cut in ins]
    shapes = [jax.ShapeDtypeStruct((tokens, columns), dtype) for columns, dtype in outs]
    out_specs = [row(columns) for columns, _ in outs]
    if sums:
        shapes.append(jax.ShapeDtypeStruct((sums, outs[0][0]), F32))
        out_specs.append(whole(sums, outs[0][0]))
    moved = sum(a.size * a.dtype.itemsize for a, _ in ins) + sum(s.size * s.dtype.itemsize for s in shapes)
    return pl.pallas_call(
        body,
        grid=(tokens // tile,),
        in_specs=specs,
        out_specs=out_specs,
        out_shape=shapes,
        compiler_params=params(),
        cost_estimate=cost(moved * 200, moved, weight),
        name=name,
    )(*[a for a, _ in ins])


def first_kernel(x_ref, gain_ref, bias_ref, w_ref, wb_ref, v_ref, kv_ref):
    hat, _ = normalize(x_ref[...].astype(F32))
    v = (hat * gain_ref[...] + bias_ref[...]).astype(BF)
    v_ref[...] = v
    kv_ref[...] = (nn(v, w_ref[...]) + wb_ref[...]).astype(BF)


def exchange_rows(part, finish, tokens, tile, firsts, ins, outs, name, collective_id, sums=0):
    count = tokens // tile
    now, late = lambda i: (jnp.minimum(i, count - 1), 0), lambda i: (jnp.maximum(i - 1, 0), 0)
    spec = lambda a, cut, at: pl.BlockSpec((tile, a.shape[1]), at) if cut else whole(*a.shape)
    width = outs[0][0]

    def kernel(*refs):
        first_refs, refs = refs[: len(firsts)], refs[len(firsts) :]
        in_refs, refs = refs[: len(ins)], refs[len(ins) :]
        out_refs, (own_s, far_s, send, recv) = refs[:-4], refs[-4:]
        step = pl.program_id(0)
        sibling = (lax.axis_index("dp"), lax.axis_index("sp"), 1 - lax.axis_index("tp"))

        def copy(k):
            return pltpu.make_async_remote_copy(
                own_s.at[k], far_s.at[k], send.at[k], recv.at[k],
                device_id=sibling, device_id_type=pl.DeviceIdType.MESH,
            )

        @pl.when(step == 0)
        def _():
            barrier = pltpu.get_barrier_semaphore()
            pl.semaphore_signal(barrier, inc=1, device_id=sibling, device_id_type=pl.DeviceIdType.MESH)
            pl.semaphore_wait(barrier, 1)
            if sums:
                out_refs[-1][...] = jnp.zeros_like(out_refs[-1])

        @pl.when(step < count)
        def _():
            own_s[step] = part(*first_refs).astype(BF)
            copy(step).start()

        @pl.when(step > 0)
        def _():
            copy(step - 1).wait_recv()
            finish(own_s[step - 1].astype(F32) + far_s[step - 1].astype(F32), in_refs, out_refs)

        @pl.when(step == count)
        def _():
            for k in range(count):
                copy(k).wait_send()

    shapes = [jax.ShapeDtypeStruct((tokens, columns), dtype) for columns, dtype in outs]
    out_specs = [pl.BlockSpec((tile, columns), late) for columns, _ in outs]
    if sums:
        shapes.append(jax.ShapeDtypeStruct((sums, width), F32))
        out_specs.append(whole(sums, width))
    moved = sum(a.size * a.dtype.itemsize for a, _ in (*firsts, *ins))
    return pl.pallas_call(
        kernel,
        grid=(count + 1,),
        in_specs=[spec(a, cut, now) for a, cut in firsts] + [spec(a, cut, late) for a, cut in ins],
        out_specs=out_specs,
        out_shape=shapes,
        scratch_shapes=[
            pltpu.VMEM((count, tile, width), BF),
            pltpu.VMEM((count, tile, width), BF),
            pltpu.SemaphoreType.DMA((count,)),
            pltpu.SemaphoreType.DMA((count,)),
        ],
        compiler_params=pltpu.CompilerParams(vmem_limit_bytes=VMEM, collective_id=collective_id, has_side_effects=True),
        cost_estimate=cost(moved * 200, moved, 1),
        name=name,
    )(*[a for a, _ in firsts], *[a for a, _ in ins])


def proj_part(attended_ref, w_ref):
    return nn(attended_ref[...], w_ref[...])


def second_finish(proj, ins, outs):
    x_ref, ob_ref, gain_ref, bias_ref = ins
    resid_ref, u_ref = outs
    resid = x_ref[...].astype(F32) + proj + ob_ref[...]
    resid_ref[...] = resid
    hat, _ = normalize(resid)
    u_ref[...] = (hat * gain_ref[...] + bias_ref[...]).astype(BF)


def dv_part(dq_ref, w_ref):
    return nt(dq_ref[...], w_ref[...])


def first_finish(dv, ins, outs):
    dkv_ref, w_ref, x_ref, dres_ref, gain_ref = ins
    grad_ref, sums_ref = outs
    dv = dv + nt(dkv_ref[...], w_ref[...])
    hat, inv_std = normalize(x_ref[...].astype(F32))
    grad_ref[...] = (dres_ref[...] + norm_back(dv, hat, inv_std, gain_ref[...])).astype(BF)
    sums_ref[...] += jnp.concatenate([column_sum(dv * hat), column_sum(dv)], axis=0)


def second_back_kernel(own_ref, far_ref, resid_ref, dm_ref, gain_ref, dres_ref, dproj_ref, sums_ref):
    @pl.when(pl.program_id(0) == 0)
    def _():
        sums_ref[...] = jnp.zeros_like(sums_ref)

    du = own_ref[...].astype(F32) + far_ref[...].astype(F32)
    hat, inv_std = normalize(resid_ref[...])
    dout = dm_ref[...].astype(F32)
    dres = dout + norm_back(du, hat, inv_std, gain_ref[...])
    dres_ref[...] = dres
    dproj_ref[...] = dres.astype(BF)
    sums_ref[...] += jnp.concatenate(
        [column_sum(du * hat), column_sum(du), column_sum(dres), column_sum(dout)], axis=0
    )


def output_kernel(resid_ref, own_ref, far_ref, bias_ref, out_ref):
    mlp = own_ref[...].astype(F32) + far_ref[...].astype(F32)
    out_ref[...] = (resid_ref[...] + mlp + bias_ref[...]).astype(BF)


def project(left, right, transposed, tile, name, bias=None):
    tokens, depth = left.shape
    columns = right.shape[0] if transposed else right.shape[1]

    def body(*refs):
        product = (nt if transposed else nn)(refs[0][...], refs[1][...])
        if bias is not None:
            product = product + refs[2][...]
        refs[-1][...] = product.astype(BF)

    spec = pl.BlockSpec((tile, depth), lambda i: (i, 0)) if transposed else pl.BlockSpec((depth, tile), lambda i: (0, i))
    extra = [] if bias is None else [bias.reshape(1, columns)]
    return pl.pallas_call(
        body,
        grid=(columns // tile,),
        in_specs=[whole(tokens, depth), spec] + [pl.BlockSpec((1, tile), lambda i: (0, i))] * len(extra),
        out_specs=pl.BlockSpec((tokens, tile), lambda i: (0, i)),
        out_shape=jax.ShapeDtypeStruct((tokens, columns), BF),
        compiler_params=params(),
        cost_estimate=cost(tokens * depth * columns, 2 * (tokens * (depth + columns) + depth * columns)),
        name=name,
    )(left, right, *extra)


def rows_kernel(groups, shard, count, spot_ref, left_ref, *refs):
    rights, (keep_ref, x_ref, y_ref) = refs[:count], refs[count:]
    step = pl.program_id(0)
    dest = spot_ref[0] ^ step
    cols = [left_ref[:, pl.ds(pl.multiple_of((g * 4 + dest) * shard, shard), shard)] for g in range(groups)]
    left = jnp.concatenate(cols, axis=1)
    product = jnp.concatenate([tn(left, right[...]).astype(BF) for right in rights], axis=1)
    half = product.shape[0] // 2
    low, high = product[:half], product[half:]

    @pl.when(step == 0)
    def _():
        keep_ref[0], keep_ref[1] = low, high

    @pl.when(step == 1)
    def _():
        x_ref[0], keep_ref[3] = low, high

    @pl.when(step == 2)
    def _():
        keep_ref[2], y_ref[0] = low, high

    @pl.when(step == 3)
    def _():
        x_ref[1], y_ref[1] = low, high


def rows_grad(spot, left, rights, groups, shard):
    tokens, width = left.shape
    columns = sum(right.shape[1] for right in rights)
    half = groups * shard // 2
    return pl.pallas_call(
        functools.partial(rows_kernel, groups, shard, len(rights)),
        grid_spec=pltpu.PrefetchScalarGridSpec(
            num_scalar_prefetch=1,
            grid=(4,),
            in_specs=[whole(tokens, width), *[whole(*right.shape) for right in rights]],
            out_specs=[whole(4, half, columns), whole(2, half, columns), whole(2, half, columns)],
        ),
        out_shape=[jax.ShapeDtypeStruct((n, half, columns), BF) for n in (4, 2, 2)],
        compiler_params=params(),
        cost_estimate=cost(tokens * width * columns, 2 * (tokens + columns) * width, 1),
        name="rows_grad",
    )(spot, left, *rights)


def direct_kernel(groups, shard, spot_ref, left_ref, right_ref, *out_refs):
    for bit in range(4):
        dest = spot_ref[0] ^ bit
        cols = [left_ref[:, pl.ds(pl.multiple_of((g * 4 + dest) * shard, shard), shard)] for g in range(groups)]
        out_refs[bit][...] = tn(jnp.concatenate(cols, axis=1), right_ref[...]).astype(BF)


def rows_direct(spot, left, right, groups, shard):
    shape = (groups * shard, right.shape[1])
    return pl.pallas_call(
        functools.partial(direct_kernel, groups, shard),
        grid_spec=pltpu.PrefetchScalarGridSpec(
            num_scalar_prefetch=1,
            grid=(1,),
            in_specs=[whole(*left.shape), whole(*right.shape)],
            out_specs=[whole(*shape)] * 4,
        ),
        out_shape=[jax.ShapeDtypeStruct(shape, BF)] * 4,
        compiler_params=params(),
        cost_estimate=cost(left.size * right.shape[1], 2 * left.size, 1),
        name="rows_direct",
    )(spot, left, right)


def add_kernel(keep_ref, x_ref, y_ref, low_ref, high_ref):
    low_ref[...] = (keep_ref[2].astype(F32) + x_ref[1].astype(F32)).astype(BF)
    high_ref[...] = (keep_ref[3].astype(F32) + y_ref[1].astype(F32)).astype(BF)


def add_passed(keep, from_x, from_y):
    shape = keep.shape[1:]
    return pl.pallas_call(
        add_kernel,
        in_specs=[whole(*keep.shape), whole(*from_x.shape), whole(*from_y.shape)],
        out_specs=[whole(*shape), whole(*shape)],
        out_shape=[jax.ShapeDtypeStruct(shape, BF)] * 2,
        grid=(1,),
        compiler_params=params(),
        cost_estimate=cost(0, 8 * shape[0] * shape[1] * 2, 1),
        name="add_passed",
    )(keep, from_x, from_y)


def total_kernel(ready, *refs):
    out_ref, offset = refs[-1], 0
    for k in range(ready):
        columns = refs[k].shape[1]
        out_ref[:, offset : offset + columns] = refs[k][...]
        offset += columns
    keep_ref, x_ref, y_ref, low_ref, high_ref = refs[ready : ready + 5]
    half, columns = low_ref.shape
    at = slice(offset, offset + columns)
    out_ref[:half, at] = (keep_ref[0].astype(F32) + x_ref[0].astype(F32) + low_ref[...].astype(F32)).astype(BF)
    out_ref[half:, at] = (keep_ref[1].astype(F32) + y_ref[0].astype(F32) + high_ref[...].astype(F32)).astype(BF)
    rest = refs[ready + 5 : -1]
    if rest:
        out_ref[:, offset + columns :] = sum(ref[...].astype(F32) for ref in rest).astype(BF)


def add_total(ready, quads):
    arrays = [*ready, *[array for quad in quads for array in quad]]
    lead = 2 * quads[0][3].shape[0]
    columns = sum(a.shape[1] for a in ready) + sum(quad[3].shape[1] for quad in quads)
    return pl.pallas_call(
        functools.partial(total_kernel, len(ready)),
        in_specs=[whole(*a.shape) for a in arrays],
        out_specs=whole(lead, columns),
        out_shape=jax.ShapeDtypeStruct((lead, columns), BF),
        grid=(1,),
        compiler_params=params(),
        cost_estimate=cost(0, 8 * lead * columns, 1),
        name="add_total",
    )(*arrays)


def finish_kernel(output_ref, both_ref, out_ref, query_ref, kv_ref):
    columns = query_ref.shape[1]
    out_ref[...] = output_ref[...].astype(F32).T
    query_ref[...] = both_ref[:, :columns].astype(F32)
    kv_ref[...] = both_ref[:, columns:].astype(F32)


def finish(output, both, columns):
    shard, total = both.shape
    shapes = [(output.shape[1], shard), (shard, columns), (shard, total - columns)]
    return pl.pallas_call(
        finish_kernel,
        in_specs=[whole(*output.shape), whole(shard, total)],
        out_specs=[whole(*shape) for shape in shapes],
        out_shape=[jax.ShapeDtypeStruct(shape, F32) for shape in shapes],
        grid=(1,),
        compiler_params=params(),
        cost_estimate=cost(0, 6 * shard * total, 1),
        name="finish",
    )(output, both)


def pack_kernel(*refs):
    *in_refs, kv_ref, out_ref = refs
    offset = 0
    for ref in in_refs:
        for k in range(ref.shape[0]):
            out_ref[:, offset : offset + ref.shape[1]] = ref[k : k + 1]
            offset += ref.shape[1]
    out_ref[:, offset:] = column_sum(kv_ref[:, HD:].astype(F32))


def pack(arrays, dkeyval):
    size = sum(a.size for a in arrays) + HD
    return pl.pallas_call(
        pack_kernel,
        in_specs=[whole(*a.shape) for a in (*arrays, dkeyval)],
        out_specs=whole(1, size),
        out_shape=jax.ShapeDtypeStruct((1, size), F32),
        grid=(1,),
        compiler_params=params(),
        cost_estimate=cost(0, 8 * size, 1),
        name="pack",
    )(*arrays, dkeyval)


def place_kernel(tile, counts, spot_ref, *refs):
    shares, (up_ref, down_ref) = refs[:-2], refs[-2:]
    units = up_ref.shape[1] // 4
    for bit in range(4):
        at = (spot_ref[0] ^ bit) * units
        tile_at = 0
        for piece, count in enumerate(counts):
            for k in range(count):
                block = shares[piece * 4 + bit][:, k * 2 * tile : (k + 1) * 2 * tile].astype(F32)
                spot = pl.ds(pl.multiple_of(at + (tile_at + k) * tile, tile), tile)
                up_ref[:, spot] = block[:, :tile]
                down_ref[spot, :] = block[:, tile:].T
            tile_at += count


def place_shares(spot, shares, counts, tile, units):
    shard = shares[0].shape[0]
    return pl.pallas_call(
        functools.partial(place_kernel, tile, counts),
        grid_spec=pltpu.PrefetchScalarGridSpec(
            num_scalar_prefetch=1,
            grid=(1,),
            in_specs=[whole(*share.shape) for share in shares],
            out_specs=[whole(shard, units), whole(units, shard)],
        ),
        out_shape=[jax.ShapeDtypeStruct((shard, units), F32), jax.ShapeDtypeStruct((units, shard), F32)],
        compiler_params=params(),
        cost_estimate=cost(0, 12 * shard * units, 1),
        name="place_shares",
    )(spot, *shares)


def build(mesh):
    sp_size, dp_size = mesh.shape["sp"], mesh.shape["dp"]
    quads = sp_size // 4

    def swap(value, bit, keep=None):
        pairs = [(i, i ^ bit) for i in range(sp_size)]
        return lax.ppermute(value, "sp", pairs if keep is None else [p for p in pairs if keep(*p)])

    def swap_dp(value, bit):
        return lax.ppermute(value, "dp", [(i, i ^ bit) for i in range(dp_size)])

    def swap_tp(value):
        return lax.ppermute(value, "tp", [(0, 1), (1, 0)])

    def sum_all(vector, fill):
        for exchange, size in ((swap, sp_size), (swap_dp, dp_size)):
            bit = 1
            while bit < size:
                if bit * 2 < size:
                    near, far, both = (exchange(vector, k) for k in (bit, 2 * bit, 3 * bit))
                    if exchange is swap_dp:
                        (near, far, both), fill = lax.optimization_barrier(((near, far, both), fill))
                    vector = (vector + near) + (far + both)
                else:
                    vector = vector + exchange(vector, bit)
                bit *= 4
        return vector, fill

    def half_of(own, core):
        half = own.shape[0] // 2
        return lax.dynamic_slice_in_dim(own, core * half, half, 0)

    def scatter_rest(value, after=None):
        if after is not None:
            value, _ = lax.optimization_barrier((value, after))
        value = lax.psum_scatter(value, "dp", scatter_dimension=0, tiled=True)
        if quads > 1:
            groups = [[q * 4 + r for q in range(quads)] for r in range(4)]
            value = lax.psum_scatter(value, "sp", scatter_dimension=0, tiled=True, axis_index_groups=groups)
        return value

    def start_quad(spot, left, rights, shard, after=()):
        groups = dp_size * quads
        if shard % 128 == 0:
            keep, to_x, to_y = rows_grad(spot.reshape(1), left, rights, groups, shard)
            to_x, to_y, _ = lax.optimization_barrier((to_x, to_y, after))
            return [keep, swap(to_x, 1), swap(to_y, 2)]
        value = jnp.concatenate([tn(left, right).astype(BF) for right in rights], axis=1)
        value = value.reshape(groups, 4, shard, -1)
        blocks = [
            lax.dynamic_index_in_dim(value, spot ^ bit, 1, keepdims=False).reshape(groups * shard, -1)
            for bit in range(4)
        ]
        return [blocks[0], *[swap(blocks[bit], bit) for bit in range(1, 4)]]

    def direct_quad(spot, left, right, shard):
        if shard % 128 == 0:
            blocks = rows_direct(spot.reshape(1), left, right, dp_size * quads, shard)
            return [blocks[0], *[swap(blocks[bit], bit) for bit in range(1, 4)]]
        return start_quad(spot, left, [right], shard)

    def middle_quad(parts):
        if len(parts) == 4:
            return parts, parts[0]
        low, high = add_passed(*parts)
        return [*parts, swap(low, 2), swap(high, 1)], low

    def end_quads(ready, quads):
        if len(quads[0]) == 5:
            return add_total(ready, quads)
        return jnp.concatenate([*ready, *[sum(p.astype(F32) for p in quad).astype(BF) for quad in quads]], axis=1)

    def per_device(
        inputs, lengths, first_gain, first_bias, query_weight, query_bias, keyval_weight, value_bias, output_weight,
        output_bias, second_gain, second_bias, up_weight, up_bias, down_weight, down_bias, cotangent,
    ):
        rows, seg, width = inputs.shape
        tokens = rows * seg
        place, core = lax.axis_index("sp").astype(jnp.int32), lax.axis_index("tp")
        spot = lax.rem(place, 4)
        row_len = seg * sp_size
        one_quad = quads == 1
        shard = width // (dp_size * sp_size)
        even = core == 0
        info = jnp.concatenate([jnp.stack([place * seg, spot if one_quad else 0 * spot, core.astype(jnp.int32)]), lengths])
        row = lambda vector: vector.reshape(1, -1)

        x = inputs.reshape(tokens, width)
        dmlp = cotangent.reshape(tokens, width)
        tile = min(tokens, 128)
        piece = lambda at: lax.dynamic_slice_in_dim(dmlp, at * (tokens // 4), tokens // 4, 0)
        x, dmlp_top, dmlp_bottom = lax.optimization_barrier((x, piece(2 * core), piece(2 * core + 1)))
        half_weight = lax.dynamic_slice_in_dim(keyval_weight, core * HD, HD, 1)
        half_bias = row(jnp.where(even, 0.0, value_bias))
        v_first, kv_half = by_rows(
            first_kernel, tokens, tile,
            [(x, True), (row(first_gain), False), (row(first_bias), False), (half_weight, False), (half_bias, False)],
            [(width, BF), (HD, BF)], "first_norm",
        )
        top_x, bottom_y = swap(dmlp_top, 1), swap(dmlp_bottom, 2)
        v_late, top_x, bottom_y = lax.optimization_barrier((v_first, top_x, bottom_y))
        query = project(v_late, query_weight, False, 512, "query", query_bias).reshape(rows, seg, -1)
        if one_quad:
            pieces = [kv_half, *[swap(kv_half, bit, lambda a, b: a < b) for bit in (1, 2, 3)]]
            pieces, query = lax.optimization_barrier((pieces, query))
            kv_mine = jnp.concatenate(pieces, axis=0).reshape(1, row_len, HD)
            size = seg
        else:
            kv_mine = lax.all_gather(kv_half.reshape(rows, seg, HD), "sp", axis=1, tiled=True)
            size = min(512, row_len)
        top_x, bottom_y, top, bottom, kv_mine = lax.optimization_barrier((top_x, bottom_y, dmlp_top, dmlp_bottom, kv_mine))
        dmlp_pieces = [top_x, swap(bottom, 1), swap(top, 2), bottom_y, swap(top_x, 2), swap(bottom_y, 1)]
        keyval_all = jnp.stack([kv_mine, swap_tp(kv_mine)])

        query, keyval_all = lax.optimization_barrier((query, keyval_all))

        attended, lse = attend_forward(info, query, keyval_all, size, query.shape[2] // HD)
        attended_flat = attended.reshape(tokens, -1)
        resid, u_second = exchange_rows(
            proj_part, second_finish, tokens, 2 * tile, [(attended_flat, True), (output_weight, False)],
            [(x, True), (row(output_bias), False), (row(second_gain), False), (row(second_bias), False)],
            [(width, F32), (width, BF)], "second_norm", 1,
        )
        up_bias_row = row(up_bias)
        hidden, du, up_bias_grad, u_all, dmlp_rest = feed_local(
            u_second, dmlp, dmlp_pieces, up_weight, down_weight, up_bias_row, 512
        )
        u_all = [u_all.reshape(4 * tokens, width)]
        dmlp_all = [dmlp_top, dmlp_bottom, *dmlp_pieces, dmlp_rest.reshape(-1, width), half_of(dmlp, 1 - core)]

        units = up_weight.shape[1]
        unit_tile = 256
        tiles = units // 4 // unit_tile
        counts = (1, tiles - 1)
        feed_part = lambda at, count: feed_grads(
            at.reshape(1), u_all, dmlp_all, up_weight, down_weight, up_bias_row, unit_tile, count
        )
        shares = []

        def spread(share):
            blocks = [lax.dynamic_slice_in_dim(share, (spot ^ bit) * shard, shard, 0) for bit in range(4)]
            shares.extend([blocks[0], *[swap(blocks[bit], bit) for bit in range(1, 4)]])

        first_part = feed_part(spot * tiles, counts[0])
        first_share = scatter_rest(first_part)
        at, _ = lax.optimization_barrier((spot * tiles + counts[0], first_part))
        last_part = feed_part(at, counts[1])
        last_share = scatter_rest(last_part)

        du_far, _ = lax.optimization_barrier((swap_tp(du), last_part))
        dres, dproj, second_sums = by_rows(
            second_back_kernel, tokens, tile,
            [(du, True), (du_far, True), (resid, True), (dmlp, True), (row(second_gain), False)],
            [(width, F32), (width, BF)], "second_back", sums=4,
        )
        output_quad = start_quad(spot, dproj, [attended_flat], shard)
        dproj, output_keep = lax.optimization_barrier((dproj, output_quad[0]))
        dattended = project(dproj, output_weight, True, 512, "dattended").reshape(rows, seg, -1)
        dattended, first_share = lax.optimization_barrier((dattended, first_share))
        dquery, query_bias_grad, dkey, dvalue = attend_backward(info, query, dattended, attended, lse, keyval_all, size, query.shape[2] // HD)
        dquery = dquery.reshape(tokens, -1)
        query_bias_grad = jnp.sum(query_bias_grad[:, 0], axis=0)
        dquery, output_quad = lax.optimization_barrier((dquery, [output_keep, *output_quad[1:]]))
        output_quad, formed = middle_quad(output_quad)
        dquery, _ = lax.optimization_barrier((dquery, formed))
        if one_quad:
            dkey, dvalue = dkey[0], dvalue[0]
            far = swap_tp(jnp.where(even, dvalue, dkey).astype(BF))
            half = jnp.where(even, dkey, dvalue) + far.astype(F32)
            sends = [half[bit * tokens : (bit + 1) * tokens].astype(BF) for bit in range(1, 4)]
            query_quad = start_quad(spot, v_first, [dquery], shard, sends)
            arrived = [swap(send, bit, lambda a, b: a > b) for bit, send in enumerate(sends, 1)]
            own = half[:tokens]
            for term in arrived:
                own = own + term.astype(F32)
            own = lax.optimization_barrier(own.astype(BF))
            far = swap_tp(own)
            output_part = end_quads([], [output_quad])
            hidden, _ = lax.optimization_barrier((hidden, (own, output_part, query_quad[0])))
            mlp = feed_out(hidden, down_weight, 512)
            far, mlp = lax.optimization_barrier((far, mlp))
        else:
            query_quad = start_quad(spot, v_first, [dquery], shard)
            mlp = feed_out(hidden, down_weight, 512)
            part = lax.psum(jnp.concatenate([dkey, dvalue], axis=2).astype(BF), "tp")
            both = lax.psum_scatter(part, "sp", scatter_dimension=1, tiled=True).reshape(tokens, 2 * HD)
            own, far = jnp.where(even, both[:, :HD], both[:, HD:]), jnp.where(even, both[:, HD:], both[:, :HD])
            output_part = end_quads([], [output_quad])
        dkeyval = jnp.concatenate([jnp.where(even, own, far), jnp.where(even, far, own)], axis=1)

        (outputs,) = by_rows(
            output_kernel, tokens, tile,
            [(resid, True), (mlp, True), (swap_tp(mlp), True), (row(down_bias), False)], [(width, BF)], "outputs", weight=1,
        )

        kv_quad = direct_quad(spot, v_first, dkeyval, shard)
        query_quad, formed = middle_quad(query_quad)
        dkv_late, _ = lax.optimization_barrier((dkeyval, (kv_quad[0], formed)))
        input_grad, first_sums = exchange_rows(
            dv_part, first_finish, tokens, 2 * tile, [(dquery, True), (query_weight, False)],
            [(dkv_late, True), (keyval_weight, False), (x, True), (dres, True), (row(first_gain), False)],
            [(width, BF)], "first_back", 2, sums=2,
        )
        query_quad, first_sums = lax.optimization_barrier((query_quad, first_sums))
        merged = end_quads([], [query_quad, kv_quad])
        output_share = scatter_rest(output_part)
        first_share, _ = lax.optimization_barrier((first_share, merged))
        spread(first_share)
        spread(last_share)
        up_weight_grad, down_weight_grad = place_shares(spot.reshape(1), shares, counts, unit_tile, units)
        both = scatter_rest(merged)

        arrays, _ = lax.optimization_barrier(([first_sums, query_bias_grad.reshape(1, -1), second_sums, up_bias_grad], merged))
        vector = pack(arrays, dkeyval)
        total, (outputs, up_weight_grad, down_weight_grad) = sum_all(vector, (outputs, up_weight_grad, down_weight_grad))
        (output_share, both), _ = lax.optimization_barrier(((output_share, both), (total, up_weight_grad)))
        output_weight_grad, query_weight_grad, keyval_weight_grad = finish(output_share, both, query_weight.shape[1])
        sizes = [width, width, query_bias.shape[0], width, width, width, width, up_bias.shape[0], HD]
        small, offset = [], 0
        for size in sizes:
            small.append(total[0, offset : offset + size])
            offset += size
        return (
            outputs.reshape(rows, seg, width),
            input_grad.reshape(rows, seg, width),
            small[0],
            small[1],
            query_weight_grad,
            small[2],
            keyval_weight_grad,
            small[8],
            output_weight_grad,
            small[5],
            small[3],
            small[4],
            up_weight_grad,
            small[7],
            down_weight_grad,
            small[6],
        )

    return per_device


def solution(mesh):
    placed = (
        P("dp", "sp", None),
        P("dp"),
        P(),
        P(),
        P(None, "tp"),
        P("tp"),
        P(),
        P(),
        P("tp", None),
        P(),
        P(),
        P(),
        P(None, "tp"),
        P("tp"),
        P("tp", None),
        P(),
        P("dp", "sp", None),
    )
    return jax.shard_map(
        build(mesh),
        mesh=mesh,
        in_specs=placed,
        out_specs=(
            P("dp", "sp", None),
            P("dp", "sp", None),
            P(),
            P(),
            P(("dp", "sp"), "tp"),
            P("tp"),
            P(("dp", "sp"), None),
            P(),
            P("tp", ("dp", "sp")),
            P(),
            P(),
            P(),
            P(("dp", "sp"), "tp"),
            P("tp"),
            P("tp", ("dp", "sp")),
            P(),
        ),
        check_vma=False,
    )
```

```python
import functools
import math

import jax
import jax.numpy as jnp
from jax import lax
from jax.experimental import pallas as pl
from jax.experimental.pallas import tpu as pltpu
from jax.sharding import PartitionSpec as P

HD = 128
EPS = 1e-05
BF = jnp.bfloat16
F32 = jnp.float32
SCALE = 1.0 / math.sqrt(HD)
SCALE2 = SCALE * math.log2(math.e)
VMEM = 60 * 2**20
GELU_A = math.sqrt(2.0 / math.pi)
GELU_B = 0.044715


def nn(left, right):
    return jnp.dot(left, right, preferred_element_type=F32)


def nt(left, right):
    return lax.dot_general(left, right, (((1,), (1,)), ((), ())), preferred_element_type=F32)


def tn(left, right):
    return lax.dot_general(left, right, (((0,), (0,)), ((), ())), preferred_element_type=F32)


def params():
    return pltpu.CompilerParams(vmem_limit_bytes=VMEM)


def cost(macs, moved, weight=10):
    return pl.CostEstimate(flops=int(2 * macs * weight), bytes_accessed=int(moved * weight), transcendentals=0)


def whole(*shape):
    return pl.BlockSpec(shape, lambda *_: (0,) * len(shape))


def chunk_mask(first, length, chunk, size, seg, wide):
    key_pos = chunk * size + lax.broadcasted_iota(jnp.int32, (size, wide), 0)
    query_pos = first + lax.rem(lax.broadcasted_iota(jnp.int32, (size, wide), 1), seg)
    return (key_pos <= query_pos) & (key_pos < length)


def chunk_bounds(info_ref, row, seg, size):
    first, length = info_ref[0], info_ref[3 + row]
    full = jnp.minimum(first + 1, length) // size
    total = (jnp.minimum(first + seg, length) + size - 1) // size
    return first, length, full, total


def stack_heads(ref, heads):
    return jnp.concatenate([ref[0, :, h * HD : (h + 1) * HD] for h in range(heads)], axis=0)


def unstack_heads(ref, values, heads, seg):
    for h in range(heads):
        ref[0, :, h * HD : (h + 1) * HD] = values[h * seg : (h + 1) * seg]


def forward_kernel(size, heads, seg, info_ref, q_ref, kv_ref, o_ref, lse_ref, top_s, sum_s, acc_s):
    first, length, full, total = chunk_bounds(info_ref, pl.program_id(0), seg, size)
    q = stack_heads(q_ref, heads)
    top_s[...] = jnp.full_like(top_s, -1e30)
    sum_s[...] = jnp.zeros_like(sum_s)
    acc_s[...] = jnp.zeros_like(acc_s)

    def step(masked, chunk, carry):
        at = pl.ds(pl.multiple_of((chunk ^ info_ref[1]) * size, size), size)
        scores = nt(kv_ref[info_ref[2], 0, at, :], q) * SCALE2
        if masked:
            scores = jnp.where(chunk_mask(first, length, chunk, size, seg, heads * seg), scores, -1e30)
        old = top_s[...]
        new = jnp.maximum(old, jnp.max(scores, axis=0, keepdims=True))
        weights = jnp.exp2(scores - new)
        shrink = jnp.exp2(old - new)
        sum_s[...] = sum_s[...] * shrink + jnp.sum(weights, axis=0, keepdims=True)
        acc_s[...] = acc_s[...] * shrink + tn(kv_ref[1 - info_ref[2], 0, at, :], weights.astype(BF))
        top_s[...] = new
        return carry

    lax.fori_loop(0, full, functools.partial(step, False), 0)
    lax.fori_loop(full, total, functools.partial(step, True), 0)
    unstack_heads(o_ref, (acc_s[...] * (1.0 / sum_s[...])).T.astype(BF), heads, seg)
    lse_ref[0, 0] = top_s[...] + jnp.log2(sum_s[...])


def attend_forward(info, query, keyval, size, heads):
    rows, seg, width = query.shape
    length = keyval.shape[2]
    groups, wide = width // (HD * heads), heads * seg
    head_spec = pl.BlockSpec((1, seg, heads * HD), lambda r, h, info: (r, 0, h))
    return pl.pallas_call(
        functools.partial(forward_kernel, size, heads, seg),
        grid_spec=pltpu.PrefetchScalarGridSpec(
            num_scalar_prefetch=1,
            grid=(rows, groups),
            in_specs=[head_spec, pl.BlockSpec((2, 1, length, HD), lambda r, h, info: (0, r, 0, 0))],
            out_specs=[head_spec, pl.BlockSpec((1, 1, 1, wide), lambda r, h, info: (r, h, 0, 0))],
            scratch_shapes=[pltpu.VMEM((1, wide), F32), pltpu.VMEM((1, wide), F32), pltpu.VMEM((HD, wide), F32)],
        ),
        out_shape=[
            jax.ShapeDtypeStruct((rows, seg, width), BF),
            jax.ShapeDtypeStruct((rows, groups, 1, wide), F32),
        ],
        compiler_params=params(),
        cost_estimate=cost(8 * 10**9, 4 * 2**20),
        name="attend_forward",
    )(info, query, keyval)


def backward_kernel(
    size, heads, seg, info_ref, q_ref, do_ref, o_ref, lse_ref, kv_ref, dq_ref, bias_ref, dk_ref, dv_ref, dqt_s
):
    row, group = pl.program_id(0), pl.program_id(1)
    first, length, full, total = chunk_bounds(info_ref, row, seg, size)

    @pl.when(group == 0)
    def _():
        dk_ref[...] = jnp.zeros_like(dk_ref)
        dv_ref[...] = jnp.zeros_like(dv_ref)

    q, dout, out = (stack_heads(ref, heads) for ref in (q_ref, do_ref, o_ref))
    delta = jnp.sum((dout.astype(F32) * out.astype(F32)).T, axis=0, keepdims=True)
    lse = lse_ref[0, 0]
    dqt_s[...] = jnp.zeros_like(dqt_s)

    def step(masked, chunk, carry):
        at = pl.ds(pl.multiple_of((chunk ^ info_ref[1]) * size, size), size)
        keys = kv_ref[info_ref[2], 0, at, :]
        prob = jnp.exp2(nt(keys, q) * SCALE2 - lse)
        if masked:
            prob = jnp.where(chunk_mask(first, length, chunk, size, seg, heads * seg), prob, 0.0)
        dprob = nt(kv_ref[1 - info_ref[2], 0, at, :], dout)
        dscore = (prob * (dprob - delta)).astype(BF)
        dv_ref[0, at, :] += nn(prob.astype(BF), dout)
        dk_ref[0, at, :] += nn(dscore, q) * SCALE
        dqt_s[...] += tn(keys, dscore)
        return carry

    lax.fori_loop(0, full, functools.partial(step, False), 0)
    lax.fori_loop(full, total, functools.partial(step, True), 0)
    dq = (dqt_s[...] * SCALE).T.astype(BF)
    unstack_heads(dq_ref, dq, heads, seg)
    for h in range(heads):
        bias_ref[0, :, h * HD : (h + 1) * HD] = jnp.sum(
            dq[h * seg : (h + 1) * seg].astype(F32), axis=0, keepdims=True
        )


def attend_backward(info, query, dout, out, lse, keyval, size, heads):
    rows, seg, width = query.shape
    length = keyval.shape[2]
    groups, wide = width // (HD * heads), heads * seg
    head_spec = pl.BlockSpec((1, seg, heads * HD), lambda r, h, info: (r, 0, h))
    key_spec = pl.BlockSpec((1, length, HD), lambda r, h, info: (r, 0, 0))
    return pl.pallas_call(
        functools.partial(backward_kernel, size, heads, seg),
        grid_spec=pltpu.PrefetchScalarGridSpec(
            num_scalar_prefetch=1,
            grid=(rows, groups),
            in_specs=[
                head_spec,
                head_spec,
                head_spec,
                pl.BlockSpec((1, 1, 1, wide), lambda r, h, info: (r, h, 0, 0)),
                pl.BlockSpec((2, 1, length, HD), lambda r, h, info: (0, r, 0, 0)),
            ],
            out_specs=[head_spec, pl.BlockSpec((1, 1, heads * HD), lambda r, h, info: (r, 0, h)), key_spec, key_spec],
            scratch_shapes=[pltpu.VMEM((HD, wide), F32)],
        ),
        out_shape=[
            jax.ShapeDtypeStruct((rows, seg, width), BF),
            jax.ShapeDtypeStruct((rows, 1, width), F32),
            jax.ShapeDtypeStruct((rows, length, HD), F32),
            jax.ShapeDtypeStruct((rows, length, HD), F32),
        ],
        compiler_params=params(),
        cost_estimate=cost(12 * 10**9, 8 * 2**20),
        name="attend_backward",
    )(info, query, dout, out, lse, keyval)


def gelu_parts(v):
    square = v * v
    t = jnp.tanh(GELU_A * v * (1.0 + GELU_B * square))
    half = 0.5 * (1.0 + t)
    slope = half + 0.5 * v * (1.0 - t * t) * (GELU_A * (1.0 + 3.0 * GELU_B * square))
    return v * half, slope


def local_kernel(parts, u_ref, dm_ref, *refs):
    piece_refs, refs = refs[:parts], refs[parts:]
    up_ref, down_ref, bias_ref, hidden_ref, du_ref, dbias_ref, u_all_ref, dm_rest_ref, du_s, u_s, send, recv, local = refs
    step, last = pl.program_id(0), pl.num_programs(0) - 1
    dp, sp, tp = lax.axis_index("dp"), lax.axis_index("sp"), lax.axis_index("tp")
    half = u_ref.shape[0] // 2
    quarter = half // 2
    over_x, over_y, sibling = (dp, sp ^ 1, tp), (dp, sp ^ 2, tp), (dp, sp, 1 - tp)

    def remote(k, source, target, device):
        return pltpu.make_async_remote_copy(
            source, target, send.at[k], recv.at[k], device_id=device, device_id_type=pl.DeviceIdType.MESH
        )

    own = u_s.at[pl.ds(pl.multiple_of(tp * half, half), half), :]
    other = u_s.at[pl.ds(pl.multiple_of((1 - tp) * half, half), half), :]
    top, bottom = pl.ds(0, quarter), pl.ds(quarter, quarter)
    own_top = u_s.at[pl.ds(pl.multiple_of(tp * half, quarter), quarter), :]
    own_bottom = u_s.at[pl.ds(pl.multiple_of(tp * half + quarter, quarter), quarter), :]
    first = [remote(0, own_top, u_all_ref.at[1, top], over_x), remote(1, own_bottom, u_all_ref.at[2, bottom], over_y)]
    second = [remote(2, own_bottom, u_all_ref.at[1, bottom], over_x), remote(3, own_top, u_all_ref.at[2, top], over_y)]
    passes = [
        remote(4, u_all_ref.at[1, top], u_all_ref.at[3, top], over_y),
        remote(5, u_all_ref.at[2, bottom], u_all_ref.at[3, bottom], over_x),
    ]
    shares = [remote(5 + k, u_all_ref.at[k], u_all_ref.at[3 + k], sibling) for k in (1, 2, 3)]
    dm_shares = [remote(9 + k, piece, dm_rest_ref.at[k], sibling) for k, piece in enumerate(piece_refs)]
    keep_own = pltpu.make_async_copy(own, u_all_ref.at[0], local.at[0])
    keep_other = pltpu.make_async_copy(other, u_all_ref.at[7], local.at[1])

    @pl.when(step == 0)
    def _():
        barrier = pltpu.get_barrier_semaphore()
        for device in (over_x, over_y, sibling):
            pl.semaphore_signal(barrier, inc=1, device_id=device, device_id_type=pl.DeviceIdType.MESH)
        pl.semaphore_wait(barrier, 3)
        u_s[...] = u_ref[...]
        for copy in (*first, *second, *dm_shares):
            copy.start()
        keep_own.start()
        keep_other.start()
        du_s[...] = jnp.zeros_like(du_s)

    @pl.when(step == (last + 1) // 2)
    def _():
        for copy in first:
            copy.wait_recv()
        for copy in passes:
            copy.start()

    @pl.when(step == last)
    def _():
        for copy in second:
            copy.wait_recv()
        shares[0].start()
        shares[1].start()

    hidden, slope = gelu_parts(nn(u_ref[...], up_ref[...]) + bias_ref[...])
    hidden_ref[...] = hidden.astype(BF)
    dpre = (nt(dm_ref[...], down_ref[...]) * slope).astype(BF)
    dbias_ref[...] = jnp.sum(dpre.astype(F32), axis=0, keepdims=True)
    du_s[...] += nt(dpre, up_ref[...])

    @pl.when(step == last)
    def _():
        for copy in passes:
            copy.wait_recv()
        shares[2].start()
        du_ref[...] = du_s[...].astype(BF)
        for copy in (*first, *second, *passes):
            copy.wait_send()
        for copy in (*shares, *dm_shares):
            copy.wait()
        keep_own.wait()
        keep_other.wait()


def feed_local(u, dmlp, pieces, up, down, bias, tile):
    tokens, width = u.shape
    units = up.shape[1]
    block = whole(tokens, width)
    anywhere = pl.BlockSpec(memory_space=pl.ANY)
    return pl.pallas_call(
        functools.partial(local_kernel, len(pieces)),
        grid=(units // tile,),
        in_specs=[
            block,
            block,
            *[anywhere] * len(pieces),
            pl.BlockSpec((width, tile), lambda i: (0, i)),
            pl.BlockSpec((tile, width), lambda i: (i, 0)),
            pl.BlockSpec((1, tile), lambda i: (0, i)),
        ],
        out_specs=[
            pl.BlockSpec((tokens, tile), lambda i: (0, i)),
            block,
            pl.BlockSpec((1, tile), lambda i: (0, i)),
            anywhere,
            anywhere,
        ],
        out_shape=[
            jax.ShapeDtypeStruct((tokens, units), BF),
            jax.ShapeDtypeStruct((tokens, width), BF),
            jax.ShapeDtypeStruct((1, units), F32),
            jax.ShapeDtypeStruct((8, tokens // 2, width), BF),
            jax.ShapeDtypeStruct((len(pieces), *pieces[0].shape), BF),
        ],
        scratch_shapes=[
            pltpu.VMEM((tokens, width), F32),
            pltpu.VMEM((tokens, width), BF),
            pltpu.SemaphoreType.DMA((9 + len(pieces),)),
            pltpu.SemaphoreType.DMA((9 + len(pieces),)),
            pltpu.SemaphoreType.DMA((2,)),
        ],
        compiler_params=pltpu.CompilerParams(vmem_limit_bytes=VMEM, collective_id=0, has_side_effects=True),
        cost_estimate=cost(3 * tokens * width * units, 4 * width * units),
        name="feed_local",
    )(u, dmlp, *pieces, up, down, bias)


def mlp_kernel(hidden_ref, down_ref, out_ref, total_s):
    @pl.when(pl.program_id(0) == 0)
    def _():
        total_s[...] = jnp.zeros_like(total_s)

    total_s[...] += nn(hidden_ref[...], down_ref[...])

    @pl.when(pl.program_id(0) == pl.num_programs(0) - 1)
    def _():
        out_ref[...] = total_s[...].astype(BF)


def feed_out(hidden, down, tile):
    tokens, units = hidden.shape
    width = down.shape[1]
    return pl.pallas_call(
        mlp_kernel,
        grid=(units // tile,),
        in_specs=[pl.BlockSpec((tokens, tile), lambda i: (0, i)), pl.BlockSpec((tile, width), lambda i: (i, 0))],
        out_specs=whole(tokens, width),
        out_shape=jax.ShapeDtypeStruct((tokens, width), BF),
        scratch_shapes=[pltpu.VMEM((tokens, width), F32)],
        compiler_params=params(),
        cost_estimate=cost(tokens * width * units, 2 * width * units, 10),
        name="feed_out",
    )(hidden, down)


def grad_kernel(u_parts, parts, at_ref, *refs):
    pieces, (up_ref, down_ref, bias_ref, out_ref, u_s, dm_s, sems) = refs[:parts], refs[parts:]

    def copies(target):
        offset = 0
        for k in range(u_parts) if target is u_s else range(u_parts, parts):
            piece = pieces[k]
            yield pltpu.make_async_copy(piece, target.at[pl.ds(offset, piece.shape[0]), :], sems.at[k])
            offset += piece.shape[0]

    @pl.when(pl.program_id(0) == 0)
    def _():
        for copy in copies(u_s):
            copy.start()
        for copy in copies(dm_s):
            copy.start()
        for copy in copies(u_s):
            copy.wait()
        for copy in copies(dm_s):
            copy.wait()

    tile = up_ref.shape[1]
    hidden, slope = gelu_parts(nn(u_s[...], up_ref[...]) + bias_ref[...])
    dpre = (nt(dm_s[...], down_ref[...]) * slope).astype(BF)
    out_ref[:, :tile] = tn(dpre, u_s[...]).T.astype(BF)
    out_ref[:, tile:] = tn(hidden.astype(BF), dm_s[...]).T.astype(BF)


def feed_grads(at, u, dmlp, up, down, bias, tile, count):
    width = up.shape[0]
    tokens = sum(part.shape[0] for part in u)
    return pl.pallas_call(
        functools.partial(grad_kernel, len(u), len(u) + len(dmlp)),
        grid_spec=pltpu.PrefetchScalarGridSpec(
            num_scalar_prefetch=1,
            grid=(count,),
            in_specs=[
                *[pl.BlockSpec(memory_space=pl.ANY)] * (len(u) + len(dmlp)),
                pl.BlockSpec((width, tile), lambda i, at: (0, at[0] + i)),
                pl.BlockSpec((tile, width), lambda i, at: (at[0] + i, 0)),
                pl.BlockSpec((1, tile), lambda i, at: (0, at[0] + i)),
            ],
            out_specs=pl.BlockSpec((width, 2 * tile), lambda i, at: (0, i)),
            scratch_shapes=[
                pltpu.VMEM((tokens, width), BF),
                pltpu.VMEM((tokens, width), BF),
                pltpu.SemaphoreType.DMA((len(u) + len(dmlp),)),
            ],
        ),
        out_shape=jax.ShapeDtypeStruct((width, 2 * tile * count), BF),
        compiler_params=params(),
        cost_estimate=cost(4 * tokens * width * tile * count, 4 * width * (tokens + 2 * tile * count)),
        name="feed_grads",
    )(at, *u, *dmlp, up, down, bias)


def normalize(values):
    average = jnp.mean(values, axis=-1, keepdims=True)
    centered = values - average
    variance = jnp.mean(centered * centered, axis=-1, keepdims=True)
    inv_std = lax.rsqrt(variance + EPS)
    return centered * inv_std, inv_std


def norm_back(gradient, scaled, inv_std, norm_gain):
    inner = gradient * norm_gain
    mean_one = jnp.mean(inner, axis=-1, keepdims=True)
    mean_two = jnp.mean(inner * scaled, axis=-1, keepdims=True)
    return inv_std * (inner - mean_one - scaled * mean_two)


def column_sum(values):
    return jnp.sum(values, axis=0, keepdims=True)


def by_rows(body, tokens, tile, ins, outs, name, sums=0, weight=1):
    row = lambda columns: pl.BlockSpec((tile, columns), lambda i: (i, 0))
    specs = [row(a.shape[1]) if cut else whole(*a.shape) for a, cut in ins]
    shapes = [jax.ShapeDtypeStruct((tokens, columns), dtype) for columns, dtype in outs]
    out_specs = [row(columns) for columns, _ in outs]
    if sums:
        shapes.append(jax.ShapeDtypeStruct((sums, outs[0][0]), F32))
        out_specs.append(whole(sums, outs[0][0]))
    moved = sum(a.size * a.dtype.itemsize for a, _ in ins) + sum(s.size * s.dtype.itemsize for s in shapes)
    return pl.pallas_call(
        body,
        grid=(tokens // tile,),
        in_specs=specs,
        out_specs=out_specs,
        out_shape=shapes,
        compiler_params=params(),
        cost_estimate=cost(moved * 200, moved, weight),
        name=name,
    )(*[a for a, _ in ins])


def first_kernel(x_ref, gain_ref, bias_ref, w_ref, wb_ref, v_ref, kv_ref):
    hat, _ = normalize(x_ref[...].astype(F32))
    v = (hat * gain_ref[...] + bias_ref[...]).astype(BF)
    v_ref[...] = v
    kv_ref[...] = (nn(v, w_ref[...]) + wb_ref[...]).astype(BF)


def exchange_rows(part, finish, tokens, tile, firsts, ins, outs, name, collective_id, sums=0):
    count = tokens // tile
    now, late = lambda i: (jnp.minimum(i, count - 1), 0), lambda i: (jnp.maximum(i - 1, 0), 0)
    spec = lambda a, cut, at: pl.BlockSpec((tile, a.shape[1]), at) if cut else whole(*a.shape)
    width = outs[0][0]

    def kernel(*refs):
        first_refs, refs = refs[: len(firsts)], refs[len(firsts) :]
        in_refs, refs = refs[: len(ins)], refs[len(ins) :]
        out_refs, (own_s, far_s, send, recv) = refs[:-4], refs[-4:]
        step = pl.program_id(0)
        sibling = (lax.axis_index("dp"), lax.axis_index("sp"), 1 - lax.axis_index("tp"))

        def copy(k):
            return pltpu.make_async_remote_copy(
                own_s.at[k], far_s.at[k], send.at[k], recv.at[k],
                device_id=sibling, device_id_type=pl.DeviceIdType.MESH,
            )

        @pl.when(step == 0)
        def _():
            barrier = pltpu.get_barrier_semaphore()
            pl.semaphore_signal(barrier, inc=1, device_id=sibling, device_id_type=pl.DeviceIdType.MESH)
            pl.semaphore_wait(barrier, 1)
            if sums:
                out_refs[-1][...] = jnp.zeros_like(out_refs[-1])

        @pl.when(step < count)
        def _():
            own_s[step] = part(*first_refs).astype(BF)
            copy(step).start()

        @pl.when(step > 0)
        def _():
            copy(step - 1).wait_recv()
            finish(own_s[step - 1].astype(F32) + far_s[step - 1].astype(F32), in_refs, out_refs)

        @pl.when(step == count)
        def _():
            for k in range(count):
                copy(k).wait_send()

    shapes = [jax.ShapeDtypeStruct((tokens, columns), dtype) for columns, dtype in outs]
    out_specs = [pl.BlockSpec((tile, columns), late) for columns, _ in outs]
    if sums:
        shapes.append(jax.ShapeDtypeStruct((sums, width), F32))
        out_specs.append(whole(sums, width))
    moved = sum(a.size * a.dtype.itemsize for a, _ in (*firsts, *ins))
    return pl.pallas_call(
        kernel,
        grid=(count + 1,),
        in_specs=[spec(a, cut, now) for a, cut in firsts] + [spec(a, cut, late) for a, cut in ins],
        out_specs=out_specs,
        out_shape=shapes,
        scratch_shapes=[
            pltpu.VMEM((count, tile, width), BF),
            pltpu.VMEM((count, tile, width), BF),
            pltpu.SemaphoreType.DMA((count,)),
            pltpu.SemaphoreType.DMA((count,)),
        ],
        compiler_params=pltpu.CompilerParams(vmem_limit_bytes=VMEM, collective_id=collective_id, has_side_effects=True),
        cost_estimate=cost(moved * 200, moved, 1),
        name=name,
    )(*[a for a, _ in firsts], *[a for a, _ in ins])


def proj_part(attended_ref, w_ref):
    return nn(attended_ref[...], w_ref[...])


def second_finish(proj, ins, outs):
    x_ref, ob_ref, gain_ref, bias_ref = ins
    resid_ref, u_ref = outs
    resid = x_ref[...].astype(F32) + proj + ob_ref[...]
    resid_ref[...] = resid
    hat, _ = normalize(resid)
    u_ref[...] = (hat * gain_ref[...] + bias_ref[...]).astype(BF)


def dv_part(dq_ref, w_ref):
    return nt(dq_ref[...], w_ref[...])


def first_finish(dv, ins, outs):
    dkv_ref, w_ref, x_ref, dres_ref, gain_ref = ins
    grad_ref, sums_ref = outs
    dv = dv + nt(dkv_ref[...], w_ref[...])
    hat, inv_std = normalize(x_ref[...].astype(F32))
    grad_ref[...] = (dres_ref[...] + norm_back(dv, hat, inv_std, gain_ref[...])).astype(BF)
    sums_ref[...] += jnp.concatenate([column_sum(dv * hat), column_sum(dv)], axis=0)


def second_back_kernel(own_ref, far_ref, resid_ref, dm_ref, gain_ref, dres_ref, dproj_ref, sums_ref):
    @pl.when(pl.program_id(0) == 0)
    def _():
        sums_ref[...] = jnp.zeros_like(sums_ref)

    du = own_ref[...].astype(F32) + far_ref[...].astype(F32)
    hat, inv_std = normalize(resid_ref[...])
    dout = dm_ref[...].astype(F32)
    dres = dout + norm_back(du, hat, inv_std, gain_ref[...])
    dres_ref[...] = dres
    dproj_ref[...] = dres.astype(BF)
    sums_ref[...] += jnp.concatenate(
        [column_sum(du * hat), column_sum(du), column_sum(dres), column_sum(dout)], axis=0
    )


def output_kernel(resid_ref, own_ref, far_ref, bias_ref, out_ref):
    mlp = own_ref[...].astype(F32) + far_ref[...].astype(F32)
    out_ref[...] = (resid_ref[...] + mlp + bias_ref[...]).astype(BF)


def project(left, right, transposed, tile, name, bias=None):
    tokens, depth = left.shape
    columns = right.shape[0] if transposed else right.shape[1]

    def body(*refs):
        product = (nt if transposed else nn)(refs[0][...], refs[1][...])
        if bias is not None:
            product = product + refs[2][...]
        refs[-1][...] = product.astype(BF)

    spec = pl.BlockSpec((tile, depth), lambda i: (i, 0)) if transposed else pl.BlockSpec((depth, tile), lambda i: (0, i))
    extra = [] if bias is None else [bias.reshape(1, columns)]
    return pl.pallas_call(
        body,
        grid=(columns // tile,),
        in_specs=[whole(tokens, depth), spec] + [pl.BlockSpec((1, tile), lambda i: (0, i))] * len(extra),
        out_specs=pl.BlockSpec((tokens, tile), lambda i: (0, i)),
        out_shape=jax.ShapeDtypeStruct((tokens, columns), BF),
        compiler_params=params(),
        cost_estimate=cost(tokens * depth * columns, 2 * (tokens * (depth + columns) + depth * columns)),
        name=name,
    )(left, right, *extra)


def rows_kernel(groups, shard, count, spot_ref, left_ref, *refs):
    rights, (keep_ref, x_ref, y_ref) = refs[:count], refs[count:]
    step = pl.program_id(0)
    dest = spot_ref[0] ^ step
    cols = [left_ref[:, pl.ds(pl.multiple_of((g * 4 + dest) * shard, shard), shard)] for g in range(groups)]
    left = jnp.concatenate(cols, axis=1)
    product = jnp.concatenate([tn(left, right[...]).astype(BF) for right in rights], axis=1)
    half = product.shape[0] // 2
    low, high = product[:half], product[half:]

    @pl.when(step == 0)
    def _():
        keep_ref[0], keep_ref[1] = low, high

    @pl.when(step == 1)
    def _():
        x_ref[0], keep_ref[3] = low, high

    @pl.when(step == 2)
    def _():
        keep_ref[2], y_ref[0] = low, high

    @pl.when(step == 3)
    def _():
        x_ref[1], y_ref[1] = low, high


def rows_grad(spot, left, rights, groups, shard):
    tokens, width = left.shape
    columns = sum(right.shape[1] for right in rights)
    half = groups * shard // 2
    return pl.pallas_call(
        functools.partial(rows_kernel, groups, shard, len(rights)),
        grid_spec=pltpu.PrefetchScalarGridSpec(
            num_scalar_prefetch=1,
            grid=(4,),
            in_specs=[whole(tokens, width), *[whole(*right.shape) for right in rights]],
            out_specs=[whole(4, half, columns), whole(2, half, columns), whole(2, half, columns)],
        ),
        out_shape=[jax.ShapeDtypeStruct((n, half, columns), BF) for n in (4, 2, 2)],
        compiler_params=params(),
        cost_estimate=cost(tokens * width * columns, 2 * (tokens + columns) * width, 1),
        name="rows_grad",
    )(spot, left, *rights)


def direct_kernel(groups, shard, spot_ref, left_ref, right_ref, *out_refs):
    for bit in range(4):
        dest = spot_ref[0] ^ bit
        cols = [left_ref[:, pl.ds(pl.multiple_of((g * 4 + dest) * shard, shard), shard)] for g in range(groups)]
        out_refs[bit][...] = tn(jnp.concatenate(cols, axis=1), right_ref[...]).astype(BF)


def rows_direct(spot, left, right, groups, shard):
    shape = (groups * shard, right.shape[1])
    return pl.pallas_call(
        functools.partial(direct_kernel, groups, shard),
        grid_spec=pltpu.PrefetchScalarGridSpec(
            num_scalar_prefetch=1,
            grid=(1,),
            in_specs=[whole(*left.shape), whole(*right.shape)],
            out_specs=[whole(*shape)] * 4,
        ),
        out_shape=[jax.ShapeDtypeStruct(shape, BF)] * 4,
        compiler_params=params(),
        cost_estimate=cost(left.size * right.shape[1], 2 * left.size, 1),
        name="rows_direct",
    )(spot, left, right)


def add_kernel(keep_ref, x_ref, y_ref, low_ref, high_ref):
    low_ref[...] = (keep_ref[2].astype(F32) + x_ref[1].astype(F32)).astype(BF)
    high_ref[...] = (keep_ref[3].astype(F32) + y_ref[1].astype(F32)).astype(BF)


def add_passed(keep, from_x, from_y):
    shape = keep.shape[1:]
    return pl.pallas_call(
        add_kernel,
        in_specs=[whole(*keep.shape), whole(*from_x.shape), whole(*from_y.shape)],
        out_specs=[whole(*shape), whole(*shape)],
        out_shape=[jax.ShapeDtypeStruct(shape, BF)] * 2,
        grid=(1,),
        compiler_params=params(),
        cost_estimate=cost(0, 8 * shape[0] * shape[1] * 2, 1),
        name="add_passed",
    )(keep, from_x, from_y)


def total_kernel(ready, *refs):
    out_ref, offset = refs[-1], 0
    for k in range(ready):
        columns = refs[k].shape[1]
        out_ref[:, offset : offset + columns] = refs[k][...]
        offset += columns
    keep_ref, x_ref, y_ref, low_ref, high_ref = refs[ready : ready + 5]
    half, columns = low_ref.shape
    at = slice(offset, offset + columns)
    out_ref[:half, at] = (keep_ref[0].astype(F32) + x_ref[0].astype(F32) + low_ref[...].astype(F32)).astype(BF)
    out_ref[half:, at] = (keep_ref[1].astype(F32) + y_ref[0].astype(F32) + high_ref[...].astype(F32)).astype(BF)
    rest = refs[ready + 5 : -1]
    if rest:
        out_ref[:, offset + columns :] = sum(ref[...].astype(F32) for ref in rest).astype(BF)


def add_total(ready, quads):
    arrays = [*ready, *[array for quad in quads for array in quad]]
    lead = 2 * quads[0][3].shape[0]
    columns = sum(a.shape[1] for a in ready) + sum(quad[3].shape[1] for quad in quads)
    return pl.pallas_call(
        functools.partial(total_kernel, len(ready)),
        in_specs=[whole(*a.shape) for a in arrays],
        out_specs=whole(lead, columns),
        out_shape=jax.ShapeDtypeStruct((lead, columns), BF),
        grid=(1,),
        compiler_params=params(),
        cost_estimate=cost(0, 8 * lead * columns, 1),
        name="add_total",
    )(*arrays)


def finish_kernel(output_ref, both_ref, out_ref, query_ref, kv_ref):
    columns = query_ref.shape[1]
    out_ref[...] = output_ref[...].astype(F32).T
    query_ref[...] = both_ref[:, :columns].astype(F32)
    kv_ref[...] = both_ref[:, columns:].astype(F32)


def finish(output, both, columns):
    shard, total = both.shape
    shapes = [(output.shape[1], shard), (shard, columns), (shard, total - columns)]
    return pl.pallas_call(
        finish_kernel,
        in_specs=[whole(*output.shape), whole(shard, total)],
        out_specs=[whole(*shape) for shape in shapes],
        out_shape=[jax.ShapeDtypeStruct(shape, F32) for shape in shapes],
        grid=(1,),
        compiler_params=params(),
        cost_estimate=cost(0, 6 * shard * total, 1),
        name="finish",
    )(output, both)


def pack_kernel(*refs):
    *in_refs, kv_ref, out_ref = refs
    offset = 0
    for ref in in_refs:
        for k in range(ref.shape[0]):
            out_ref[:, offset : offset + ref.shape[1]] = ref[k : k + 1]
            offset += ref.shape[1]
    out_ref[:, offset:] = column_sum(kv_ref[:, HD:].astype(F32))


def pack(arrays, dkeyval):
    size = sum(a.size for a in arrays) + HD
    return pl.pallas_call(
        pack_kernel,
        in_specs=[whole(*a.shape) for a in (*arrays, dkeyval)],
        out_specs=whole(1, size),
        out_shape=jax.ShapeDtypeStruct((1, size), F32),
        grid=(1,),
        compiler_params=params(),
        cost_estimate=cost(0, 8 * size, 1),
        name="pack",
    )(*arrays, dkeyval)


def place_kernel(tile, counts, spot_ref, *refs):
    shares, (up_ref, down_ref) = refs[:-2], refs[-2:]
    units = up_ref.shape[1] // 4
    for bit in range(4):
        at = (spot_ref[0] ^ bit) * units
        tile_at = 0
        for piece, count in enumerate(counts):
            for k in range(count):
                block = shares[piece * 4 + bit][:, k * 2 * tile : (k + 1) * 2 * tile].astype(F32)
                spot = pl.ds(pl.multiple_of(at + (tile_at + k) * tile, tile), tile)
                up_ref[:, spot] = block[:, :tile]
                down_ref[spot, :] = block[:, tile:].T
            tile_at += count


def place_shares(spot, shares, counts, tile, units):
    shard = shares[0].shape[0]
    return pl.pallas_call(
        functools.partial(place_kernel, tile, counts),
        grid_spec=pltpu.PrefetchScalarGridSpec(
            num_scalar_prefetch=1,
            grid=(1,),
            in_specs=[whole(*share.shape) for share in shares],
            out_specs=[whole(shard, units), whole(units, shard)],
        ),
        out_shape=[jax.ShapeDtypeStruct((shard, units), F32), jax.ShapeDtypeStruct((units, shard), F32)],
        compiler_params=params(),
        cost_estimate=cost(0, 12 * shard * units, 1),
        name="place_shares",
    )(spot, *shares)


def build(mesh):
    sp_size, dp_size = mesh.shape["sp"], mesh.shape["dp"]
    quads = sp_size // 4

    def swap(value, bit, keep=None):
        pairs = [(i, i ^ bit) for i in range(sp_size)]
        return lax.ppermute(value, "sp", pairs if keep is None else [p for p in pairs if keep(*p)])

    def swap_dp(value, bit):
        return lax.ppermute(value, "dp", [(i, i ^ bit) for i in range(dp_size)])

    def swap_tp(value):
        return lax.ppermute(value, "tp", [(0, 1), (1, 0)])

    def sum_all(vector, fill):
        for exchange, size in ((swap, sp_size), (swap_dp, dp_size)):
            bit = 1
            while bit < size:
                if bit * 2 < size:
                    near, far, both = (exchange(vector, k) for k in (bit, 2 * bit, 3 * bit))
                    if exchange is swap_dp:
                        (near, far, both), fill = lax.optimization_barrier(((near, far, both), fill))
                    vector = (vector + near) + (far + both)
                else:
                    vector = vector + exchange(vector, bit)
                bit *= 4
        return vector, fill

    def half_of(own, core):
        half = own.shape[0] // 2
        return lax.dynamic_slice_in_dim(own, core * half, half, 0)

    def scatter_rest(value, after=None):
        if after is not None:
            value, _ = lax.optimization_barrier((value, after))
        value = lax.psum_scatter(value, "dp", scatter_dimension=0, tiled=True)
        if quads > 1:
            groups = [[q * 4 + r for q in range(quads)] for r in range(4)]
            value = lax.psum_scatter(value, "sp", scatter_dimension=0, tiled=True, axis_index_groups=groups)
        return value

    def start_quad(spot, left, rights, shard, after=()):
        groups = dp_size * quads
        if shard % 128 == 0:
            keep, to_x, to_y = rows_grad(spot.reshape(1), left, rights, groups, shard)
            to_x, to_y, _ = lax.optimization_barrier((to_x, to_y, after))
            return [keep, swap(to_x, 1), swap(to_y, 2)]
        value = jnp.concatenate([tn(left, right).astype(BF) for right in rights], axis=1)
        value = value.reshape(groups, 4, shard, -1)
        blocks = [
            lax.dynamic_index_in_dim(value, spot ^ bit, 1, keepdims=False).reshape(groups * shard, -1)
            for bit in range(4)
        ]
        return [blocks[0], *[swap(blocks[bit], bit) for bit in range(1, 4)]]

    def direct_quad(spot, left, right, shard):
        if shard % 128 == 0:
            blocks = rows_direct(spot.reshape(1), left, right, dp_size * quads, shard)
            return [blocks[0], *[swap(blocks[bit], bit) for bit in range(1, 4)]]
        return start_quad(spot, left, [right], shard)

    def middle_quad(parts):
        if len(parts) == 4:
            return parts, parts[0]
        low, high = add_passed(*parts)
        return [*parts, swap(low, 2), swap(high, 1)], low

    def end_quads(ready, quads):
        if len(quads[0]) == 5:
            return add_total(ready, quads)
        return jnp.concatenate([*ready, *[sum(p.astype(F32) for p in quad).astype(BF) for quad in quads]], axis=1)

    def per_device(
        inputs, lengths, first_gain, first_bias, query_weight, query_bias, keyval_weight, value_bias, output_weight,
        output_bias, second_gain, second_bias, up_weight, up_bias, down_weight, down_bias, cotangent,
    ):
        rows, seg, width = inputs.shape
        tokens = rows * seg
        place, core = lax.axis_index("sp").astype(jnp.int32), lax.axis_index("tp")
        spot = lax.rem(place, 4)
        row_len = seg * sp_size
        one_quad = quads == 1
        shard = width // (dp_size * sp_size)
        even = core == 0
        info = jnp.concatenate([jnp.stack([place * seg, spot if one_quad else 0 * spot, core.astype(jnp.int32)]), lengths])
        row = lambda vector: vector.reshape(1, -1)

        x = inputs.reshape(tokens, width)
        dmlp = cotangent.reshape(tokens, width)
        tile = min(tokens, 128)
        piece = lambda at: lax.dynamic_slice_in_dim(dmlp, at * (tokens // 4), tokens // 4, 0)
        x, dmlp_top, dmlp_bottom = lax.optimization_barrier((x, piece(2 * core), piece(2 * core + 1)))
        half_weight = lax.dynamic_slice_in_dim(keyval_weight, core * HD, HD, 1)
        half_bias = row(jnp.where(even, 0.0, value_bias))
        v_first, kv_half = by_rows(
            first_kernel, tokens, tile,
            [(x, True), (row(first_gain), False), (row(first_bias), False), (half_weight, False), (half_bias, False)],
            [(width, BF), (HD, BF)], "first_norm",
        )
        top_x, bottom_y = swap(dmlp_top, 1), swap(dmlp_bottom, 2)
        v_late, top_x, bottom_y = lax.optimization_barrier((v_first, top_x, bottom_y))
        query = project(v_late, query_weight, False, 512, "query", query_bias).reshape(rows, seg, -1)
        if one_quad:
            pieces = [kv_half, *[swap(kv_half, bit, lambda a, b: a < b) for bit in (1, 2, 3)]]
            pieces, query = lax.optimization_barrier((pieces, query))
            kv_mine = jnp.concatenate(pieces, axis=0).reshape(1, row_len, HD)
            size = seg
        else:
            kv_mine = lax.all_gather(kv_half.reshape(rows, seg, HD), "sp", axis=1, tiled=True)
            size = min(512, row_len)
        top_x, bottom_y, top, bottom, kv_mine = lax.optimization_barrier((top_x, bottom_y, dmlp_top, dmlp_bottom, kv_mine))
        dmlp_pieces = [top_x, swap(bottom, 1), swap(top, 2), bottom_y, swap(top_x, 2), swap(bottom_y, 1)]
        keyval_all = jnp.stack([kv_mine, swap_tp(kv_mine)])

        query, keyval_all = lax.optimization_barrier((query, keyval_all))

        attended, lse = attend_forward(info, query, keyval_all, size, query.shape[2] // HD)
        attended_flat = attended.reshape(tokens, -1)
        resid, u_second = exchange_rows(
            proj_part, second_finish, tokens, 2 * tile, [(attended_flat, True), (output_weight, False)],
            [(x, True), (row(output_bias), False), (row(second_gain), False), (row(second_bias), False)],
            [(width, F32), (width, BF)], "second_norm", 1,
        )
        up_bias_row = row(up_bias)
        hidden, du, up_bias_grad, u_all, dmlp_rest = feed_local(
            u_second, dmlp, dmlp_pieces, up_weight, down_weight, up_bias_row, 256
        )
        u_all = [u_all.reshape(4 * tokens, width)]
        dmlp_all = [dmlp_top, dmlp_bottom, *dmlp_pieces, dmlp_rest.reshape(-1, width), half_of(dmlp, 1 - core)]

        units = up_weight.shape[1]
        unit_tile = 256
        tiles = units // 4 // unit_tile
        counts = (1, tiles - 1)
        feed_part = lambda at, count: feed_grads(
            at.reshape(1), u_all, dmlp_all, up_weight, down_weight, up_bias_row, unit_tile, count
        )
        shares = []

        def spread(share):
            blocks = [lax.dynamic_slice_in_dim(share, (spot ^ bit) * shard, shard, 0) for bit in range(4)]
            shares.extend([blocks[0], *[swap(blocks[bit], bit) for bit in range(1, 4)]])

        first_part = feed_part(spot * tiles, counts[0])
        first_share = scatter_rest(first_part)
        at, _ = lax.optimization_barrier((spot * tiles + counts[0], first_part))
        last_part = feed_part(at, counts[1])
        last_share = scatter_rest(last_part)

        du_far, _ = lax.optimization_barrier((swap_tp(du), last_part))
        dres, dproj, second_sums = by_rows(
            second_back_kernel, tokens, tile,
            [(du, True), (du_far, True), (resid, True), (dmlp, True), (row(second_gain), False)],
            [(width, F32), (width, BF)], "second_back", sums=4,
        )
        output_quad = start_quad(spot, dproj, [attended_flat], shard)
        dproj, output_keep = lax.optimization_barrier((dproj, output_quad[0]))
        dattended = project(dproj, output_weight, True, 512, "dattended").reshape(rows, seg, -1)
        dattended, first_share = lax.optimization_barrier((dattended, first_share))
        dquery, query_bias_grad, dkey, dvalue = attend_backward(info, query, dattended, attended, lse, keyval_all, size, query.shape[2] // HD)
        dquery = dquery.reshape(tokens, -1)
        query_bias_grad = jnp.sum(query_bias_grad[:, 0], axis=0)
        dquery, output_quad = lax.optimization_barrier((dquery, [output_keep, *output_quad[1:]]))
        output_quad, formed = middle_quad(output_quad)
        dquery, _ = lax.optimization_barrier((dquery, formed))
        if one_quad:
            dkey, dvalue = dkey[0], dvalue[0]
            far = swap_tp(jnp.where(even, dvalue, dkey).astype(BF))
            half = jnp.where(even, dkey, dvalue) + far.astype(F32)
            sends = [half[bit * tokens : (bit + 1) * tokens].astype(BF) for bit in range(1, 4)]
            query_quad = start_quad(spot, v_first, [dquery], shard, sends)
            arrived = [swap(send, bit, lambda a, b: a > b) for bit, send in enumerate(sends, 1)]
            own = half[:tokens]
            for term in arrived:
                own = own + term.astype(F32)
            own = lax.optimization_barrier(own.astype(BF))
            far = swap_tp(own)
            output_part = end_quads([], [output_quad])
            hidden, _ = lax.optimization_barrier((hidden, (own, output_part, query_quad[0])))
            mlp = feed_out(hidden, down_weight, 512)
            far, mlp = lax.optimization_barrier((far, mlp))
        else:
            query_quad = start_quad(spot, v_first, [dquery], shard)
            mlp = feed_out(hidden, down_weight, 512)
            part = lax.psum(jnp.concatenate([dkey, dvalue], axis=2).astype(BF), "tp")
            both = lax.psum_scatter(part, "sp", scatter_dimension=1, tiled=True).reshape(tokens, 2 * HD)
            own, far = jnp.where(even, both[:, :HD], both[:, HD:]), jnp.where(even, both[:, HD:], both[:, :HD])
            output_part = end_quads([], [output_quad])
        dkeyval = jnp.concatenate([jnp.where(even, own, far), jnp.where(even, far, own)], axis=1)

        (outputs,) = by_rows(
            output_kernel, tokens, tile,
            [(resid, True), (mlp, True), (swap_tp(mlp), True), (row(down_bias), False)], [(width, BF)], "outputs", weight=1,
        )

        kv_quad = direct_quad(spot, v_first, dkeyval, shard)
        query_quad, formed = middle_quad(query_quad)
        dkv_late, _ = lax.optimization_barrier((dkeyval, (kv_quad[0], formed)))
        input_grad, first_sums = exchange_rows(
            dv_part, first_finish, tokens, 2 * tile, [(dquery, True), (query_weight, False)],
            [(dkv_late, True), (keyval_weight, False), (x, True), (dres, True), (row(first_gain), False)],
            [(width, BF)], "first_back", 2, sums=2,
        )
        query_quad, first_sums = lax.optimization_barrier((query_quad, first_sums))
        merged = end_quads([], [query_quad, kv_quad])
        output_share = scatter_rest(output_part)
        first_share, _ = lax.optimization_barrier((first_share, merged))
        spread(first_share)
        spread(last_share)
        up_weight_grad, down_weight_grad = place_shares(spot.reshape(1), shares, counts, unit_tile, units)
        both = scatter_rest(merged)

        arrays, _ = lax.optimization_barrier(([first_sums, query_bias_grad.reshape(1, -1), second_sums, up_bias_grad], merged))
        vector = pack(arrays, dkeyval)
        total, (outputs, up_weight_grad, down_weight_grad) = sum_all(vector, (outputs, up_weight_grad, down_weight_grad))
        (output_share, both), _ = lax.optimization_barrier(((output_share, both), (total, up_weight_grad)))
        output_weight_grad, query_weight_grad, keyval_weight_grad = finish(output_share, both, query_weight.shape[1])
        sizes = [width, width, query_bias.shape[0], width, width, width, width, up_bias.shape[0], HD]
        small, offset = [], 0
        for size in sizes:
            small.append(total[0, offset : offset + size])
            offset += size
        return (
            outputs.reshape(rows, seg, width),
            input_grad.reshape(rows, seg, width),
            small[0],
            small[1],
            query_weight_grad,
            small[2],
            keyval_weight_grad,
            small[8],
            output_weight_grad,
            small[5],
            small[3],
            small[4],
            up_weight_grad,
            small[7],
            down_weight_grad,
            small[6],
        )

    return per_device


def solution(mesh):
    placed = (
        P("dp", "sp", None),
        P("dp"),
        P(),
        P(),
        P(None, "tp"),
        P("tp"),
        P(),
        P(),
        P("tp", None),
        P(),
        P(),
        P(),
        P(None, "tp"),
        P("tp"),
        P("tp", None),
        P(),
        P("dp", "sp", None),
    )
    return jax.shard_map(
        build(mesh),
        mesh=mesh,
        in_specs=placed,
        out_specs=(
            P("dp", "sp", None),
            P("dp", "sp", None),
            P(),
            P(),
            P(("dp", "sp"), "tp"),
            P("tp"),
            P(("dp", "sp"), None),
            P(),
            P("tp", ("dp", "sp")),
            P(),
            P(),
            P(),
            P(("dp", "sp"), "tp"),
            P("tp"),
            P("tp", ("dp", "sp")),
            P(),
        ),
        check_vma=False,
    )
```
